32 devices in a mesh: dp: 8 (over y, x, core), fsdp: 4 (over z).
Axes of the slice: x: 2, y: 2, z: 4, core: 2. Of those that a mesh axis runs over, the one named last changes fastest.
Arguments:
- tokens: bfloat16 [131072, 768], P(('dp', 'fsdp')), may hold values from -6 to 6
- row_index: int32 [128, 256], P(('dp', 'fsdp')), may hold values from 0 to 1023, as said below
- row_valid: int32 [128, 256], P(('dp', 'fsdp')), may hold values from 0 to 1, as said below
- w_query: bfloat16 [768, 768], P('fsdp'), may hold values from -0.21875 to 0.21875
- w_key: bfloat16 [768, 768], P('fsdp'), may hold values from -0.21875 to 0.21875
- w_value: bfloat16 [768, 768], P('fsdp'), may hold values from -0.21875 to 0.21875
- w_out: bfloat16 [768, 768], P('fsdp'), may hold values from -0.875 to 0.875
- w_up: bfloat16 [768, 3072], P('fsdp'), may hold values from -0.21875 to 0.21875
- w_down: bfloat16 [3072, 768], P('fsdp'), may hold values from -0.109375 to 0.109375
- gain_attn: bfloat16 [768], P('fsdp'), may hold values from 0.099609375 to 1.8984375
- gain_mlp: bfloat16 [768], P('fsdp'), may hold values from 0.099609375 to 1.8984375
- w_router: bfloat16 [768], P('fsdp'), may hold values from -0.21875 to 0.21875
- cotangent: bfloat16 [131072, 768], P(('dp', 'fsdp')), may hold values from -13 to 13
Outputs:
- out_tokens: bfloat16 [131072, 768], P(('dp', 'fsdp'))
- grad_tokens: bfloat16 [131072, 768], P(('dp', 'fsdp'))
- grad_query: float32 [768, 768], P('fsdp')
- grad_key: float32 [768, 768], P('fsdp')
- grad_value: float32 [768, 768], P('fsdp')
- grad_out: float32 [768, 768], P('fsdp')
- grad_up: float32 [768, 3072], P('fsdp')
- grad_down: float32 [3072, 768], P('fsdp')
- grad_gain_attn: float32 [768], P('fsdp')
- grad_gain_mlp: float32 [768], P('fsdp')
- grad_router: float32 [768], P('fsdp')
The draws below stay inside these ranges and needn't reach their ends.
Inputs may be any that keep to these rules, and one draw needn't show every extreme that they name: `row_index`: the 256 positions of one sequence are distinct. `row_valid`: each sequence's live slots come first; at least 42 are live, and in every draw some sequence has all 256 slots live.
All inputs are finite; a program needn't handle non-finite values.
Results may differ from the reference program's by a relative error of at most 0.012.
Values may be sent and summed in bfloat16 or wider, within the bound.
A program may use at most 256 MiB of HBM per device.

```python
import jax
import jax.numpy as jnp
from jax import lax

D = 768
HEADS = 12
FF = 3072
LEN = 1024
CAP = 256
SEQS = 128
TOKENS = 131072


def draw_row_index(key, part):
    key = jax.random.fold_in(key, 11)
    noise = jax.random.randint(key, (SEQS, LEN), 0, 2 ** 19)
    order = jnp.argsort(noise * LEN + jnp.arange(LEN, dtype=jnp.int32)[None, :], axis=1)
    return order[:, :CAP].astype(jnp.int32)


def draw_row_valid(key, part):
    key = jax.random.fold_in(key, 23)
    key_base, key_factor, key_chosen = jax.random.split(key, 3)
    base_rows = jax.random.randint(key_base, (SEQS,), CAP // 6, 3 * CAP // 8)
    factor = jax.random.randint(key_factor, (SEQS,), 1, 4)
    chosen = jax.random.randint(key_chosen, (), 0, SEQS)
    live_count = jnp.minimum(base_rows * factor, CAP)
    live_count = jnp.where(jnp.arange(SEQS) == chosen, CAP, live_count)
    return (jnp.arange(CAP)[None, :] < live_count[:, None]).astype(jnp.int32)


def draw_cotangent(key, part):
    key = jax.random.fold_in(key, 37)
    key_rows = jax.random.fold_in(key, 0)
    ramp = 1.0 + 2.0 * (jnp.arange(TOKENS) // LEN).astype(jnp.float32) / max(SEQS - 1, 1)
    noise = jnp.clip(jax.random.normal(key_rows, (TOKENS, D), jnp.float32), -4.0, 4.0)
    return (noise * ramp[:, None]).astype(jnp.bfloat16)


def shard_levels(own_key, dims, shards, least, high):
    factor_of = 1.0
    for axis_at, shards_of in shards:
        steps = jax.random.uniform(jax.random.fold_in(jax.random.fold_in(own_key, 6), axis_at), (shards_of,), jnp.float32, least / len(shards), high / len(shards))
        factor_of = factor_of * jnp.repeat(jnp.exp(steps), dims[axis_at] // shards_of).reshape((-1,) + (1,) * (len(dims) - 1 - axis_at))
    return factor_of


def gaussian(key, dims, scale, limit, cuts=(), held_as=jnp.bfloat16):
    drawn = scale * jax.random.normal(key, dims, jnp.float32)
    if cuts:
        drawn = drawn * shard_levels(key, dims, cuts, -0.22, 0.18)
    return jnp.clip(drawn, -limit, limit).astype(held_as)


def setup_inputs(seed: int = 0) -> dict:
    seeds = jax.random.split(jax.random.key(seed), 14)
    tokens = gaussian(seeds[0], (TOKENS, D), 1.0, 6.0, ((0, 32),))
    row_index = draw_row_index(jax.random.fold_in(seeds[13], 71), 0)
    row_valid = draw_row_valid(jax.random.fold_in(seeds[13], 71), 0)
    w_query = gaussian(seeds[3], (D, D), D ** -0.5, 0.21875, ((0, 4),))
    w_key = gaussian(seeds[4], (D, D), D ** -0.5, 0.21875, ((0, 4),))
    w_value = gaussian(seeds[5], (D, D), D ** -0.5, 0.21875, ((0, 4),))
    w_out = gaussian(seeds[6], (D, D), (D // 16) ** -0.5, 0.875, ((0, 4),))
    w_up = gaussian(seeds[7], (D, FF), D ** -0.5, 0.21875, ((0, 4),))
    w_down = gaussian(seeds[8], (FF, D), FF ** -0.5, 0.109375, ((0, 4),))
    gain_attn = jnp.clip(1.0 + 0.18 * jax.random.normal(seeds[9], (D,), jnp.float32), 0.099609375, 1.8984375).astype(jnp.bfloat16)
    gain_mlp = jnp.clip(1.0 + 0.18 * jax.random.normal(seeds[10], (D,), jnp.float32), 0.099609375, 1.8984375).astype(jnp.bfloat16)
    w_router = gaussian(seeds[11], (D,), D ** -0.5, 0.21875, ((0, 4),))
    cotangent = draw_cotangent(jax.random.fold_in(seeds[13], 71), 0)
    return {"tokens": tokens, "row_index": row_index, "row_valid": row_valid, "w_query": w_query, "w_key": w_key, "w_value": w_value, "w_out": w_out, "w_up": w_up, "w_down": w_down, "gain_attn": gain_attn, "gain_mlp": gain_mlp, "w_router": w_router, "cotangent": cotangent}


@jax.custom_vjp
def low(v):
    return lax.optimization_barrier(v.astype(jnp.bfloat16)).astype(jnp.float32)

@jax.custom_vjp
def low_back(v):
    return v

def low_keep(v):
    return (low(v), None)

def low_pass(kept, grad):
    return (grad,)

def back_keep(v):
    return (v, None)

def back_low(kept, grad):
    return (low(grad),)
low.defvjp(low_keep, low_pass)
low_back.defvjp(back_keep, back_low)
EPS = 1e-06
NEG = -1e+30

def both_ways(values):
    return low(low_back(values))

def product(left_mat, right_mat):
    return jnp.dot(left_mat, right_mat, precision=lax.Precision.HIGHEST)

def rms_norm(values, gain_vec):
    return values * lax.rsqrt(lax.optimization_barrier(jnp.mean(values * values, axis=-1, keepdims=True)) + EPS) * gain_vec

def gelu_tanh(values):
    return jax.nn.gelu(values, approximate=True)

def sequence_change(picked, live_slots, slot_index, weights):
    w_query, w_key, w_value, w_out, w_up, w_down, gain_attn, gain_mlp, w_router = weights
    slots, model_width = picked.shape
    head_size = model_width // HEADS
    router_gate = jax.nn.sigmoid(product(picked, w_router))
    normed_attn = low(rms_norm(picked, gain_attn))
    queries = both_ways(product(normed_attn, w_query)).reshape(slots, HEADS, head_size)
    keys_head = both_ways(product(normed_attn, w_key)).reshape(slots, HEADS, head_size)
    values_head = both_ways(product(normed_attn, w_value)).reshape(slots, HEADS, head_size)
    raw_scores = jnp.einsum('qhe,khe->hqk', queries, keys_head, precision=lax.Precision.HIGHEST)
    scores = low_back(raw_scores * head_size ** (-0.5))
    pair_mask = (slot_index[None, :] < slot_index[:, None]) & (live_slots[None, :] > 0) | (slot_index[None, :] == slot_index[:, None])
    scores = jnp.where(pair_mask[None], scores, NEG)
    probs = low(jax.nn.softmax(scores, axis=-1))
    mixed_raw = jnp.einsum('hqk,khe->qhe', probs, values_head, precision=lax.Precision.HIGHEST)
    mixed_heads = both_ways(mixed_raw.reshape(slots, model_width))
    attn_out = low_back(product(mixed_heads, w_out))
    hidden = picked + router_gate[:, None] * attn_out
    normed_mlp = low(rms_norm(hidden, gain_mlp))
    upward = low_back(product(normed_mlp, w_up))
    active = low(gelu_tanh(upward))
    down_out = low_back(product(active, w_down))
    return (router_gate[:, None] * attn_out + down_out) * live_slots[:, None].astype(jnp.float32)

def layer_forward(tokens_wide, slot_index, live_slots, weights):
    seq_blocks = tokens_wide.reshape(-1, LEN, tokens_wide.shape[1])

    def one_sequence(carry, items):
        seq_rows, seq_index, seq_live = items
        picked = jnp.take(seq_rows, seq_index, axis=0)
        change = sequence_change(picked, seq_live, seq_index, weights)
        return (carry, seq_rows.at[seq_index].add(change))
    _, stacked = lax.scan(jax.checkpoint(one_sequence), jnp.zeros((), jnp.float32), (seq_blocks, slot_index, live_slots))
    return stacked.reshape(tokens_wide.shape)

def reference(tokens, row_index, row_valid, w_query, w_key, w_value, w_out, w_up, w_down, gain_attn, gain_mlp, w_router, cotangent):
    weights = tuple((matrix.astype(jnp.float32) for matrix in (w_query, w_key, w_value, w_out, w_up, w_down, gain_attn, gain_mlp, w_router)))

    def forward(tokens_wide, weight_set):
        return layer_forward(tokens_wide, row_index, row_valid, weight_set)
    out_wide, pull_back = jax.vjp(forward, tokens.astype(jnp.float32), weights)
    grad_wide, grad_set = pull_back(cotangent.astype(jnp.float32))
    return (out_wide.astype(jnp.bfloat16), grad_wide.astype(jnp.bfloat16), grad_set[0], grad_set[1], grad_set[2], grad_set[3], grad_set[4], grad_set[5], grad_set[6], grad_set[7], grad_set[8])
```

```python
import functools

import jax
import jax.numpy as jnp
from jax import lax
from jax.experimental import pallas as pl
from jax.experimental.pallas import tpu as pltpu

from jax.sharding import PartitionSpec as P

HEADS = 12
EPS = 1e-06
NEG = -1e30
BF = jnp.bfloat16
F32 = jnp.float32
GATE, R1, R2, LIVE, DLOG, POS = range(6)


def nn(a, b):
    return lax.dot_general(a, b, (((1,), (0,)), ((), ())), preferred_element_type=F32)


def nt(a, b):
    return lax.dot_general(a, b, (((1,), (1,)), ((), ())), preferred_element_type=F32)


def tn(a, b):
    return lax.dot_general(a, b, (((0,), (0,)), ((), ())), preferred_element_type=F32)


def flat(v):
    return v.reshape(-1, v.shape[-1])


def pick_phase(tokens, cot, idx, valid, picked, up, cols, tok_buf, tok_sem):
    seqs, slots = idx.shape
    length = tokens.shape[0] // seqs

    def fetch(t, slot):
        src = tokens if t % 2 == 0 else cot
        return pltpu.make_async_copy(
            src.at[pl.ds((t // 2) * length, length)], tok_buf[slot], tok_sem.at[slot]
        )

    fetch(0, 0).start()
    fetch(1, 1).start()
    pad = jnp.zeros((8 - seqs, slots), F32) if seqs < 8 else None
    for what, k in ((idx, POS), (valid, LIVE)):
        rows8 = what[...].astype(F32)
        if pad is not None:
            rows8 = jnp.concatenate([rows8, pad], axis=0)
        turned = rows8.T
        for s in range(seqs):
            cols[s * slots : (s + 1) * slots, k : k + 1] = turned[:, s : s + 1]
    lane = lax.broadcasted_iota(jnp.int32, (slots, length), 1).astype(F32)
    for s in range(seqs):
        rows = slice(s * slots, (s + 1) * slots)
        hot = jnp.where(lane == cols[rows, POS : POS + 1], 1.0, 0.0).astype(BF)
        for b, dst in ((0, picked), (1, up)):
            fetch(2 * s + b, b).wait()
            dst[rows, :] = nn(hot, tok_buf[b][...]).astype(BF)
            if s + 1 < seqs:
                fetch(2 * s + 2 + b, b).start()


def norm_phase(picked, gains, cols, na, tile=256):
    total = picked.shape[0]

    @pl.loop(0, total // tile)
    def _(i):
        rows = pl.ds(pl.multiple_of(i * tile, tile), tile)
        x = picked[rows, :].astype(F32)
        cols[rows, GATE : GATE + 1] = jax.nn.sigmoid(
            jnp.sum(x * gains[2:3, :], axis=1, keepdims=True)
        )
        r1 = lax.rsqrt(jnp.mean(x * x, axis=1, keepdims=True) + EPS)
        cols[rows, R1 : R1 + 1] = r1
        na[rows, :] = (x * r1 * gains[0:1, :]).astype(BF)


def qkv_phase(na, wa, qkv, scale):
    width = na.shape[1]
    for m in range(3):

        @pl.loop(0, width // 256)
        def _(n):
            at = pl.ds(pl.multiple_of(n * 256, 256), 256)
            out = nn(na[...], flat(wa[m, :, :, :, :, at]))
            if m == 0:
                out = out * scale
            qkv[m, :, at] = out.astype(BF)


def two_heads(v2, low_half):
    zero = jnp.zeros_like(v2)
    return jnp.concatenate([jnp.where(low_half, v2, zero), jnp.where(low_half, zero, v2)], axis=0)


def attention_forward(idx, valid, cols, qkv, probs, mixed, s):
    slots = idx.shape[1]
    width = mixed.shape[1]
    rows = pl.ds(pl.multiple_of(s * slots, slots), slots)
    low_half = lax.broadcasted_iota(jnp.int32, (slots, 128), 1) < 64
    mine = cols[rows, POS : POS + 1]
    other = idx[pl.ds(s, 1), :].astype(F32)
    seen = ((other < mine) & (valid[pl.ds(s, 1), :] > 0)) | (other == mine)
    bias = jnp.where(seen, 0.0, NEG)
    bias = jnp.concatenate([bias, bias], axis=0)
    for p in range(width // 128):
        at = slice(p * 128, p * 128 + 128)
        q2 = two_heads(qkv[0, rows, at], low_half)
        scores = nt(q2, qkv[1, rows, at]) + bias
        e = jnp.exp(scores - jnp.max(scores, axis=1, keepdims=True))
        pr = (e * (1.0 / jnp.sum(e, axis=1, keepdims=True))).astype(BF)
        probs[s * (width // 128) + p] = pr
        o = nn(pr, qkv[2, rows, at])
        mixed[rows, at] = jnp.where(low_half, o[:slots], o[slots:]).astype(BF)


def attention_backward(qkv, probs, mixed, dmix, s, slots, scale):
    width = mixed.shape[1]
    rows = pl.ds(pl.multiple_of(s * slots, slots), slots)
    low_half = lax.broadcasted_iota(jnp.int32, (slots, 128), 1) < 64
    for p in range(width // 128):
        at = slice(p * 128, p * 128 + 128)
        do2 = two_heads(dmix[rows, at], low_half)
        o2 = mixed[rows, at].astype(F32)
        o2 = jnp.concatenate([o2, o2], axis=0)
        delta = jnp.sum(do2.astype(F32) * o2, axis=1, keepdims=True)
        k2 = qkv[1, rows, at]
        dp = nt(do2, qkv[2, rows, at])
        pr = probs[s * (width // 128) + p]
        ds = (pr.astype(F32) * (dp - delta)).astype(BF)
        q2 = two_heads(qkv[0, rows, at], low_half)
        dq = nn(ds, k2) * scale
        qkv[0, rows, at] = jnp.where(low_half, dq[:slots], dq[slots:]).astype(BF)
        qkv[1, rows, at] = tn(ds, q2).astype(BF)
        qkv[2, rows, at] = tn(pr, do2).astype(BF)


def out_phase(mixed, wa, attn_out):
    width = mixed.shape[1]

    @pl.loop(0, width // 256)
    def _(n):
        at = pl.ds(pl.multiple_of(n * 256, 256), 256)
        attn_out[:, at] = nn(mixed[...], flat(wa[3, :, :, :, :, at]))


def mid_norm(picked, attn_out, up, gains, cols, nm, nmt, dd, down, dnm, tile=256):
    total = picked.shape[0]
    for i in range(total // tile):
        rows = slice(i * tile, (i + 1) * tile)
        hidden = picked[rows, :].astype(F32) + cols[rows, GATE : GATE + 1] * attn_out[rows, :]
        r2 = lax.rsqrt(jnp.mean(hidden * hidden, axis=1, keepdims=True) + EPS)
        cols[rows, R2 : R2 + 1] = r2
        normed = (hidden * r2 * gains[1:2, :]).astype(BF)
        nm[rows, :] = normed
        nmt[:, rows] = normed.T
        dd[rows, :] = (up[rows, :].astype(F32) * cols[rows, LIVE : LIVE + 1]).astype(BF)


def gelu_both(u):
    k = 0.7978845608028654
    u2 = u * u
    t = jnp.tanh(u * (k + (k * 0.044715) * u2))
    half = 0.5 + 0.5 * t
    act = u * half
    slope = half + act * (1.0 - t) * (k + (3 * k * 0.044715) * u2)
    return act, slope


def mlp_up(nm, dd, wu, wd, act, dup, c, n):
    ff = act.shape[1]
    at = pl.ds(pl.multiple_of(n * 256, 256), 256)
    u = nn(nm[...], flat(wu[c, :, :, :, :, at]))
    dact = nt(dd[...], flat(wd[c, n]))
    a, slope = gelu_both(u)
    act[:, at] = a.astype(BF)
    dup[:, at] = (slope * dact).astype(BF)


def mlp_down(act, wd, down, c):
    @pl.loop(0, down.shape[1] // 256)
    def _(n):
        at = pl.ds(pl.multiple_of(n * 256, 256), 256)
        out = nn(act[...], flat(wd[c, :, :, :, :, at]))
        down[:, at] = out if c == 0 else down[:, at] + out


def mlp_dnormed(dup, wu, dnm, c):
    @pl.loop(0, 2)
    def _(i):
        half = dnm.shape[0] // 2
        rows = pl.ds(pl.multiple_of(i * half, half), half)
        out = nt(dup[rows, :], flat(wu[c]))
        dnm[rows, :] = out if c == 0 else dnm[rows, :] + out


def mlp_grad_down(act, dd, wd, c):
    @pl.loop(0, act.shape[1] // 256)
    def _(n):
        at = pl.ds(pl.multiple_of(n * 256, 256), 256)
        g = tn(act[:, at], dd[...]).astype(BF)
        wd[c, n] = g.reshape(wd.shape[2:])


def mlp_grad_up(nmt, dup, wu, c):
    @pl.loop(0, dup.shape[1] // 256)
    def _(n):
        at = pl.ds(pl.multiple_of(n * 256, 256), 256)
        g = nn(nmt[...], dup[:, at]).astype(BF)
        wu[c, :, :, :, :, at] = g.reshape(wu.shape[1:5] + (256,))


def mid_backward(picked, attn_out, up, down, dnm, gains, cols, datt, new_rows, small, tile=128):
    total = picked.shape[0]
    small[...] = jnp.zeros_like(small)

    @pl.loop(0, total // tile)
    def _(i):
        rows = pl.ds(pl.multiple_of(i * tile, tile), tile)
        x = picked[rows, :].astype(F32)
        gate = cols[rows, GATE : GATE + 1]
        live = cols[rows, LIVE : LIVE + 1]
        r = cols[rows, R2 : R2 + 1]
        ao = attn_out[rows, :]
        branch = gate * ao
        hidden = x + branch
        new_rows[rows, :] = (x + live * (branch + down[rows, :])).astype(BF)
        d = dnm[rows, :]
        hr = hidden * r
        dh = d * hr
        small[1:2, :] += jnp.sum(dh, axis=0, keepdims=True)
        mean = jnp.mean(dh * gains[1:2, :], axis=1, keepdims=True)
        d_hidden = r * (gains[1:2, :] * d - hr * mean)
        dnm[rows, :] = d_hidden
        d_branch = live * up[rows, :].astype(F32) + d_hidden
        d_logit = jnp.sum(d_branch * ao, axis=1, keepdims=True) * gate * (1.0 - gate)
        cols[rows, DLOG : DLOG + 1] = d_logit
        small[2:3, :] += jnp.sum(x * d_logit, axis=0, keepdims=True)
        datt[rows, :] = (d_branch * gate).astype(BF)


def out_backward(datt, mixed, wa, dmix):
    total, width = datt.shape

    @pl.loop(0, 2)
    def _(i):
        half = total // 2
        rows = pl.ds(pl.multiple_of(i * half, half), half)
        dmix[rows, :] = nt(datt[rows, :], flat(wa[3])).astype(BF)

    wa[3] = grad_of(mixed, datt[...]).reshape(wa.shape[1:])


def grad_of(left, right):
    parts = [tn(left[:, n * 384 : n * 384 + 384], right).astype(BF) for n in range(2)]
    return jnp.concatenate(parts, axis=0)


def qkv_backward(dqkv, na, wa, dnorm):
    total, width = na.shape

    @pl.loop(0, 4)
    def _(i):
        half = total // 4
        rows = pl.ds(pl.multiple_of(i * half, half), half)
        dnorm[rows, :] = (
            nt(dqkv[0, rows, :], flat(wa[0]))
            + nt(dqkv[1, rows, :], flat(wa[1]))
            + nt(dqkv[2, rows, :], flat(wa[2]))
        )

    for m in range(3):
        wa[m] = grad_of(na, dqkv[m]).reshape(wa.shape[1:])


def first_backward(picked, up, dnorm, dhid, gains, cols, new_grads, small, tile=128):
    total = picked.shape[0]

    @pl.loop(0, total // tile)
    def _(i):
        rows = pl.ds(pl.multiple_of(i * tile, tile), tile)
        x = picked[rows, :].astype(F32)
        r = cols[rows, R1 : R1 + 1]
        d = dnorm[rows, :]
        xr = x * r
        dx = d * xr
        small[0:1, :] += jnp.sum(dx, axis=0, keepdims=True)
        mean = jnp.mean(dx * gains[0:1, :], axis=1, keepdims=True)
        d_first = r * (gains[0:1, :] * d - xr * mean)
        d_picked = d_first + dhid[rows, :] + cols[rows, DLOG : DLOG + 1] * gains[2:3, :]
        new_grads[rows, :] = (up[rows, :].astype(F32) + d_picked).astype(BF)


def compute_kernel(
    tokens, cot, idx, valid, wa_in, wu_in, wd_in, gains,
    ga, gu, gd, small, new_rows, new_grads,
    wa, wu, wd, picked, up, cols, na, qkv, probs, mixed, attn_out, nm, nmt, dd,
    act, dup, down, dnm, tok_sem, w_sem,
):
    seqs, slots = idx.shape
    width = picked.shape[1]
    scale = (width // HEADS) ** -0.5
    loads = [pltpu.make_async_copy(a, b, w_sem.at[i]) for i, (a, b) in enumerate(((wa_in, wa), (wu_in, wu), (wd_in, wd)))]
    for l in loads:
        l.start()
    pick_phase(tokens, cot, idx, valid, picked, up, cols, (new_rows, new_grads), tok_sem)
    norm_phase(picked, gains, cols, na)
    loads[0].wait()
    qkv_phase(na, wa, qkv, scale)

    @pl.loop(0, seqs)
    def _(s):
        attention_forward(idx, valid, cols, qkv, probs, mixed, s)

    out_phase(mixed, wa, attn_out)
    mid_norm(picked, attn_out, up, gains, cols, nm, nmt, dd, down, dnm)
    loads[1].wait()
    loads[2].wait()
    for c in range(wu.shape[0]):

        @pl.loop(0, 4)
        def _(n):
            mlp_up(nm, dd, wu, wd, act, dup, c, n)

        mlp_down(act, wd, down, c)
        mlp_dnormed(dup, wu, dnm, c)
        mlp_grad_down(act, dd, wd, c)
        mlp_grad_up(nmt, dup, wu, c)
    datt = nm
    dmix = dd
    mid_backward(picked, attn_out, up, down, dnm, gains, cols, datt, new_rows, small)
    out_backward(datt, mixed, wa, dmix)

    @pl.loop(0, seqs)
    def _(s):
        attention_backward(qkv, probs, mixed, dmix, s, slots, scale)

    qkv_backward(qkv, na, wa, down)
    first_backward(picked, up, down, dnm, gains, cols, new_grads, small)
    outs = [pltpu.make_async_copy(a, b, w_sem.at[i]) for i, (a, b) in enumerate(((wa, ga), (wu, gu), (wd, gd)))]
    for o in outs:
        o.start()
    for o in outs:
        o.wait()


MESH_ID = pl.DeviceIdType.MESH
A_MATS, CHUNKS, PLANE = 4, 3, 8


class Place:
    def __init__(self, depth):
        dp = lax.axis_index("dp")
        self.depth = depth
        self.z = lax.axis_index("fsdp")
        self.core = lax.rem(dp, 2)
        self.x = lax.rem(lax.div(dp, 2), 2)
        self.y = lax.rem(lax.div(dp, 4), 2)
        self.sib = (dp + 1 - 2 * self.core, self.z)
        self.xn = (dp + 2 - 4 * self.x, self.z)
        self.yn = (dp + 4 - 8 * self.y, self.z)
        self.dp = dp

    def ahead(self, o):
        return lax.rem(self.z + o, self.depth)

    def behind(self, o):
        return lax.rem(self.z + self.depth - o, self.depth)

    def at_z(self, z):
        return (self.dp, z)

    def greet(self):
        barrier = pltpu.get_barrier_semaphore()
        peers = [self.sib, self.xn, self.yn]
        peers += [self.at_z(self.ahead(o)) for o in range(1, self.depth)]
        for peer in peers:
            pl.semaphore_signal(barrier, inc=1, device_id=peer, device_id_type=MESH_ID)
        pl.semaphore_wait(barrier, len(peers))


def half_of(ref, core):
    width = ref.shape[-1] // 2
    return pl.ds(pl.multiple_of(core * width, 128), width)


class Gather:
    SLOTS = 18

    def __init__(self, me, wa, wu, wd, sends, recvs):
        self.me, self.refs, self.sends, self.recvs = me, (wa, wu, wd), sends, recvs

    def piece(self, a, zi, xi, yi, core):
        wa, wu, wd = self.refs
        if a == 0:
            return wa.at[:, zi, xi, yi, :, half_of(wa, core)]
        ref = wu if a % 2 else wd
        return ref.at[(a - 1) // 2, zi, xi, yi, :, half_of(ref, core)]

    def part(self, a, zi, xi, yi, core, h):
        wa = self.refs[0]
        if a == 0:
            return wa.at[2 * h : 2 * h + 2, zi, xi, yi, :, half_of(wa, core)]
        return self.piece(a, zi, xi, yi, core)

    def ways(self, a):
        return (0, 1) if a == 0 else ((0,) if a % 2 else (1,))

    def copy(self, a, k, ref, dev):
        at = a * self.SLOTS + k
        return pltpu.make_async_remote_copy(
            src_ref=ref, dst_ref=ref, send_sem=self.sends.at[at], recv_sem=self.recvs.at[at],
            device_id=dev, device_id_type=MESH_ID,
        )

    def z_out(self, a, o):
        m = self.me
        return self.copy(a, o, self.piece(a, m.z, m.x, m.y, m.core), m.at_z(m.ahead(o)))

    def x_out(self, a, o):
        m = self.me
        return self.copy(a, 3 + o, self.piece(a, m.behind(o), m.x, m.y, m.core), m.xn)

    def y_out(self, a, o):
        m = self.me
        return self.copy(a, 6 + o, self.piece(a, m.behind(o), m.x, m.y, m.core), m.yn)

    def far_out(self, a, o, h):
        m = self.me
        if h == 0:
            return self.copy(a, 9 + o, self.part(a, m.behind(o), 1 - m.x, m.y, m.core, 0), m.yn)
        return self.copy(a, 12 + o, self.part(a, m.behind(o), m.x, 1 - m.y, m.core, 1), m.xn)

    def core_out(self, a):
        m = self.me
        wa, wu, wd = self.refs
        if a == 0:
            ref = wa.at[:, :, :, :, :, half_of(wa, m.core)]
        else:
            ref = wu if a % 2 else wd
            ref = ref.at[(a - 1) // 2, :, :, :, :, half_of(ref, m.core)]
        return self.copy(a, 0, ref, m.sib)

    def z_in(self, a, o):
        m = self.me
        return self.copy(a, o, self.piece(a, m.behind(o), m.x, m.y, m.core), m.at_z(m.behind(o)))

    def x_in(self, a, o):
        m = self.me
        return self.copy(a, 3 + o, self.piece(a, m.behind(o), 1 - m.x, m.y, m.core), m.xn)

    def y_in(self, a, o):
        m = self.me
        return self.copy(a, 6 + o, self.piece(a, m.behind(o), m.x, 1 - m.y, m.core), m.yn)

    def far_in(self, a, o, h):
        m = self.me
        part = self.part(a, m.behind(o), 1 - m.x, 1 - m.y, m.core, h)
        return self.copy(a, (9 if h == 0 else 12) + o, part, m.yn if h == 0 else m.xn)

    def core_in(self, a):
        m = self.me
        wa, wu, wd = self.refs
        if a == 0:
            ref = wa.at[:, :, :, :, :, half_of(wa, 1 - m.core)]
        else:
            ref = wu if a % 2 else wd
            ref = ref.at[(a - 1) // 2, :, :, :, :, half_of(ref, 1 - m.core)]
        return self.copy(a, 0, ref, m.sib)

    def origins(self):
        return range(1, self.me.depth)

    def send_z(self, a):
        for o in self.origins():
            self.z_out(a, o).start()

    def spread(self, a, o):
        self.z_in(a, o).wait_recv()
        self.x_out(a, o).start()
        self.y_out(a, o).start()

    def forward(self, a, o):
        self.x_in(a, o).wait_recv()
        if 0 in self.ways(a):
            self.far_out(a, o, 0).start()
        self.y_in(a, o).wait_recv()
        if 1 in self.ways(a):
            self.far_out(a, o, 1).start()

    def across(self, a):
        for o in self.origins():
            for h in self.ways(a):
                self.far_in(a, o, h).wait_recv()
        self.core_out(a).start()

    def ready(self, a):
        self.core_in(a).wait_recv()

    def settle(self, a):
        for o in self.origins():
            self.z_out(a, o).wait_send()
            self.x_out(a, o).wait_send()
            self.y_out(a, o).wait_send()
            for h in self.ways(a):
                self.far_out(a, o, h).wait_send()
        self.core_out(a).wait_send()


class Owned:
    def __init__(self, me, shards, wa, wu, wd, sems):
        wq, wk, wv, wo, up, down = shards
        z, core = me.z, me.core
        half = half_of(wa, core)
        self.copies = {0: [], 1: [], 2: [], 3: [], 4: [], 5: [], 6: []}
        for m, w in enumerate((wq, wk, wv, wo)):
            self.copies[0].append((w.at[:, :, :, half], wa.at[m, z, :, :, :, half]))
        ff_own = up.shape[-1] // me.depth
        for c in range(CHUNKS):
            for j in range(2):
                block = 2 * core + j
                src = up.at[:, :, :, pl.ds(pl.multiple_of(block * ff_own + c * 256, 128), 256)]
                dst = wu.at[c, z, :, :, :, pl.ds(pl.multiple_of(block * 256, 128), 256)]
                self.copies[1 + 2 * c].append((src, dst))
            self.copies[2 + 2 * c].append((down.at[c, :, :, :, half], wd.at[c, z, :, :, :, half]))
        self.sems = sems

    def all_of(self, a):
        base = sum(len(self.copies[b]) for b in range(a))
        for i, (src, dst) in enumerate(self.copies[a]):
            yield pltpu.make_async_copy(src, dst, self.sems.at[base + i])

    def start(self, a):
        for c in self.all_of(a):
            c.start()

    def wait(self, a):
        for c in self.all_of(a):
            c.wait()


class Reduce:
    SLOTS = 14

    def __init__(
        self, me, w, from_core, from_x, from_y, then_x, then_y, from_z, sends, recvs, frees, at, way
    ):
        self.me, self.w, self.way, self.free, base = me, w, way, frees.at[at], at * self.SLOTS
        self.from_core, self.from_x, self.from_y = from_core, from_x, from_y
        self.then_x, self.then_y, self.from_z = then_x, then_y, from_z
        self.sends, self.recvs, self.base = sends, recvs, base
        self.mine, self.theirs = half_of(w, me.core), half_of(w, 1 - me.core)

    def copy(self, k, src, dst, dev):
        at = self.base + k
        return pltpu.make_async_remote_copy(
            src_ref=src, dst_ref=dst, send_sem=self.sends.at[at], recv_sem=self.recvs.at[at],
            device_id=dev, device_id_type=MESH_ID,
        )

    def core_copy(self):
        return self.copy(0, self.w.at[:, :, :, :, self.theirs], self.from_core, self.me.sib)

    def plane_first(self):
        m, w = self.me, self.w
        return (
            self.copy(1, w.at[0:2, 1 - m.x, :, :, self.mine], self.from_x, m.xn),
            self.copy(2, w.at[2:4, :, 1 - m.y, :, self.mine], self.from_y, m.yn),
        )

    def plane_second(self):
        m, w = self.me, self.w
        return (
            self.copy(3, w.at[0:2, m.x, 1 - m.y, :, self.mine], self.then_y, m.yn),
            self.copy(4, w.at[2:4, 1 - m.x, m.y, :, self.mine], self.then_x, m.xn),
        )

    def z_copy(self, o):
        m = self.me
        src = self.w.at[m.ahead(o), m.x, m.y, :, self.mine]
        return self.copy(4 + o, src, self.from_z.at[o - 1], m.at_z(m.ahead(o)))

    def back(self, k, xi, yi, dev):
        ref = self.from_core.at[0, xi, yi]
        return self.copy(k, ref, ref, dev)

    def core_back(self):
        return self.copy(11, self.from_core.at[0], self.from_core.at[1], self.me.sib)

    def add(self, at, arrived):
        self.w[at] = (self.w[at].astype(F32) + arrived.astype(F32)).astype(BF)

    def t1(self):
        self.core_copy().start()

    def t2(self):
        m = self.me
        self.core_copy().wait()

        @pl.loop(0, 2 * m.depth)
        def _(i):
            zi, xi = lax.div(i, 2), lax.rem(i, 2)
            self.add((zi, xi, slice(None), slice(None), self.mine), self.from_core[zi, xi])

        pl.semaphore_signal(self.free, inc=1, device_id=m.sib, device_id_type=MESH_ID)
        for c in self.plane_first():
            c.start()

    def t3(self):
        m = self.me
        first = self.plane_first()
        first[0].wait()
        for zi in range(2):
            self.add((zi, m.x, slice(None), slice(None), self.mine), self.from_x[zi])
        first[1].wait()
        for zi in range(2):
            self.add((2 + zi, slice(None), m.y, slice(None), self.mine), self.from_y[zi])
        for c in self.plane_second():
            c.start()

    def t4(self):
        m = self.me
        second = self.plane_second()
        second[0].wait()
        self.add((slice(0, 2), m.x, m.y, slice(None), self.mine), self.then_y[...])
        second[1].wait()
        self.add((slice(2, 4), m.x, m.y, slice(None), self.mine), self.then_x[...])
        for o in range(1, m.depth):
            self.z_copy(o).start()

    def t5(self):
        m = self.me
        at = (m.z, m.x, m.y, slice(None), self.mine)
        total = self.w[at].astype(F32)
        for o in range(1, m.depth):
            self.z_copy(o).wait()
            total = total + self.from_z[o - 1].astype(F32)
        self.from_core[0, m.x, m.y] = total.astype(BF)
        self.back(8, m.x, m.y, m.xn).start()
        self.back(9, m.x, m.y, m.yn).start()

    def far(self):
        m = self.me
        if self.way == 0:
            return self.back(10, 1 - m.x, m.y, m.yn)
        return self.back(10, m.x, 1 - m.y, m.xn)

    def t6(self):
        m = self.me
        self.back(8, 1 - m.x, m.y, m.xn).wait_recv()
        self.back(9, m.x, 1 - m.y, m.yn).wait_recv()
        self.far().start()

    def t7(self):
        m = self.me
        self.back(10, 1 - m.x, 1 - m.y, m.yn if self.way == 0 else m.xn).wait_recv()
        pl.semaphore_wait(self.free, 1)
        self.core_back().start()

    def t8(self):
        m = self.me
        self.core_back().wait()
        self.back(8, m.x, m.y, m.xn).wait_send()
        self.back(9, m.x, m.y, m.yn).wait_send()
        self.far().wait_send()


class SmallSum:
    def __init__(self, me, small, inbox, sends, recvs, base):
        self.me, self.small, self.inbox = me, small, inbox
        self.sends, self.recvs, self.base = sends, recvs, base

    def copy(self, k, dev):
        return pltpu.make_async_remote_copy(
            src_ref=self.small.at[k], dst_ref=self.inbox.at[k],
            send_sem=self.sends.at[self.base + k], recv_sem=self.recvs.at[self.base + k],
            device_id=dev, device_id_type=MESH_ID,
        )

    def peer(self, k):
        return (self.me.sib, self.me.xn, self.me.yn)[k]

    def step(self, k):
        m = self.me
        if 1 <= k <= 3:
            self.copy(k - 1, self.peer(k - 1)).wait()
            self.small[k] = self.small[k - 1] + self.inbox[k - 1]
        if k <= 2:
            self.copy(k, self.peer(k)).start()
        if k == 3:
            for o in range(1, m.depth):
                self.z_copy(o).start()
        if k == 4:
            total = self.small[3]
            for o in range(1, m.depth):
                self.z_copy(o).wait()
                total = total + self.inbox[2 + o]
            self.small[4] = total

    def z_copy(self, o):
        m = self.me
        at = self.base + 2 + o
        return pltpu.make_async_remote_copy(
            src_ref=self.small.at[3], dst_ref=self.inbox.at[2 + o],
            send_sem=self.sends.at[at], recv_sem=self.recvs.at[at],
            device_id=m.at_z(m.ahead(o)), device_id_type=MESH_ID,
        )


def gather_kernel(depth, wq, wk, wv, wo, up, down, gpad, wa_out, wu_out, wd_out, gains_out,
                  wa, wu, wd, gbox, own_sem, sends, recvs):
    me = Place(depth)
    me.greet()
    own = Owned(me, (wq, wk, wv, wo, up, down), wa, wu, wd, own_sem)
    ag = Gather(me, wa, wu, wd, sends, recvs)
    arrays = range(7)
    gsem = 7 * Gather.SLOTS
    def gcopy(o):
        return pltpu.make_async_remote_copy(
            src_ref=gpad, dst_ref=gbox.at[o - 1], send_sem=sends.at[gsem + o], recv_sem=recvs.at[gsem + o],
            device_id=me.at_z(me.ahead(o)), device_id_type=MESH_ID)
    for o in range(1, depth):
        gcopy(o).start()
    for a in arrays:
        own.start(a)
    for a in arrays:
        own.wait(a)
        ag.send_z(a)
    for t in range(len(arrays) + 3):
        if t < 7:
            for o in range(1, depth):
                ag.spread(t, o)
        if 0 <= t - 1 < 7:
            for o in range(1, depth):
                ag.forward(t - 1, o)
        if 0 <= t - 2 < 7:
            ag.across(t - 2)
        if 0 <= t - 3 < 7:
            ag.ready(t - 3)
    total = gpad[...].astype(F32)
    for o in range(1, depth):
        gcopy(o).wait()
        total = total + gbox[o - 1].astype(F32)
    gains_out[...] = total[:8]
    for a in arrays:
        ag.settle(a)
    outs = [pltpu.make_async_copy(a, b, own_sem.at[i]) for i, (a, b) in enumerate(((wa, wa_out), (wu, wu_out), (wd, wd_out)))]
    for o in outs:
        o.start()
    for o in outs:
        o.wait()


def reduce_scratch(total_depth, rows_a, width, rows_d, ff_c):
    def boxes(n, rows, cols):
        v = lambda *s: pltpu.VMEM((n,) + s + (rows, cols), BF)
        return [v(4, 2, 2), v(2, 2), v(2, 2), v(2), v(2), v(3)]
    return boxes(4, rows_a, width // 2) + boxes(3, rows_a, ff_c // 2) + boxes(3, rows_d, width // 2)


def reducers(me, wa, wu, wd, boxes, sends, recvs, frees):
    out = []
    for w, b, ways in ((wa, boxes[0:6], (0, 1, 0, 1)), (wu, boxes[6:12], (0, 0, 0)), (wd, boxes[12:18], (1, 1, 1))):
        for i, way in enumerate(ways):
            out.append(Reduce(me, w.at[i], *[x.at[i] for x in b], sends, recvs, frees, len(out), way))
    return out


def reduce_kernel(depth, ga, gu, gd, small_in, fa, fu, fd, small_out,
                  wa, wu, wd, small, inbox, load_sem, sends, recvs, frees, *boxes):
    me = Place(depth)
    me.greet()
    loads = [pltpu.make_async_copy(a, b, load_sem.at[i]) for i, (a, b) in enumerate(((ga, wa), (gu, wu), (gd, wd)))]
    for l in loads:
        l.start()
    for l in loads:
        l.wait()
    rs = reducers(me, wa, wu, wd, boxes, sends, recvs, frees)
    order = [4, 7, 5, 8, 6, 9, 3, 0, 1, 2]
    ss = SmallSum(me, small, inbox, sends, recvs, 10 * Reduce.SLOTS)
    small[0] = small_in[...]
    steps = ("t1", "t2", "t3", "t4", "t5", "t6", "t7", "t8")
    for t in range(len(order) + len(steps) - 1):
        for k in range(len(steps)):
            if 0 <= t - k < len(order):
                getattr(rs[order[t - k]], steps[k])()
    for k in range(5):
        ss.step(k)
    small_out[...] = small[4]
    outs = []
    for box, dst in ((boxes[0], fa), (boxes[6], fu), (boxes[12], fd)):
        for h, core in ((0, me.core), (1, 1 - me.core)):
            outs.append(pltpu.make_async_copy(box.at[:, h], dst.at[:, :, :, :, half_of(dst, core)], load_sem.at[len(outs)]))
    for o in outs:
        o.start()
    for o in outs:
        o.wait()


def place_kernel(idx, tokens, cot, new_rows, new_grads, fa, fu, fd,
                 out, grad, gq, gk, gv, go, gup, gdown):
    s = pl.program_id(0)
    length, slots = tokens.shape[0], idx.shape[1]
    spot = lax.broadcasted_iota(jnp.int32, (length, slots), 0)
    hot = jnp.where(spot == idx[pl.ds(s, 1), :], 1.0, 0.0)
    hit = jnp.sum(hot, axis=1, keepdims=True) > 0
    hot = hot.astype(BF)
    for src, rows, dst in ((tokens, new_rows, out), (cot, new_grads, grad)):
        dst[...] = jnp.where(hit, nn(hot, rows[...]), src[...].astype(F32)).astype(BF)
    for m, g in enumerate((gq, gk, gv, go)):
        g[...] = fa[m, 0].astype(F32)
    quarter = 256
    ff_own = gup.shape[1] // 4
    for c in range(CHUNKS):
        for j in range(4):
            gup[:, j * ff_own + c * quarter : j * ff_own + (c + 1) * quarter] = fu[c, 0, :, j * quarter : (j + 1) * quarter].astype(F32)
        gdown[c, 0] = fd[c, 0].astype(F32)


def remote_params(collective_id, limit=60):
    return pltpu.CompilerParams(
        collective_id=collective_id, has_side_effects=True, vmem_limit_bytes=limit * 2**20
    )


def over_groups(groups, terms):
    if groups == 1:
        return terms
    dp = groups * PLANE
    total = [t.astype(F32) for t in terms]
    for k in range(groups.bit_length() - 1):
        hop = PLANE << k
        pairs = [(i, i ^ hop) for i in range(dp)]
        total = [t + lax.ppermute(t, "dp", pairs) for t in total]
    return total


def body(depth, groups, tokens, row_index, row_valid, w_query, w_key, w_value, w_out, w_up, w_down,
         gain_attn, gain_mlp, w_router, cotangent):
    seqs, slots = row_index.shape
    width = tokens.shape[1]
    own = w_query.shape[0]
    ff = w_up.shape[1]
    length = tokens.shape[0] // seqs
    total = seqs * slots
    rq, cw = own // 4, ff // CHUNKS
    dq = w_down.shape[0] // (4 * CHUNKS)
    sd = jax.ShapeDtypeStruct
    hbm, vm = pl.BlockSpec(memory_space=pl.ANY), pl.BlockSpec(memory_space=pltpu.VMEM)
    sem = pltpu.SemaphoreType.DMA
    vmem = pltpu.VMEM
    z = lax.axis_index("fsdp")
    gains3 = jnp.stack([gain_attn, gain_mlp, w_router])
    gpad = lax.dynamic_update_slice(jnp.zeros((16, width), BF), gains3, (0, z * own))
    squares = [w.reshape(2, 2, rq, width) for w in (w_query, w_key, w_value, w_out)]
    sa, su, sdn = (A_MATS, depth, 2, 2, rq, width), (CHUNKS, depth, 2, 2, rq, cw), (CHUNKS, depth, 2, 2, dq, width)
    nag = 7 * Gather.SLOTS + 8
    wa, wu, wd, gains = pl.pallas_call(
        functools.partial(gather_kernel, depth),
        out_shape=(sd(sa, BF), sd(su, BF), sd(sdn, BF), sd((8, width), F32)),
        in_specs=[hbm] * 6 + [vm], out_specs=(hbm, hbm, hbm, vm),
        scratch_shapes=[vmem(sa, BF), vmem(su, BF), vmem(sdn, BF), vmem((depth - 1, 16, width), BF), sem((16,)), sem((nag,)), sem((nag,))],
        compiler_params=remote_params(0),
    )(*squares, w_up.reshape(2, 2, rq, ff), w_down.reshape(CHUNKS, 2, 2, dq, width), gpad)
    rows = (total, width)
    ga, gu, gd, small, new_rows, new_grads = pl.pallas_call(
        compute_kernel,
        out_shape=(sd(sa, BF), sd(su, BF), sd(sdn, BF), sd((8, width), F32), sd(rows, BF), sd(rows, BF)),
        in_specs=[hbm, hbm, vm, vm, hbm, hbm, hbm, vm], out_specs=(hbm, hbm, hbm, vm, vm, vm),
        scratch_shapes=[
            vmem(sa, BF), vmem(su, BF), vmem(sdn, BF), vmem(rows, BF), vmem(rows, BF), vmem((total, 128), F32),
            vmem(rows, BF), vmem((3,) + rows, BF), vmem((seqs * width // 128, 2 * slots, slots), BF), vmem(rows, BF),
            vmem(rows, F32), vmem(rows, BF), vmem((width, total), BF), vmem(rows, BF), vmem((total, cw), BF),
            vmem((total, cw), BF), vmem(rows, F32), vmem(rows, F32), sem((2,)), sem((3,)),
        ],
        compiler_params=pltpu.CompilerParams(vmem_limit_bytes=60 * 2**20),
    )(tokens, cotangent, row_index, row_valid, wa, wu, wd, gains)
    nrs = 10 * Reduce.SLOTS + 8
    fa, fu, fd, sums = pl.pallas_call(
        functools.partial(reduce_kernel, depth),
        out_shape=(sd(sa[:1] + sa[2:], BF), sd(su[:1] + su[2:], BF), sd(sdn[:1] + sdn[2:], BF), sd((8, width), F32)),
        in_specs=[hbm, hbm, hbm, vm], out_specs=(hbm, hbm, hbm, vm),
        scratch_shapes=[vmem(sa, BF), vmem(su, BF), vmem(sdn, BF), vmem((5, 8, width), F32), vmem((2 + depth, 8, width), F32),
                        sem((6,)), sem((nrs,)), sem((nrs,)), pltpu.SemaphoreType.REGULAR((10,))] + reduce_scratch(depth, rq, width, dq, cw),
        compiler_params=remote_params(1),
    )(ga, gu, gd, small)
    fa, fu, fd, sums = over_groups(groups, (fa, fu, fd, sums))
    out, grad, gq, gk, gv, go, gup, gdown = pl.pallas_call(
        place_kernel,
        grid=(seqs,),
        out_shape=(sd(tokens.shape, BF), sd(tokens.shape, BF)) + (sd((own, width), F32),) * 4 + (sd((own, ff), F32), sd((CHUNKS, 4, dq, width), F32)),
        in_specs=[pl.BlockSpec((seqs, slots), lambda s: (0, 0))] + [pl.BlockSpec((length, width), lambda s: (s, 0))] * 2
        + [pl.BlockSpec((slots, width), lambda s: (s, 0))] * 2
        + [pl.BlockSpec((A_MATS, 1, rq, width), lambda s: (0, s, 0, 0)), pl.BlockSpec((CHUNKS, 1, rq, cw), lambda s: (0, s, 0, 0)), pl.BlockSpec((CHUNKS, 1, dq, width), lambda s: (0, s, 0, 0))],
        out_specs=[pl.BlockSpec((length, width), lambda s: (s, 0))] * 2 + [pl.BlockSpec((rq, width), lambda s: (s, 0))] * 4
        + [pl.BlockSpec((rq, ff), lambda s: (s, 0)), pl.BlockSpec((CHUNKS, 1, dq, width), lambda s: (0, s, 0, 0))],
        compiler_params=pltpu.CompilerParams(vmem_limit_bytes=50 * 2**20),
    )(row_index, tokens, cotangent, new_rows, new_grads, fa.reshape(A_MATS, 4, rq, width), fu.reshape(CHUNKS, 4, rq, cw), fd.reshape(CHUNKS, 4, dq, width))
    vec = lax.dynamic_slice(sums, (0, z * own), (3, own))
    return (out, grad, gq, gk, gv, go, gup, gdown.reshape(w_down.shape), vec[0], vec[1], vec[2])


def solution(mesh):
    depth = mesh.shape["fsdp"]
    both = P(("dp", "fsdp"), None)
    weight, vector = P("fsdp", None), P("fsdp")
    return jax.shard_map(
        functools.partial(body, depth, mesh.shape["dp"] // PLANE),
        mesh=mesh,
        in_specs=(both,) * 3 + (weight,) * 6 + (vector,) * 3 + (both,),
        out_specs=(both, both) + (weight,) * 6 + (vector,) * 3,
        check_vma=False,
    )
```

```python
import functools

import jax
import jax.numpy as jnp
from jax import lax
from jax.experimental import pallas as pl
from jax.experimental.pallas import tpu as pltpu

from jax.sharding import PartitionSpec as P

HEADS = 12
EPS = 1e-06
NEG = -1e30
BF = jnp.bfloat16
F32 = jnp.float32
GATE, R1, R2, LIVE, DLOG, POS = range(6)


def nn(a, b):
    return lax.dot_general(a, b, (((1,), (0,)), ((), ())), preferred_element_type=F32)


def nt(a, b):
    return lax.dot_general(a, b, (((1,), (1,)), ((), ())), preferred_element_type=F32)


def tn(a, b):
    return lax.dot_general(a, b, (((0,), (0,)), ((), ())), preferred_element_type=F32)


def flat(v):
    return v.reshape(-1, v.shape[-1])


class Picker:
    def __init__(self, tokens, cot, picked, up, cols, bufs, sems):
        self.srcs, self.dsts, self.cols, self.bufs, self.sems = (tokens, cot), (picked, up), cols, bufs, sems

    def fetch(self, s, b):
        width = self.srcs[b].shape[-1]
        dst = self.bufs[b].at[:, :, :, :, 0:width]
        return pltpu.make_async_copy(self.srcs[b].at[s], dst, self.sems.at[b])

    def start(self, s):
        for b in range(2):
            self.fetch(s, b).start()

    def turn(self, idx, valid):
        seqs, slots = idx.shape
        for what, k in ((idx, POS), (valid, LIVE)):
            rows8 = what[...].astype(F32)
            if seqs < 8:
                rows8 = jnp.concatenate([rows8, jnp.zeros((8 - seqs, slots), F32)], axis=0)
            turned = rows8.T
            for s in range(seqs):
                self.cols[s * slots : (s + 1) * slots, k : k + 1] = turned[:, s : s + 1]

    def pick(self, s, slots, more):
        width = self.srcs[0].shape[-1]
        rows = slice(s * slots, (s + 1) * slots)
        length = self.bufs[0].shape[0] * self.bufs[0].shape[1] * self.bufs[0].shape[2] * self.bufs[0].shape[3]
        lane = lax.broadcasted_iota(jnp.int32, (slots, length), 1).astype(F32)
        hot = jnp.where(lane == self.cols[rows, POS : POS + 1], 1.0, 0.0).astype(BF)
        for b in range(2):
            self.fetch(s, b).wait()
            self.dsts[b][rows, :] = nn(hot, flat(self.bufs[b][:, :, :, :, 0:width])).astype(BF)
            if more:
                self.fetch(s + 1, b).start()


def norm_phase(picked, gains, cols, na, tile=256):
    total = picked.shape[0]

    @pl.loop(0, total // tile)
    def _(i):
        rows = pl.ds(pl.multiple_of(i * tile, tile), tile)
        x = picked[rows, :].astype(F32)
        cols[rows, GATE : GATE + 1] = jax.nn.sigmoid(
            jnp.sum(x * gains[2:3, :], axis=1, keepdims=True)
        )
        r1 = lax.rsqrt(jnp.mean(x * x, axis=1, keepdims=True) + EPS)
        cols[rows, R1 : R1 + 1] = r1
        na[rows, :] = (x * r1 * gains[0:1, :]).astype(BF)


def norm_again(picked, gains, cols, na, tile=256):
    @pl.loop(0, picked.shape[0] // tile)
    def _(i):
        rows = pl.ds(pl.multiple_of(i * tile, tile), tile)
        x = picked[rows, :].astype(F32)
        na[rows, :] = (x * cols[rows, R1 : R1 + 1] * gains[0:1, :]).astype(BF)


def qkv_phase(na, wa, qkv, scale):
    width = na.shape[1]
    for m in range(3):

        @pl.loop(0, width // 256)
        def _(n):
            at = pl.ds(pl.multiple_of(n * 256, 256), 256)
            out = nn(na[...], flat(wa[m, :, :, :, :, at]))
            if m == 0:
                out = out * scale
            qkv[m, :, at] = out.astype(BF)


def two_heads(v2, low_half):
    zero = jnp.zeros_like(v2)
    return jnp.concatenate([jnp.where(low_half, v2, zero), jnp.where(low_half, zero, v2)], axis=0)


def prob_spot(s, p, slots):
    at = pl.ds(pl.multiple_of(s * slots, slots), slots)
    return (p // 2, slice(2 * (p % 2), 2 * (p % 2) + 2), slice(None), slice(None), slice(None), at)


def attention_forward(idx, valid, cols, qkv, probs, mixed, s):
    slots = idx.shape[1]
    width = mixed.shape[1]
    rows = pl.ds(pl.multiple_of(s * slots, slots), slots)
    low_half = lax.broadcasted_iota(jnp.int32, (slots, 128), 1) < 64
    mine = cols[rows, POS : POS + 1]
    other = idx[pl.ds(s, 1), :].astype(F32)
    seen = ((other < mine) & (valid[pl.ds(s, 1), :] > 0)) | (other == mine)
    bias = jnp.where(seen, 0.0, NEG)
    bias = jnp.concatenate([bias, bias], axis=0)
    for p in range(width // 128):
        at = slice(p * 128, p * 128 + 128)
        q2 = two_heads(qkv[0, rows, at], low_half)
        scores = nt(q2, qkv[1, rows, at]) + bias
        e = jnp.exp(scores - jnp.max(scores, axis=1, keepdims=True))
        pr = (e * (1.0 / jnp.sum(e, axis=1, keepdims=True))).astype(BF)
        spot = prob_spot(s, p, slots)
        probs[spot] = pr.reshape(2, 2, 2, 64, slots)
        o = nn(pr, qkv[2, rows, at])
        mixed[rows, at] = jnp.where(low_half, o[:slots], o[slots:]).astype(BF)


def attention_backward(qkv, probs, mixed, dmix, s, slots, scale):
    width = mixed.shape[1]
    rows = pl.ds(pl.multiple_of(s * slots, slots), slots)
    low_half = lax.broadcasted_iota(jnp.int32, (slots, 128), 1) < 64
    for p in range(width // 128):
        at = slice(p * 128, p * 128 + 128)
        do2 = two_heads(dmix[rows, at], low_half)
        o2 = mixed[rows, at].astype(F32)
        o2 = jnp.concatenate([o2, o2], axis=0)
        delta = jnp.sum(do2.astype(F32) * o2, axis=1, keepdims=True)
        k2 = qkv[1, rows, at]
        dp = nt(do2, qkv[2, rows, at])
        pr = flat(probs[prob_spot(s, p, slots)])
        ds = (pr.astype(F32) * (dp - delta)).astype(BF)
        q2 = two_heads(qkv[0, rows, at], low_half)
        dq = nn(ds, k2) * scale
        qkv[0, rows, at] = jnp.where(low_half, dq[:slots], dq[slots:]).astype(BF)
        qkv[1, rows, at] = tn(ds, q2).astype(BF)
        qkv[2, rows, at] = tn(pr, do2).astype(BF)


def out_phase(mixed, wa, attn_out):
    width = mixed.shape[1]

    @pl.loop(0, width // 256)
    def _(n):
        at = pl.ds(pl.multiple_of(n * 256, 256), 256)
        attn_out[:, at] = nn(mixed[...], flat(wa[3, :, :, :, :, at]))


def mid_norm(picked, attn_out, up, gains, cols, nm, nmt, dd, tile=256):
    total = picked.shape[0]
    for i in range(total // tile):
        rows = slice(i * tile, (i + 1) * tile)
        hidden = picked[rows, :].astype(F32) + cols[rows, GATE : GATE + 1] * attn_out[rows, :]
        r2 = lax.rsqrt(jnp.mean(hidden * hidden, axis=1, keepdims=True) + EPS)
        cols[rows, R2 : R2 + 1] = r2
        normed = (hidden * r2 * gains[1:2, :]).astype(BF)
        nm[rows, :] = normed
        nmt[:, rows] = normed.T
        dd[rows, :] = (up[rows, :].astype(F32) * cols[rows, LIVE : LIVE + 1]).astype(BF)


def gelu_both(u):
    k = 0.7978845608028654
    u2 = u * u
    t = jnp.tanh(u * (k + (k * 0.044715) * u2))
    half = 0.5 + 0.5 * t
    act = u * half
    slope = half + act * (1.0 - t) * (k + (3 * k * 0.044715) * u2)
    return act, slope


def mlp_up(nm, dd, wu, wd, act, dup, c, n):
    at = pl.ds(pl.multiple_of(n * 256, 256), 256)
    u = nn(nm[...], flat(wu[c, :, :, :, :, at]))
    dact = nt(dd[...], flat(wd[c, n]))
    a, slope = gelu_both(u)
    shape = act.shape[:4] + (256,)
    act[:, :, :, :, at] = a.astype(BF).reshape(shape)
    dup[:, :, :, :, at] = (slope * dact).astype(BF).reshape(shape)


def mlp_down(act, wd, down, c):
    @pl.loop(0, down.shape[1] // 256)
    def _(n):
        at = pl.ds(pl.multiple_of(n * 256, 256), 256)
        out = nn(flat(act[...]), flat(wd[c, :, :, :, :, at]))
        down[:, at] = out if c == 0 else down[:, at] + out


def mlp_dnormed(dup, wu, dnm, c):
    @pl.loop(0, 2)
    def _(i):
        half = dnm.shape[0] // 2
        rows = pl.ds(pl.multiple_of(i * half, half), half)
        out = nt(flat(dup[pl.ds(2 * i, 2)]), flat(wu[c]))
        dnm[rows, :] = out if c == 0 else dnm[rows, :] + out


def mlp_grad_down(act, dd, wd, c):
    @pl.loop(0, act.shape[-1] // 256)
    def _(n):
        at = pl.ds(pl.multiple_of(n * 256, 256), 256)
        g = tn(flat(act[:, :, :, :, at]), dd[...]).astype(BF)
        wd[c, n] = g.reshape(wd.shape[2:])


def mlp_grad_up(nmt, dup, wu, c):
    @pl.loop(0, dup.shape[-1] // 256)
    def _(n):
        at = pl.ds(pl.multiple_of(n * 256, 256), 256)
        g = nn(nmt[...], flat(dup[:, :, :, :, at])).astype(BF)
        wu[c, :, :, :, :, at] = g.reshape(wu.shape[1:5] + (256,))


def mid_backward(picked, attn_out, up, down, dnm, gains, cols, datt, new_rows, small, tile=128):
    total = picked.shape[0]
    small[...] = jnp.zeros_like(small)

    @pl.loop(0, total // tile)
    def _(i):
        rows = pl.ds(pl.multiple_of(i * tile, tile), tile)
        x = picked[rows, :].astype(F32)
        gate = cols[rows, GATE : GATE + 1]
        live = cols[rows, LIVE : LIVE + 1]
        r = cols[rows, R2 : R2 + 1]
        ao = attn_out[rows, :]
        branch = gate * ao
        hidden = x + branch
        new_rows[rows, :] = (x + live * (branch + down[rows, :])).astype(BF)
        d = dnm[rows, :]
        hr = hidden * r
        dh = d * hr
        small[1:2, :] += jnp.sum(dh, axis=0, keepdims=True)
        mean = jnp.mean(dh * gains[1:2, :], axis=1, keepdims=True)
        d_hidden = r * (gains[1:2, :] * d - hr * mean)
        dnm[rows, :] = d_hidden
        d_branch = live * up[rows, :].astype(F32) + d_hidden
        d_logit = jnp.sum(d_branch * ao, axis=1, keepdims=True) * gate * (1.0 - gate)
        cols[rows, DLOG : DLOG + 1] = d_logit
        small[2:3, :] += jnp.sum(x * d_logit, axis=0, keepdims=True)
        datt[rows, :] = (d_branch * gate).astype(BF)


def out_backward(datt, mixed, wa, dmix):
    total, width = datt.shape

    @pl.loop(0, 2)
    def _(i):
        half = total // 2
        rows = pl.ds(pl.multiple_of(i * half, half), half)
        dmix[rows, :] = nt(datt[rows, :], flat(wa[3])).astype(BF)

    wa[3] = grad_of(mixed, datt[...]).reshape(wa.shape[1:])


def grad_of(left, right):
    parts = [tn(left[:, n * 384 : n * 384 + 384], right).astype(BF) for n in range(2)]
    return jnp.concatenate(parts, axis=0)


def qkv_normed(dqkv, wa, dnorm):
    total = dqkv.shape[1]

    @pl.loop(0, 4)
    def _(i):
        part = total // 4
        rows = pl.ds(pl.multiple_of(i * part, part), part)
        dnorm[rows, :] = (
            nt(dqkv[0, rows, :], flat(wa[0]))
            + nt(dqkv[1, rows, :], flat(wa[1]))
            + nt(dqkv[2, rows, :], flat(wa[2]))
        )


def first_backward(picked, up, dnorm, dhid, gains, cols, new_grads, small, tile=128):
    total = picked.shape[0]

    @pl.loop(0, total // tile)
    def _(i):
        rows = pl.ds(pl.multiple_of(i * tile, tile), tile)
        x = picked[rows, :].astype(F32)
        r = cols[rows, R1 : R1 + 1]
        d = dnorm[rows, :]
        xr = x * r
        dx = d * xr
        small[0:1, :] += jnp.sum(dx, axis=0, keepdims=True)
        mean = jnp.mean(dx * gains[0:1, :], axis=1, keepdims=True)
        d_first = r * (gains[0:1, :] * d - xr * mean)
        d_picked = d_first + dhid[rows, :] + cols[rows, DLOG : DLOG + 1] * gains[2:3, :]
        new_grads[rows, :] = (up[rows, :].astype(F32) + d_picked).astype(BF)


MESH_ID = pl.DeviceIdType.MESH
A_MATS, CHUNKS, PLANE = 4, 3, 8


class Place:
    def __init__(self, depth):
        dp = lax.axis_index("dp")
        self.depth = depth
        self.z = lax.axis_index("fsdp")
        self.core = lax.rem(dp, 2)
        self.x = lax.rem(lax.div(dp, 2), 2)
        self.y = lax.rem(lax.div(dp, 4), 2)
        self.sib = (dp + 1 - 2 * self.core, self.z)
        self.xn = (dp + 2 - 4 * self.x, self.z)
        self.yn = (dp + 4 - 8 * self.y, self.z)
        self.dp = dp

    def ahead(self, o):
        return lax.rem(self.z + o, self.depth)

    def behind(self, o):
        return lax.rem(self.z + self.depth - o, self.depth)

    def at_z(self, z):
        return (self.dp, z)

    def greet(self):
        barrier = pltpu.get_barrier_semaphore()
        peers = [self.sib, self.xn, self.yn]
        peers += [self.at_z(self.ahead(o)) for o in range(1, self.depth)]
        for peer in peers:
            pl.semaphore_signal(barrier, inc=1, device_id=peer, device_id_type=MESH_ID)
        pl.semaphore_wait(barrier, len(peers))


def half_of(ref, core):
    width = ref.shape[-1] // 2
    return pl.ds(pl.multiple_of(core * width, 128), width)


class Gather:
    SLOTS = 18

    def __init__(self, me, wa, wu, wd, sends, recvs):
        self.me, self.refs, self.sends, self.recvs = me, (wa, wu, wd), sends, recvs

    def piece(self, a, zi, xi, yi, core):
        wa, wu, wd = self.refs
        if a == 0:
            return wa.at[:, zi, xi, yi, :, half_of(wa, core)]
        ref = wu if a % 2 else wd
        return ref.at[(a - 1) // 2, zi, xi, yi, :, half_of(ref, core)]

    def part(self, a, zi, xi, yi, core, h):
        wa = self.refs[0]
        if a == 0:
            return wa.at[2 * h : 2 * h + 2, zi, xi, yi, :, half_of(wa, core)]
        return self.piece(a, zi, xi, yi, core)

    def ways(self, a):
        return (0, 1) if a == 0 else ((0,) if a % 2 else (1,))

    def copy(self, a, k, ref, dev):
        at = a * self.SLOTS + k
        return pltpu.make_async_remote_copy(
            src_ref=ref, dst_ref=ref, send_sem=self.sends.at[at], recv_sem=self.recvs.at[at],
            device_id=dev, device_id_type=MESH_ID,
        )

    def z_out(self, a, o):
        m = self.me
        return self.copy(a, o, self.piece(a, m.z, m.x, m.y, m.core), m.at_z(m.ahead(o)))

    def x_out(self, a, o):
        m = self.me
        return self.copy(a, 3 + o, self.piece(a, m.behind(o), m.x, m.y, m.core), m.xn)

    def y_out(self, a, o):
        m = self.me
        return self.copy(a, 6 + o, self.piece(a, m.behind(o), m.x, m.y, m.core), m.yn)

    def far_out(self, a, o, h):
        m = self.me
        if h == 0:
            return self.copy(a, 9 + o, self.part(a, m.behind(o), 1 - m.x, m.y, m.core, 0), m.yn)
        return self.copy(a, 12 + o, self.part(a, m.behind(o), m.x, 1 - m.y, m.core, 1), m.xn)

    def core_out(self, a):
        m = self.me
        wa, wu, wd = self.refs
        if a == 0:
            ref = wa.at[:, :, :, :, :, half_of(wa, m.core)]
        else:
            ref = wu if a % 2 else wd
            ref = ref.at[(a - 1) // 2, :, :, :, :, half_of(ref, m.core)]
        return self.copy(a, 0, ref, m.sib)

    def z_in(self, a, o):
        m = self.me
        return self.copy(a, o, self.piece(a, m.behind(o), m.x, m.y, m.core), m.at_z(m.behind(o)))

    def x_in(self, a, o):
        m = self.me
        return self.copy(a, 3 + o, self.piece(a, m.behind(o), 1 - m.x, m.y, m.core), m.xn)

    def y_in(self, a, o):
        m = self.me
        return self.copy(a, 6 + o, self.piece(a, m.behind(o), m.x, 1 - m.y, m.core), m.yn)

    def far_in(self, a, o, h):
        m = self.me
        part = self.part(a, m.behind(o), 1 - m.x, 1 - m.y, m.core, h)
        return self.copy(a, (9 if h == 0 else 12) + o, part, m.yn if h == 0 else m.xn)

    def core_in(self, a):
        m = self.me
        wa, wu, wd = self.refs
        if a == 0:
            ref = wa.at[:, :, :, :, :, half_of(wa, 1 - m.core)]
        else:
            ref = wu if a % 2 else wd
            ref = ref.at[(a - 1) // 2, :, :, :, :, half_of(ref, 1 - m.core)]
        return self.copy(a, 0, ref, m.sib)

    def origins(self):
        return range(1, self.me.depth)

    def send_z(self, a):
        for o in self.origins():
            self.z_out(a, o).start()

    def spread(self, a, o):
        self.z_in(a, o).wait_recv()
        self.x_out(a, o).start()
        self.y_out(a, o).start()

    def forward(self, a, o):
        self.x_in(a, o).wait_recv()
        if 0 in self.ways(a):
            self.far_out(a, o, 0).start()
        self.y_in(a, o).wait_recv()
        if 1 in self.ways(a):
            self.far_out(a, o, 1).start()

    def across(self, a):
        for o in self.origins():
            for h in self.ways(a):
                self.far_in(a, o, h).wait_recv()
        self.core_out(a).start()

    def ready(self, a):
        self.core_in(a).wait_recv()

    def settle(self, a):
        for o in self.origins():
            self.z_out(a, o).wait_send()
            self.x_out(a, o).wait_send()
            self.y_out(a, o).wait_send()
            for h in self.ways(a):
                self.far_out(a, o, h).wait_send()
        self.core_out(a).wait_send()


class Owned:
    def __init__(self, me, shards, wa, wu, wd, sems):
        wq, wk, wv, wo, up, down = shards
        z, core = me.z, me.core
        half = half_of(wa, core)
        self.copies = {0: [], 1: [], 2: [], 3: [], 4: [], 5: [], 6: []}
        for m, w in enumerate((wq, wk, wv, wo)):
            self.copies[0].append((w.at[:, :, :, half], wa.at[m, z, :, :, :, half]))
        ff_own = up.shape[-1] // me.depth
        for c in range(CHUNKS):
            for j in range(2):
                block = 2 * core + j
                src = up.at[:, :, :, pl.ds(pl.multiple_of(block * ff_own + c * 256, 128), 256)]
                dst = wu.at[c, z, :, :, :, pl.ds(pl.multiple_of(block * 256, 128), 256)]
                self.copies[1 + 2 * c].append((src, dst))
            self.copies[2 + 2 * c].append((down.at[c, :, :, :, half], wd.at[c, z, :, :, :, half]))
        self.sems = sems

    def all_of(self, a):
        base = sum(len(self.copies[b]) for b in range(a))
        for i, (src, dst) in enumerate(self.copies[a]):
            yield pltpu.make_async_copy(src, dst, self.sems.at[base + i])

    def start(self, a):
        for c in self.all_of(a):
            c.start()

    def wait(self, a):
        for c in self.all_of(a):
            c.wait()


class Reduce:
    SLOTS = 14

    def __init__(
        self, me, w, from_core, from_x, from_y, then_x, then_y, from_z, sends, recvs, frees, at, way
    ):
        self.me, self.w, self.way, self.free, base = me, w, way, frees.at[at], at * self.SLOTS
        self.from_core, self.from_x, self.from_y = from_core, from_x, from_y
        self.then_x, self.then_y, self.from_z = then_x, then_y, from_z
        self.sends, self.recvs, self.base = sends, recvs, base
        self.mine, self.theirs = half_of(w, me.core), half_of(w, 1 - me.core)

    def copy(self, k, src, dst, dev):
        at = self.base + k
        return pltpu.make_async_remote_copy(
            src_ref=src, dst_ref=dst, send_sem=self.sends.at[at], recv_sem=self.recvs.at[at],
            device_id=dev, device_id_type=MESH_ID,
        )

    def core_copy(self):
        return self.copy(0, self.w.at[:, :, :, :, self.theirs], self.from_core, self.me.sib)

    def plane_first(self):
        m, w = self.me, self.w
        return (
            self.copy(1, w.at[0:2, 1 - m.x, :, :, self.mine], self.from_x, m.xn),
            self.copy(2, w.at[2:4, :, 1 - m.y, :, self.mine], self.from_y, m.yn),
        )

    def plane_second(self):
        m, w = self.me, self.w
        return (
            self.copy(3, w.at[0:2, m.x, 1 - m.y, :, self.mine], self.then_y, m.yn),
            self.copy(4, w.at[2:4, 1 - m.x, m.y, :, self.mine], self.then_x, m.xn),
        )

    def z_copy(self, o):
        m = self.me
        src = self.w.at[m.ahead(o), m.x, m.y, :, self.mine]
        return self.copy(4 + o, src, self.from_z.at[o - 1], m.at_z(m.ahead(o)))

    def back(self, k, xi, yi, dev):
        ref = self.from_core.at[0, xi, yi]
        return self.copy(k, ref, ref, dev)

    def core_back(self):
        return self.copy(11, self.from_core.at[0], self.from_core.at[1], self.me.sib)

    def add(self, at, arrived):
        self.w[at] = (self.w[at].astype(F32) + arrived.astype(F32)).astype(BF)

    def t1(self):
        self.core_copy().start()

    def t2(self):
        m = self.me
        self.core_copy().wait()

        @pl.loop(0, 2 * m.depth)
        def _(i):
            zi, xi = lax.div(i, 2), lax.rem(i, 2)
            self.add((zi, xi, slice(None), slice(None), self.mine), self.from_core[zi, xi])

        pl.semaphore_signal(self.free, inc=1, device_id=m.sib, device_id_type=MESH_ID)
        for c in self.plane_first():
            c.start()

    def t3(self):
        m = self.me
        first = self.plane_first()
        first[0].wait()
        for zi in range(2):
            self.add((zi, m.x, slice(None), slice(None), self.mine), self.from_x[zi])
        first[1].wait()
        for zi in range(2):
            self.add((2 + zi, slice(None), m.y, slice(None), self.mine), self.from_y[zi])
        for c in self.plane_second():
            c.start()

    def t4(self):
        m = self.me
        second = self.plane_second()
        second[0].wait()
        self.add((slice(0, 2), m.x, m.y, slice(None), self.mine), self.then_y[...])
        second[1].wait()
        self.add((slice(2, 4), m.x, m.y, slice(None), self.mine), self.then_x[...])
        for o in range(1, m.depth):
            self.z_copy(o).start()

    def t5(self):
        m = self.me
        at = (m.z, m.x, m.y, slice(None), self.mine)
        total = self.w[at].astype(F32)
        for o in range(1, m.depth):
            self.z_copy(o).wait()
            total = total + self.from_z[o - 1].astype(F32)
        self.from_core[0, m.x, m.y] = total.astype(BF)
        self.back(8, m.x, m.y, m.xn).start()
        self.back(9, m.x, m.y, m.yn).start()

    def far(self):
        m = self.me
        if self.way == 0:
            return self.back(10, 1 - m.x, m.y, m.yn)
        return self.back(10, m.x, 1 - m.y, m.xn)

    def t6(self):
        m = self.me
        self.back(8, 1 - m.x, m.y, m.xn).wait_recv()
        self.back(9, m.x, 1 - m.y, m.yn).wait_recv()
        self.far().start()

    def t7(self):
        m = self.me
        self.back(10, 1 - m.x, 1 - m.y, m.yn if self.way == 0 else m.xn).wait_recv()
        pl.semaphore_wait(self.free, 1)
        self.core_back().start()

    def t8(self):
        m = self.me
        self.core_back().wait()
        self.back(8, m.x, m.y, m.xn).wait_send()
        self.back(9, m.x, m.y, m.yn).wait_send()
        self.far().wait_send()


class SmallSum:
    def __init__(self, me, small, inbox, sends, recvs, base):
        self.me, self.small, self.inbox = me, small, inbox
        self.sends, self.recvs, self.base = sends, recvs, base

    def copy(self, k, dev):
        return pltpu.make_async_remote_copy(
            src_ref=self.small.at[k], dst_ref=self.inbox.at[k],
            send_sem=self.sends.at[self.base + k], recv_sem=self.recvs.at[self.base + k],
            device_id=dev, device_id_type=MESH_ID,
        )

    def peer(self, k):
        return (self.me.sib, self.me.xn, self.me.yn)[k]

    def step(self, k):
        m = self.me
        if 1 <= k <= 3:
            self.copy(k - 1, self.peer(k - 1)).wait()
            self.small[k] = self.small[k - 1] + self.inbox[k - 1]
        if k <= 2:
            self.copy(k, self.peer(k)).start()
        if k == 3:
            for o in range(1, m.depth):
                self.z_copy(o).start()
        if k == 4:
            total = self.small[3]
            for o in range(1, m.depth):
                self.z_copy(o).wait()
                total = total + self.inbox[2 + o]
            self.small[4] = total

    def z_copy(self, o):
        m = self.me
        at = self.base + 2 + o
        return pltpu.make_async_remote_copy(
            src_ref=self.small.at[3], dst_ref=self.inbox.at[2 + o],
            send_sem=self.sends.at[at], recv_sem=self.recvs.at[at],
            device_id=m.at_z(m.ahead(o)), device_id_type=MESH_ID,
        )


def chunk_boxes(rows_a, width, rows_d, ff_c):
    def boxes(n, rows, cols, first):
        def box(*lead):
            return pltpu.VMEM((n,) + lead + (rows, cols), BF)

        return ([box(4, 2, 2)] if first else []) + [box(2, 2), box(2, 2), box(2), box(2), box(3)]

    return (
        boxes(CHUNKS, rows_a, ff_c // 2, True)
        + boxes(CHUNKS, rows_d, width // 2, True)
        + boxes(A_MATS, rows_a, width // 2, False)
    )


def block_kernel(
    depth, tokens, cot, idx, valid, wq, wk, wv, wo, up_in, down_in, gpad,
    new_rows, new_grads, fa, fu, fd, small_out,
    wa, wu, wd, picked, up, cols, na, nmt, dd, qkv, probs, mixed, attn_out, act, dup, down, dnm,
    gains, gbox, small, inbox,
    tok_sem, own_sem, out_sem, ag_send, ag_recv, rs_send, rs_recv, frees, opened, *boxes,
):
    seqs, slots = idx.shape
    width = picked.shape[1]
    scale = (width // HEADS) ** -0.5
    rows_a = wa.shape[-2]
    half = width // 2
    me = Place(depth)
    me.greet()
    own = Owned(me, (wq, wk, wv, wo, up_in, down_in), wa, wu, wd, own_sem)
    ag = Gather(me, wa, wu, wd, ag_send, ag_recv)
    gsem = 7 * Gather.SLOTS
    others = range(1, depth)

    def gain_copy(o):
        return pltpu.make_async_remote_copy(
            src_ref=gpad, dst_ref=gbox.at[o - 1], send_sem=ag_send.at[gsem + o], recv_sem=ag_recv.at[gsem + o],
            device_id=me.at_z(me.ahead(o)), device_id_type=MESH_ID,
        )

    def spread(*arrays):
        for a in arrays:
            for o in others:
                ag.spread(a, o)

    def forward(*arrays):
        for a in arrays:
            for o in others:
                ag.forward(a, o)

    def across(*arrays):
        for a in arrays:
            ag.across(a)

    own.start(0)
    picker = Picker(tokens, cot, picked, up, cols, (act, dup), tok_sem)
    for a in range(1, 7):
        own.start(a)
    picker.start(0)
    own.wait(0)
    ag.send_z(0)
    for o in others:
        gain_copy(o).start()
    for a in range(1, 7):
        own.wait(a)
        ag.send_z(a)
    picker.turn(idx, valid)
    picker.pick(0, slots, True)
    picker.pick(1, slots, True)
    spread(0)
    picker.pick(2, slots, True)
    picker.pick(3, slots, False)
    total = gpad[...].astype(F32)
    for o in others:
        gain_copy(o).wait()
        total = total + gbox[o - 1].astype(F32)
    gains[...] = total[:8]
    norm_phase(picked, gains, cols, na)
    forward(0)
    spread(1, 2)
    across(0)
    ag.ready(0)
    qkv_phase(na, wa, qkv, scale)
    spread(3, 4)
    forward(1, 2)

    @pl.loop(0, seqs)
    def _(s):
        attention_forward(idx, valid, cols, qkv, probs, mixed, s)

        @pl.when(s == 0)
        def _():
            across(1, 2)
            spread(5, 6)
            forward(3, 4)

        @pl.when(s == 1)
        def _():
            across(3, 4)
            forward(5, 6)

        @pl.when(s == 2)
        def _():
            across(5, 6)

    out_phase(mixed, wa, attn_out)
    mid_norm(picked, attn_out, up, gains, cols, na, nmt, dd)

    ubox, dbox, abox = boxes[0:6], boxes[6:12], boxes[12:17]
    reducers = {}

    def reducer(name, at, w, core_box, rest, i, way):
        reducers[name] = Reduce(me, w, core_box, *[x.at[i] for x in rest], rs_send, rs_recv, frees, at, way)

    for c in range(CHUNKS):
        reducer("u%d" % c, c, wu.at[c], ubox[0].at[c], ubox[1:], c, 0)
        reducer("d%d" % c, 3 + c, wd.at[c], dbox[0].at[c], dbox[1:], c, 1)
    spots = ((act, 0), (act, half), (dup, 0), (dup, half))
    terms = [probs.at[m, :, :, :, 0:rows_a, 0:width] for m in range(3)] + [wa.at[3]]
    for m, name in enumerate("qkvo"):
        ref, lane = spots[m]
        box = ref.at[:, :, :, 0:rows_a, lane : lane + half]
        reducer(name, 6 + m, terms[m], box, abox, m, m % 2)
    finals = {"q": (fa, 0), "k": (fa, 1), "v": (fa, 2), "o": (fa, 3)}
    for c in range(CHUNKS):
        finals["u%d" % c] = (fu, c)
        finals["d%d" % c] = (fd, c)
    order = list(finals)

    def result_copies(name):
        dst, i = finals[name]
        box = reducers[name].from_core
        base = 2 * order.index(name)
        for h, core in ((0, me.core), (1, 1 - me.core)):
            yield pltpu.make_async_copy(box.at[h], dst.at[i, :, :, :, half_of(dst, core)], out_sem.at[base + h])

    def step(k, *names):
        for name in names:
            getattr(reducers[name], "t%d" % k)()
            if k == 8:
                for c in result_copies(name):
                    c.start()

    for c in range(CHUNKS):
        for a in (1 + 2 * c, 2 + 2 * c):
            ag.ready(a)

        @pl.loop(0, 4)
        def _(n):
            mlp_up(na, dd, wu, wd, act, dup, c, n)

        if c == 1:
            step(2, "u0", "d0")
        if c == 2:
            step(4, "u0", "d0")
            step(2, "u1", "d1")
        mlp_down(act, wd, down, c)
        mlp_dnormed(dup, wu, dnm, c)
        if c == 2:
            step(5, "u0", "d0")
        ag.settle(1 + 2 * c)
        ag.settle(2 + 2 * c)
        mlp_grad_down(act, dd, wd, c)
        step(1, "d%d" % c)
        mlp_grad_up(nmt, dup, wu, c)
        step(1, "u%d" % c)
        if c == 1:
            step(3, "u0", "d0")
        if c == 2:
            step(3, "u1", "d1")
            step(6, "u0", "d0")
    pl.semaphore_signal(opened, inc=1, device_id=me.sib, device_id_type=MESH_ID)
    ag.settle(0)
    datt, dmix = na, dd
    mid_backward(picked, attn_out, up, down, dnm, gains, cols, datt, dd, small.at[0])
    rows_out = pltpu.make_async_copy(dd, new_rows, tok_sem.at[0])
    rows_out.start()
    step(2, "u2", "d2")
    step(4, "u1", "d1")
    step(7, "u0", "d0")
    rows_out.wait()
    out_backward(datt, mixed, wa, dmix)
    pl.semaphore_wait(opened, 1)
    step(1, "o")
    step(8, "u0", "d0")
    norm_again(picked, gains, cols, na)

    @pl.loop(0, seqs)
    def _(s):
        attention_backward(qkv, probs, mixed, dmix, s, slots, scale)

        @pl.when(s == 0)
        def _():
            step(3, "u2", "d2")
            step(5, "u1", "d1")
            step(2, "o")

        @pl.when(s == 1)
        def _():
            step(4, "u2", "d2")
            step(6, "u1", "d1")
            step(3, "o")

        @pl.when(s == 2)
        def _():
            step(5, "u2", "d2")
            step(7, "u1", "d1")
            step(4, "o")

    for m, name in enumerate("qkv"):
        terms[m][...] = grad_of(na, qkv[m]).reshape(wa.shape[1:])
        step(1, name)
        if m > 0:
            step(2, "qkv"[m - 1])
    step(6, "u2", "d2")
    step(8, "u1", "d1")
    step(5, "o")
    qkv_normed(qkv, wa, down)
    step(2, "v")
    first_backward(picked, up, down, dnm, gains, cols, dd, small.at[0])
    grads_out = pltpu.make_async_copy(dd, new_grads, tok_sem.at[1])
    grads_out.start()
    sums = SmallSum(me, small, inbox, rs_send, rs_recv, 10 * Reduce.SLOTS)
    sums.step(0)
    step(3, *"qkv")
    step(7, "u2", "d2")
    step(6, "o")
    sums.step(1)
    step(4, *"qkv")
    sums.step(2)
    step(8, "u2", "d2")
    step(7, "o")
    sums.step(3)
    step(5, *"qkv")
    step(8, "o")
    step(6, *"qkv")
    sums.step(4)
    step(7, *"qkv")
    step(8, *"qkv")
    small_out[...] = small[4]
    for name in order:
        for c in result_copies(name):
            c.wait()
    grads_out.wait()


def place_kernel(idx, tokens, cot, new_rows, new_grads, fa, fu, fd,
                 out, grad, gq, gk, gv, go, gup, gdown):
    s = pl.program_id(0)
    length, slots = tokens.shape[0], idx.shape[1]
    spot = lax.broadcasted_iota(jnp.int32, (length, slots), 0)
    hot = jnp.where(spot == idx[pl.ds(s, 1), :], 1.0, 0.0)
    hit = jnp.sum(hot, axis=1, keepdims=True) > 0
    hot = hot.astype(BF)
    for src, rows, dst in ((tokens, new_rows, out), (cot, new_grads, grad)):
        dst[...] = jnp.where(hit, nn(hot, rows[...]), src[...].astype(F32)).astype(BF)
    for m, g in enumerate((gq, gk, gv, go)):
        g[...] = fa[m, 0].astype(F32)
    quarter = 256
    ff_own = gup.shape[1] // 4
    for c in range(CHUNKS):
        for j in range(4):
            gup[:, j * ff_own + c * quarter : j * ff_own + (c + 1) * quarter] = fu[c, 0, :, j * quarter : (j + 1) * quarter].astype(F32)
        gdown[c, 0] = fd[c, 0].astype(F32)


def remote_params(collective_id, limit=60):
    return pltpu.CompilerParams(
        collective_id=collective_id, has_side_effects=True, vmem_limit_bytes=limit * 2**20
    )


def over_groups(groups, terms):
    if groups == 1:
        return terms
    dp = groups * PLANE
    total = [t.astype(F32) for t in terms]
    for k in range(groups.bit_length() - 1):
        hop = PLANE << k
        pairs = [(i, i ^ hop) for i in range(dp)]
        total = [t + lax.ppermute(t, "dp", pairs) for t in total]
    return total


def body(depth, groups, tokens, row_index, row_valid, w_query, w_key, w_value, w_out, w_up, w_down,
         gain_attn, gain_mlp, w_router, cotangent):
    seqs, slots = row_index.shape
    width = tokens.shape[1]
    own = w_query.shape[0]
    ff = w_up.shape[1]
    length = tokens.shape[0] // seqs
    total = seqs * slots
    rq, cw = own // 4, ff // CHUNKS
    dq = w_down.shape[0] // (4 * CHUNKS)
    sd = jax.ShapeDtypeStruct
    hbm, vm = pl.BlockSpec(memory_space=pl.ANY), pl.BlockSpec(memory_space=pltpu.VMEM)
    sem = pltpu.SemaphoreType.DMA
    vmem = pltpu.VMEM
    z = lax.axis_index("fsdp")
    gains3 = jnp.stack([gain_attn, gain_mlp, w_router])
    gpad = lax.dynamic_update_slice(jnp.zeros((16, width), BF), gains3, (0, z * own))
    squares = [w.reshape(2, 2, rq, width) for w in (w_query, w_key, w_value, w_out)]
    sa, su, sdn = (A_MATS, depth, 2, 2, rq, width), (CHUNKS, depth, 2, 2, rq, cw), (CHUNKS, depth, 2, 2, dq, width)
    nag, nrs = 7 * Gather.SLOTS + 8, 10 * Reduce.SLOTS + 8
    rows = (total, width)
    work = (4, 2, 2, total // 16, cw)
    regular = pltpu.SemaphoreType.REGULAR
    blocks = (seqs, 4, 2, 2, length // 16, width)
    new_rows, new_grads, fa, fu, fd, sums = pl.pallas_call(
        functools.partial(block_kernel, depth),
        out_shape=(
            sd(rows, BF), sd(rows, BF), sd(sa[:1] + sa[2:], BF), sd(su[:1] + su[2:], BF), sd(sdn[:1] + sdn[2:], BF),
            sd((8, width), F32),
        ),
        in_specs=[hbm, hbm, vm, vm] + [hbm] * 6 + [vm],
        out_specs=(hbm,) * 5 + (vm,),
        scratch_shapes=[
            vmem(sa, BF), vmem(su, BF), vmem(sdn, BF), vmem(rows, BF), vmem(rows, BF), vmem((total, 128), F32),
            vmem(rows, BF), vmem((width, total), BF), vmem(rows, BF), vmem((3,) + rows, BF), vmem((3,) + work, BF),
            vmem(rows, BF), vmem(rows, F32), vmem(work, BF), vmem(work, BF), vmem(rows, F32), vmem(rows, F32),
            vmem((8, width), F32), vmem((depth - 1, 16, width), BF), vmem((5, 8, width), F32), vmem((2 + depth, 8, width), F32),
            sem((2,)), sem((16,)), sem((20,)), sem((nag,)), sem((nag,)), sem((nrs,)), sem((nrs,)), regular((10,)), regular,
        ]
        + chunk_boxes(rq, width, dq, cw),
        compiler_params=remote_params(0, 63),
    )(
        tokens.reshape(blocks), cotangent.reshape(blocks), row_index, row_valid, *squares,
        w_up.reshape(2, 2, rq, ff), w_down.reshape(CHUNKS, 2, 2, dq, width), gpad,
    )
    fa, fu, fd, sums = over_groups(groups, (fa, fu, fd, sums))
    out, grad, gq, gk, gv, go, gup, gdown = pl.pallas_call(
        place_kernel,
        grid=(seqs,),
        out_shape=(sd(tokens.shape, BF), sd(tokens.shape, BF)) + (sd((own, width), F32),) * 4 + (sd((own, ff), F32), sd((CHUNKS, 4, dq, width), F32)),
        in_specs=[pl.BlockSpec((seqs, slots), lambda s: (0, 0))] + [pl.BlockSpec((length, width), lambda s: (s, 0))] * 2
        + [pl.BlockSpec((slots, width), lambda s: (s, 0))] * 2
        + [pl.BlockSpec((A_MATS, 1, rq, width), lambda s: (0, s, 0, 0)), pl.BlockSpec((CHUNKS, 1, rq, cw), lambda s: (0, s, 0, 0)), pl.BlockSpec((CHUNKS, 1, dq, width), lambda s: (0, s, 0, 0))],
        out_specs=[pl.BlockSpec((length, width), lambda s: (s, 0))] * 2 + [pl.BlockSpec((rq, width), lambda s: (s, 0))] * 4
        + [pl.BlockSpec((rq, ff), lambda s: (s, 0)), pl.BlockSpec((CHUNKS, 1, dq, width), lambda s: (0, s, 0, 0))],
        compiler_params=pltpu.CompilerParams(vmem_limit_bytes=50 * 2**20),
    )(row_index, tokens, cotangent, new_rows, new_grads, fa.reshape(A_MATS, 4, rq, width), fu.reshape(CHUNKS, 4, rq, cw), fd.reshape(CHUNKS, 4, dq, width))
    vec = lax.dynamic_slice(sums, (0, z * own), (3, own))
    return (out, grad, gq, gk, gv, go, gup, gdown.reshape(w_down.shape), vec[0], vec[1], vec[2])


def solution(mesh):
    depth = mesh.shape["fsdp"]
    both = P(("dp", "fsdp"), None)
    weight, vector = P("fsdp", None), P("fsdp")
    return jax.shard_map(
        functools.partial(body, depth, mesh.shape["dp"] // PLANE),
        mesh=mesh,
        in_specs=(both,) * 3 + (weight,) * 6 + (vector,) * 3 + (both,),
        out_specs=(both, both) + (weight,) * 6 + (vector,) * 3,
        check_vma=False,
    )
```

```python
import functools

import jax
import jax.numpy as jnp
from jax import lax
from jax.experimental import pallas as pl
from jax.experimental.pallas import tpu as pltpu

from jax.sharding import PartitionSpec as P

HEADS = 12
EPS = 1e-06
NEG = -1e30
BF = jnp.bfloat16
F32 = jnp.float32
GATE, R1, R2, LIVE, DLOG, POS = range(6)


def nn(a, b):
    return lax.dot_general(a, b, (((1,), (0,)), ((), ())), preferred_element_type=F32)


def nt(a, b):
    return lax.dot_general(a, b, (((1,), (1,)), ((), ())), preferred_element_type=F32)


def tn(a, b):
    return lax.dot_general(a, b, (((0,), (0,)), ((), ())), preferred_element_type=F32)


def flat(v):
    return v.reshape(-1, v.shape[-1])


class Picker:
    def __init__(self, tokens, cot, picked, up, cols, bufs, sems):
        self.srcs, self.dsts, self.cols, self.bufs, self.sems = (tokens, cot), (picked, up), cols, bufs, sems

    def fetch(self, s, b):
        width = self.srcs[b].shape[-1]
        dst = self.bufs[b].at[:, :, :, :, 0:width]
        return pltpu.make_async_copy(self.srcs[b].at[s], dst, self.sems.at[b])

    def start(self, s):
        for b in range(2):
            self.fetch(s, b).start()

    def turn(self, idx, valid):
        seqs, slots = idx.shape
        for what, k in ((idx, POS), (valid, LIVE)):
            rows8 = what[...].astype(F32)
            if seqs < 8:
                rows8 = jnp.concatenate([rows8, jnp.zeros((8 - seqs, slots), F32)], axis=0)
            turned = rows8.T
            for s in range(seqs):
                self.cols[s * slots : (s + 1) * slots, k : k + 1] = turned[:, s : s + 1]

    def pick(self, s, slots, more):
        width = self.srcs[0].shape[-1]
        rows = slice(s * slots, (s + 1) * slots)
        length = self.bufs[0].shape[0] * self.bufs[0].shape[1] * self.bufs[0].shape[2] * self.bufs[0].shape[3]
        lane = lax.broadcasted_iota(jnp.int32, (slots, length), 1).astype(F32)
        hot = jnp.where(lane == self.cols[rows, POS : POS + 1], 1.0, 0.0).astype(BF)
        for b in range(2):
            self.fetch(s, b).wait()
            self.dsts[b][rows, :] = nn(hot, flat(self.bufs[b][:, :, :, :, 0:width])).astype(BF)
            if more:
                self.fetch(s + 1, b).start()


def norm_phase(picked, gains, cols, na, tile=256):
    total = picked.shape[0]

    @pl.loop(0, total // tile)
    def _(i):
        rows = pl.ds(pl.multiple_of(i * tile, tile), tile)
        x = picked[rows, :].astype(F32)
        cols[rows, GATE : GATE + 1] = jax.nn.sigmoid(
            jnp.sum(x * gains[2:3, :], axis=1, keepdims=True)
        )
        r1 = lax.rsqrt(jnp.mean(x * x, axis=1, keepdims=True) + EPS)
        cols[rows, R1 : R1 + 1] = r1
        na[rows, :] = (x * r1 * gains[0:1, :]).astype(BF)


def norm_again(picked, gains, cols, na, tile=256):
    @pl.loop(0, picked.shape[0] // tile)
    def _(i):
        rows = pl.ds(pl.multiple_of(i * tile, tile), tile)
        x = picked[rows, :].astype(F32)
        na[rows, :] = (x * cols[rows, R1 : R1 + 1] * gains[0:1, :]).astype(BF)


def qkv_one(na, wa, qkv, scale, m):
    @pl.loop(0, na.shape[1] // 256)
    def _(n):
        at = pl.ds(pl.multiple_of(n * 256, 256), 256)
        out = nn(na[...], flat(wa[m, :, :, :, :, at]))
        if m == 0:
            out = out * scale
        qkv[m, :, at] = out.astype(BF)


def two_heads(v2, low_half):
    zero = jnp.zeros_like(v2)
    return jnp.concatenate([jnp.where(low_half, v2, zero), jnp.where(low_half, zero, v2)], axis=0)


def prob_spot(s, p, slots):
    at = pl.ds(pl.multiple_of(s * slots, slots), slots)
    return (p // 2, slice(2 * (p % 2), 2 * (p % 2) + 2), slice(None), slice(None), slice(None), at)


def attention_forward(idx, valid, cols, qkv, probs, mixed, s):
    slots = idx.shape[1]
    width = mixed.shape[1]
    rows = pl.ds(pl.multiple_of(s * slots, slots), slots)
    low_half = lax.broadcasted_iota(jnp.int32, (slots, 128), 1) < 64
    mine = cols[rows, POS : POS + 1]
    other = idx[pl.ds(s, 1), :].astype(F32)
    seen = ((other < mine) & (valid[pl.ds(s, 1), :] > 0)) | (other == mine)
    bias = jnp.where(seen, 0.0, NEG)
    bias = jnp.concatenate([bias, bias], axis=0)
    for p in range(width // 128):
        at = slice(p * 128, p * 128 + 128)
        q2 = two_heads(qkv[0, rows, at], low_half)
        scores = nt(q2, qkv[1, rows, at]) + bias
        e = jnp.exp(scores - jnp.max(scores, axis=1, keepdims=True))
        pr = (e * (1.0 / jnp.sum(e, axis=1, keepdims=True))).astype(BF)
        spot = prob_spot(s, p, slots)
        probs[spot] = pr.reshape(2, 2, 2, 64, slots)
        o = nn(pr, qkv[2, rows, at])
        mixed[rows, at] = jnp.where(low_half, o[:slots], o[slots:]).astype(BF)


def attention_backward(qkv, probs, mixed, dmix, s, slots, scale):
    width = mixed.shape[1]
    rows = pl.ds(pl.multiple_of(s * slots, slots), slots)
    low_half = lax.broadcasted_iota(jnp.int32, (slots, 128), 1) < 64
    for p in range(width // 128):
        at = slice(p * 128, p * 128 + 128)
        do2 = two_heads(dmix[rows, at], low_half)
        o2 = mixed[rows, at].astype(F32)
        o2 = jnp.concatenate([o2, o2], axis=0)
        delta = jnp.sum(do2.astype(F32) * o2, axis=1, keepdims=True)
        k2 = qkv[1, rows, at]
        dp = nt(do2, qkv[2, rows, at])
        pr = flat(probs[prob_spot(s, p, slots)])
        ds = (pr.astype(F32) * (dp - delta)).astype(BF)
        q2 = two_heads(qkv[0, rows, at], low_half)
        dq = nn(ds, k2) * scale
        qkv[0, rows, at] = jnp.where(low_half, dq[:slots], dq[slots:]).astype(BF)
        qkv[1, rows, at] = tn(ds, q2).astype(BF)
        qkv[2, rows, at] = tn(pr, do2).astype(BF)


def out_phase(mixed, wa, attn_out):
    width = mixed.shape[1]

    @pl.loop(0, width // 256)
    def _(n):
        at = pl.ds(pl.multiple_of(n * 256, 256), 256)
        attn_out[:, at] = nn(mixed[...], flat(wa[3, :, :, :, :, at]))


def mid_norm(picked, attn_out, up, gains, cols, nm, nmt, dd, tile=256):
    total = picked.shape[0]
    for i in range(total // tile):
        rows = slice(i * tile, (i + 1) * tile)
        hidden = picked[rows, :].astype(F32) + cols[rows, GATE : GATE + 1] * attn_out[rows, :]
        r2 = lax.rsqrt(jnp.mean(hidden * hidden, axis=1, keepdims=True) + EPS)
        cols[rows, R2 : R2 + 1] = r2
        normed = (hidden * r2 * gains[1:2, :]).astype(BF)
        nm[rows, :] = normed
        nmt[:, rows] = normed.T
        dd[rows, :] = (up[rows, :].astype(F32) * cols[rows, LIVE : LIVE + 1]).astype(BF)


def gelu_both(u):
    k = 0.7978845608028654
    u2 = u * u
    t = jnp.tanh(u * (k + (k * 0.044715) * u2))
    half = 0.5 + 0.5 * t
    act = u * half
    slope = half + act * (1.0 - t) * (k + (3 * k * 0.044715) * u2)
    return act, slope


def mlp_up(nm, dd, wu, wd, act, dup, c, n):
    at = pl.ds(pl.multiple_of(n * 256, 256), 256)
    u = nn(nm[...], flat(wu[c, :, :, :, :, at]))
    dact = nt(dd[...], flat(wd[c, n]))
    a, slope = gelu_both(u)
    shape = act.shape[:4] + (256,)
    act[:, :, :, :, at] = a.astype(BF).reshape(shape)
    dup[:, :, :, :, at] = (slope * dact).astype(BF).reshape(shape)


def mlp_down(act, wd, down, c):
    @pl.loop(0, down.shape[1] // 256)
    def _(n):
        at = pl.ds(pl.multiple_of(n * 256, 256), 256)
        out = nn(flat(act[...]), flat(wd[c, :, :, :, :, at]))
        down[:, at] = out if c == 0 else down[:, at] + out


def mlp_dnormed(dup, wu, dnm, c):
    @pl.loop(0, 2)
    def _(i):
        half = dnm.shape[0] // 2
        rows = pl.ds(pl.multiple_of(i * half, half), half)
        out = nt(flat(dup[pl.ds(2 * i, 2)]), flat(wu[c]))
        dnm[rows, :] = out if c == 0 else dnm[rows, :] + out


def mlp_grad_down(act, dd, wd, c):
    @pl.loop(0, act.shape[-1] // 256)
    def _(n):
        at = pl.ds(pl.multiple_of(n * 256, 256), 256)
        g = tn(flat(act[:, :, :, :, at]), dd[...]).astype(BF)
        wd[c, n] = g.reshape(wd.shape[2:])


def mlp_grad_up(nmt, dup, wu, c):
    @pl.loop(0, dup.shape[-1] // 256)
    def _(n):
        at = pl.ds(pl.multiple_of(n * 256, 256), 256)
        g = nn(nmt[...], flat(dup[:, :, :, :, at])).astype(BF)
        wu[c, :, :, :, :, at] = g.reshape(wu.shape[1:5] + (256,))


def mid_backward(picked, attn_out, up, down, dnm, gains, cols, datt, new_rows, small, tile=128):
    total = picked.shape[0]
    small[...] = jnp.zeros_like(small)

    @pl.loop(0, total // tile)
    def _(i):
        rows = pl.ds(pl.multiple_of(i * tile, tile), tile)
        x = picked[rows, :].astype(F32)
        gate = cols[rows, GATE : GATE + 1]
        live = cols[rows, LIVE : LIVE + 1]
        r = cols[rows, R2 : R2 + 1]
        ao = attn_out[rows, :]
        branch = gate * ao
        hidden = x + branch
        new_rows[rows, :] = (x + live * (branch + down[rows, :])).astype(BF)
        d = dnm[rows, :]
        hr = hidden * r
        dh = d * hr
        small[1:2, :] += jnp.sum(dh, axis=0, keepdims=True)
        mean = jnp.mean(dh * gains[1:2, :], axis=1, keepdims=True)
        d_hidden = r * (gains[1:2, :] * d - hr * mean)
        dnm[rows, :] = d_hidden
        d_branch = live * up[rows, :].astype(F32) + d_hidden
        d_logit = jnp.sum(d_branch * ao, axis=1, keepdims=True) * gate * (1.0 - gate)
        cols[rows, DLOG : DLOG + 1] = d_logit
        small[2:3, :] += jnp.sum(x * d_logit, axis=0, keepdims=True)
        datt[rows, :] = (d_branch * gate).astype(BF)


def out_backward(datt, mixed, wa, dmix):
    total, width = datt.shape

    @pl.loop(0, 2)
    def _(i):
        half = total // 2
        rows = pl.ds(pl.multiple_of(i * half, half), half)
        dmix[rows, :] = nt(datt[rows, :], flat(wa[3])).astype(BF)

    wa[3] = grad_of(mixed, datt[...]).reshape(wa.shape[1:])


def grad_of(left, right):
    parts = [tn(left[:, n * 384 : n * 384 + 384], right).astype(BF) for n in range(2)]
    return jnp.concatenate(parts, axis=0)


def qkv_normed(dqkv, wa, dnorm):
    total = dqkv.shape[1]

    @pl.loop(0, 4)
    def _(i):
        part = total // 4
        rows = pl.ds(pl.multiple_of(i * part, part), part)
        dnorm[rows, :] = (
            nt(dqkv[0, rows, :], flat(wa[0]))
            + nt(dqkv[1, rows, :], flat(wa[1]))
            + nt(dqkv[2, rows, :], flat(wa[2]))
        )


def first_backward(picked, up, dnorm, dhid, gains, cols, new_grads, small, tile=128):
    total = picked.shape[0]

    @pl.loop(0, total // tile)
    def _(i):
        rows = pl.ds(pl.multiple_of(i * tile, tile), tile)
        x = picked[rows, :].astype(F32)
        r = cols[rows, R1 : R1 + 1]
        d = dnorm[rows, :]
        xr = x * r
        dx = d * xr
        small[0:1, :] += jnp.sum(dx, axis=0, keepdims=True)
        mean = jnp.mean(dx * gains[0:1, :], axis=1, keepdims=True)
        d_first = r * (gains[0:1, :] * d - xr * mean)
        d_picked = d_first + dhid[rows, :] + cols[rows, DLOG : DLOG + 1] * gains[2:3, :]
        new_grads[rows, :] = (up[rows, :].astype(F32) + d_picked).astype(BF)


MESH_ID = pl.DeviceIdType.MESH
A_MATS, CHUNKS, PLANE = 4, 3, 8


class Place:
    def __init__(self, depth):
        dp = lax.axis_index("dp")
        self.depth = depth
        self.z = lax.axis_index("fsdp")
        self.core = lax.rem(dp, 2)
        self.x = lax.rem(lax.div(dp, 2), 2)
        self.y = lax.rem(lax.div(dp, 4), 2)
        self.sib = (dp + 1 - 2 * self.core, self.z)
        self.xn = (dp + 2 - 4 * self.x, self.z)
        self.yn = (dp + 4 - 8 * self.y, self.z)
        self.dp = dp

    def ahead(self, o):
        return lax.rem(self.z + o, self.depth)

    def behind(self, o):
        return lax.rem(self.z + self.depth - o, self.depth)

    def at_z(self, z):
        return (self.dp, z)

    def greet(self):
        barrier = pltpu.get_barrier_semaphore()
        peers = [self.sib, self.xn, self.yn]
        peers += [self.at_z(self.ahead(o)) for o in range(1, self.depth)]
        for peer in peers:
            pl.semaphore_signal(barrier, inc=1, device_id=peer, device_id_type=MESH_ID)
        pl.semaphore_wait(barrier, len(peers))


def half_of(ref, core):
    width = ref.shape[-1] // 2
    return pl.ds(pl.multiple_of(core * width, 128), width)


class Gather:
    SENDS, RECVS = 2, 5
    CORE, Z, X, Y, FAR = range(5)
    ARRAYS = A_MATS + 2 * CHUNKS

    def __init__(self, me, wa, wu, wd, sends, recvs):
        self.me, self.refs, self.sends, self.recvs = me, (wa, wu, wd), sends, recvs

    def array(self, a):
        wa, wu, wd = self.refs
        if a < A_MATS:
            return wa.at[a]
        return (wd if a % 2 else wu).at[(a - A_MATS) // 2]

    def piece(self, a, zi, xi, yi, core):
        ref = self.array(a)
        return ref.at[zi, xi, yi, :, half_of(ref, core)]

    def way(self, a):
        return a % 2

    def copy(self, a, kind, ref, dev):
        send = self.sends.at[a * self.SENDS + (0 if kind == self.CORE else 1)]
        recv = self.recvs.at[a * self.RECVS + kind]
        return pltpu.make_async_remote_copy(
            src_ref=ref, dst_ref=ref, send_sem=send, recv_sem=recv, device_id=dev, device_id_type=MESH_ID
        )

    def mine(self, a, zi, flip_x=False, flip_y=False):
        m = self.me
        return self.piece(a, zi, 1 - m.x if flip_x else m.x, 1 - m.y if flip_y else m.y, m.core)

    def took(self, a, kind):
        self.copy(a, kind, self.mine(a, slice(0, self.me.depth - 1)), self.me.xn).wait_recv()

    def core_copy(self, a, core):
        ref = self.array(a)
        return self.copy(a, self.CORE, ref.at[:, :, :, :, half_of(ref, core)], self.me.sib)

    def origins(self):
        return range(1, self.me.depth)

    def send_z(self, a):
        m = self.me
        for o in self.origins():
            self.copy(a, self.Z, self.mine(a, m.z), m.at_z(m.ahead(o))).start()

    def spread(self, a):
        m = self.me
        self.took(a, self.Z)
        for o in self.origins():
            self.copy(a, self.X, self.mine(a, m.behind(o)), m.xn).start()
            self.copy(a, self.Y, self.mine(a, m.behind(o)), m.yn).start()

    def forward(self, a):
        m, by_x = self.me, self.way(a) == 0
        self.took(a, self.X if by_x else self.Y)
        for o in self.origins():
            ref = self.mine(a, m.behind(o), by_x, not by_x)
            self.copy(a, self.FAR, ref, m.yn if by_x else m.xn).start()

    def across(self, a):
        self.took(a, self.Y if self.way(a) == 0 else self.X)
        self.took(a, self.FAR)
        self.core_copy(a, self.me.core).start()

    def ready(self, a):
        self.core_copy(a, 1 - self.me.core).wait_recv()

    def settle(self, a):
        m, ref = self.me, self.array(a)
        self.core_copy(a, m.core).wait_send()
        sent = ref.at[0 : m.depth - 1, :, :, :, half_of(ref, m.core)]
        self.copy(a, self.Z, sent, m.xn).wait_send()

    def slot(self, t, ahead=2):
        if t < self.ARRAYS:
            self.spread(t)
        if ahead <= t + ahead < self.ARRAYS:
            self.send_z(t + ahead)
        if 0 <= t - 1 < self.ARRAYS:
            self.forward(t - 1)
        if 0 <= t - 2 < self.ARRAYS:
            self.across(t - 2)


class Owned:
    def __init__(self, me, shards, wa, wu, wd, sems):
        wq, wk, wv, wo, up, down = shards
        z, core = me.z, me.core
        half = half_of(wa, core)
        self.copies = {a: [] for a in range(Gather.ARRAYS)}
        for m, w in enumerate((wq, wk, wv, wo)):
            self.copies[m].append((w.at[:, :, :, half], wa.at[m, z, :, :, :, half]))
        ff_own = up.shape[-1] // me.depth
        for c in range(CHUNKS):
            for j in range(2):
                block = 2 * core + j
                src = up.at[:, :, :, pl.ds(pl.multiple_of(block * ff_own + c * 256, 128), 256)]
                dst = wu.at[c, z, :, :, :, pl.ds(pl.multiple_of(block * 256, 128), 256)]
                self.copies[A_MATS + 2 * c].append((src, dst))
            self.copies[A_MATS + 1 + 2 * c].append((down.at[c, :, :, :, half], wd.at[c, z, :, :, :, half]))
        self.sems = sems

    def all_of(self, a):
        for i, (src, dst) in enumerate(self.copies[a]):
            yield pltpu.make_async_copy(src, dst, self.sems.at[2 * a + i])

    def start(self, a):
        for c in self.all_of(a):
            c.start()

    def wait(self, a):
        for c in self.all_of(a):
            c.wait()


class Reduce:
    SENDS, RECVS = 2, 7
    CORE, FIRST, SECOND, Z, BACK, FAR, LAST = range(7)

    def __init__(
        self, me, w, from_core, from_x, from_y, then_x, then_y, from_z, sends, recvs, frees, at, way
    ):
        self.me, self.w, self.way, self.free, base = me, w, way, frees.at[at], at
        self.from_core, self.from_x, self.from_y = from_core, from_x, from_y
        self.then_x, self.then_y, self.from_z = then_x, then_y, from_z
        self.sends, self.recvs, self.base = sends, recvs, base
        self.mine, self.theirs = half_of(w, me.core), half_of(w, 1 - me.core)

    def copy(self, kind, src, dst, dev):
        small = kind in (self.Z, self.BACK, self.FAR)
        send = self.sends.at[self.base * self.SENDS + small]
        recv = self.recvs.at[self.base * self.RECVS + kind]
        return pltpu.make_async_remote_copy(
            src_ref=src, dst_ref=dst, send_sem=send, recv_sem=recv, device_id=dev, device_id_type=MESH_ID
        )

    def took(self, kind, ref):
        self.copy(kind, ref, ref, self.me.sib).wait_recv()

    def sent(self, kind, ref):
        self.copy(kind, ref, ref, self.me.sib).wait_send()

    def z_copy(self, o):
        m = self.me
        src = self.w.at[m.ahead(o), m.x, m.y, :, self.mine]
        return self.copy(self.Z, src, self.from_z.at[o - 1], m.at_z(m.ahead(o)))

    def back(self, kind, xi, yi, dev):
        ref = self.from_core.at[0, xi, yi]
        return self.copy(kind, ref, ref, dev)

    def add(self, at, arrived):
        self.w[at] = (self.w[at].astype(F32) + arrived.astype(F32)).astype(BF)

    def t1(self):
        self.copy(self.CORE, self.w.at[:, :, :, :, self.theirs], self.from_core, self.me.sib).start()

    def t2(self):
        m, w = self.me, self.w
        self.took(self.CORE, self.from_core)

        @pl.loop(0, 2 * m.depth)
        def _(i):
            zi, xi = lax.div(i, 2), lax.rem(i, 2)
            self.add((zi, xi, slice(None), slice(None), self.mine), self.from_core[zi, xi])

        pl.semaphore_signal(self.free, inc=1, device_id=m.sib, device_id_type=MESH_ID)
        self.copy(self.FIRST, w.at[0:2, 1 - m.x, :, :, self.mine], self.from_x, m.xn).start()
        self.copy(self.FIRST, w.at[2:4, :, 1 - m.y, :, self.mine], self.from_y, m.yn).start()

    def t3(self):
        m, w = self.me, self.w
        self.took(self.FIRST, w.at[0:2, :, :, :, self.mine])

        @pl.loop(0, 2)
        def _(zi):
            self.add((zi, m.x, slice(None), slice(None), self.mine), self.from_x[zi])
            self.add((2 + zi, slice(None), m.y, slice(None), self.mine), self.from_y[zi])

        self.copy(self.SECOND, w.at[0:2, m.x, 1 - m.y, :, self.mine], self.then_y, m.yn).start()
        self.copy(self.SECOND, w.at[2:4, 1 - m.x, m.y, :, self.mine], self.then_x, m.xn).start()

    def t4(self):
        m = self.me
        self.took(self.SECOND, self.w.at[0:2, 0:2, 0, :, self.mine])
        self.add((slice(0, 2), m.x, m.y, slice(None), self.mine), self.then_y[...])
        self.add((slice(2, 4), m.x, m.y, slice(None), self.mine), self.then_x[...])
        for o in range(1, m.depth):
            self.z_copy(o).start()

    def t5(self):
        m = self.me
        total = self.w[m.z, m.x, m.y, :, self.mine].astype(F32)
        self.took(self.Z, self.from_z)
        for o in range(1, m.depth):
            total = total + self.from_z[o - 1].astype(F32)
        self.from_core[0, m.x, m.y] = total.astype(BF)
        self.back(self.BACK, m.x, m.y, m.xn).start()
        self.back(self.BACK, m.x, m.y, m.yn).start()

    def t6(self):
        m = self.me
        self.took(self.BACK, self.from_core.at[0, 0:2, 0])
        if self.way == 0:
            self.back(self.FAR, 1 - m.x, m.y, m.yn).start()
        else:
            self.back(self.FAR, m.x, 1 - m.y, m.xn).start()

    def t7(self):
        m = self.me
        self.took(self.FAR, self.from_core.at[0, 0, 0])
        pl.semaphore_wait(self.free, 1)
        self.copy(self.LAST, self.from_core.at[0], self.from_core.at[1], m.sib).start()

    def t8(self):
        m = self.me
        self.took(self.LAST, self.from_core.at[1])
        self.sent(self.CORE, self.w)
        self.sent(self.Z, self.w.at[0 : m.depth - 1, 0:2, 0, :, self.mine])


class SmallSum:
    def __init__(self, me, small, inbox, sends, recvs, base):
        self.me, self.small, self.inbox = me, small, inbox
        self.sends, self.recvs, self.base = sends, recvs, base

    def copy(self, k, src, dst, dev):
        return pltpu.make_async_remote_copy(
            src_ref=src, dst_ref=dst, send_sem=self.sends.at[self.base[0]], recv_sem=self.recvs.at[self.base[1] + k],
            device_id=dev, device_id_type=MESH_ID,
        )

    def peer(self, k):
        return (self.me.sib, self.me.xn, self.me.yn)[k]

    def step(self, k):
        m, small, inbox = self.me, self.small, self.inbox
        if 1 <= k <= 3:
            self.copy(k - 1, small.at[0], inbox.at[k - 1], m.sib).wait_recv()
            small[k] = small[k - 1] + inbox[k - 1]
        if k <= 2:
            self.copy(k, small.at[k], inbox.at[k], self.peer(k)).start()
        if k == 3:
            for o in range(1, m.depth):
                self.copy(3, small.at[3], inbox.at[2 + o], m.at_z(m.ahead(o))).start()
        if k == 4:
            self.copy(3, inbox.at[3:], inbox.at[3:], m.sib).wait_recv()
            total = small[3]
            for o in range(1, m.depth):
                total = total + inbox[2 + o]
            small[4] = total
            self.copy(3, inbox, inbox, m.sib).wait_send()


def chunk_boxes(rows_a, width, rows_d, ff_c):
    def boxes(n, rows, cols, first):
        def box(*lead):
            return pltpu.VMEM((n,) + lead + (rows, cols), BF)

        return ([box(4, 2, 2)] if first else []) + [box(2, 2), box(2, 2), box(2), box(2), box(3)]

    return (
        boxes(CHUNKS, rows_a, ff_c // 2, True)
        + boxes(CHUNKS, rows_d, width // 2, True)
        + boxes(A_MATS, rows_a, width // 2, False)
    )


def block_kernel(
    depth, tokens, cot, idx, valid, wq, wk, wv, wo, up_in, down_in, gain1, gain2, gain3,
    new_rows, new_grads, fa, fu, fd, small_out,
    wa, wu, wd, picked, up, cols, na, nmt, dd, qkv, probs, mixed, attn_out, act, dup, down, dnm,
    gains, gpad, gbox, small, inbox,
    tok_sem, own_sem, out_sem, ag_send, ag_recv, rs_send, rs_recv, frees, opened, *boxes,
):
    seqs, slots = idx.shape
    width = picked.shape[1]
    scale = (width // HEADS) ** -0.5
    rows_a = wa.shape[-2]
    half = width // 2
    me = Place(depth)
    me.greet()
    own = Owned(me, (wq, wk, wv, wo, up_in, down_in), wa, wu, wd, own_sem)
    ag = Gather(me, wa, wu, wd, ag_send, ag_recv)
    sem_at = (20, 70)
    others = range(1, depth)

    def gain_copy(o):
        return pltpu.make_async_remote_copy(
            src_ref=gpad, dst_ref=gbox.at[o - 1], send_sem=rs_send.at[21], recv_sem=rs_recv.at[74],
            device_id=me.at_z(me.ahead(o)), device_id_type=MESH_ID,
        )

    own.start(0)
    own.start(1)
    picker = Picker(tokens, cot, picked, up, cols, (act, dup), tok_sem)
    picker.start(0)
    for a in range(2, Gather.ARRAYS):
        own.start(a)
    own.wait(0)
    ag.send_z(0)
    own.wait(1)
    ag.send_z(1)
    owned = gain1.shape[0]
    spot = lax.broadcasted_iota(jnp.int32, (owned, width), 1) - lax.broadcasted_iota(jnp.int32, (owned, width), 0)
    spot = jnp.where(spot == me.z * owned, 1.0, 0.0).astype(BF)
    gpad[...] = jnp.zeros_like(gpad)
    for i, g in enumerate((gain1, gain2, gain3)):
        gpad[i : i + 1, :] = nn(g[...].astype(F32).reshape(1, owned).astype(BF), spot)
    for o in others:
        gain_copy(o).start()
    picker.turn(idx, valid)
    picker.pick(0, slots, True)
    for a in range(2, Gather.ARRAYS):
        own.wait(a)
    ag.slot(0)
    picker.pick(1, slots, True)
    ag.slot(1)
    picker.pick(2, slots, True)
    ag.slot(2)
    picker.pick(3, slots, False)
    ag.slot(3)
    pltpu.make_async_remote_copy(
        src_ref=gbox, dst_ref=gbox, send_sem=rs_send.at[21], recv_sem=rs_recv.at[74],
        device_id=me.sib, device_id_type=MESH_ID,
    ).wait()
    total = gpad[...]
    for o in others:
        total = total + gbox[o - 1]
    gains[...] = total
    norm_phase(picked, gains, cols, na)
    ag.slot(4)
    for m in range(3):
        ag.ready(m)
        qkv_one(na, wa, qkv, scale, m)
        ag.slot(5 + m)

    @pl.loop(0, seqs)
    def _(s):
        attention_forward(idx, valid, cols, qkv, probs, mixed, s)
        for k in range(4):

            @pl.when(s == k)
            def _():
                ag.slot(8 + k)

    ag.ready(3)
    out_phase(mixed, wa, attn_out)
    mid_norm(picked, attn_out, up, gains, cols, na, nmt, dd)

    ubox, dbox, abox = boxes[0:6], boxes[6:12], boxes[12:17]
    reducers = {}

    def reducer(name, at, w, core_box, rest, i, way):
        reducers[name] = Reduce(me, w, core_box, *[x.at[i] for x in rest], rs_send, rs_recv, frees, at, way)

    for c in range(CHUNKS):
        reducer("u%d" % c, c, wu.at[c], ubox[0].at[c], ubox[1:], c, 0)
        reducer("d%d" % c, 3 + c, wd.at[c], dbox[0].at[c], dbox[1:], c, 1)
    spots = ((act, 0), (act, half), (dup, 0), (dup, half))
    terms = [probs.at[m, :, :, :, 0:rows_a, 0:width] for m in range(3)] + [wa.at[3]]
    for m, name in enumerate("qkvo"):
        ref, lane = spots[m]
        box = ref.at[:, :, :, 0:rows_a, lane : lane + half]
        reducer(name, 6 + m, terms[m], box, abox, m, m % 2)
    finals = {"q": (fa, 0), "k": (fa, 1), "v": (fa, 2), "o": (fa, 3)}
    for c in range(CHUNKS):
        finals["u%d" % c] = (fu, c)
        finals["d%d" % c] = (fd, c)
    order = list(finals)

    def result_copies(name):
        dst, i = finals[name]
        box = reducers[name].from_core
        for h, core in ((0, me.core), (1, 1 - me.core)):
            yield pltpu.make_async_copy(box.at[h], dst.at[i, :, :, :, half_of(dst, core)], out_sem.at[{"u": 1, "d": 2}.get(name[0], 0)])

    def step(k, *names):
        for name in names:
            getattr(reducers[name], "t%d" % k)()
            if k == 8:
                for c in result_copies(name):
                    c.start()

    for c in range(CHUNKS):
        for a in (A_MATS + 2 * c, A_MATS + 1 + 2 * c):
            ag.ready(a)

        @pl.loop(0, 4)
        def _(n):
            mlp_up(na, dd, wu, wd, act, dup, c, n)
            if c > 0:

                @pl.when(n == 1)
                def _():
                    step(2, "d%d" % (c - 1), "u%d" % (c - 1))

        mlp_down(act, wd, down, c)
        mlp_dnormed(dup, wu, dnm, c)
        if c == 2:
            step(4, "d0", "u0")
        ag.settle(A_MATS + 2 * c)
        ag.settle(A_MATS + 1 + 2 * c)
        mlp_grad_down(act, dd, wd, c)
        step(1, "d%d" % c)
        mlp_grad_up(nmt, dup, wu, c)
        step(1, "u%d" % c)
        if c > 0:
            step(3, "d%d" % (c - 1), "u%d" % (c - 1))
    pl.semaphore_signal(opened, inc=1, device_id=me.sib, device_id_type=MESH_ID)
    for a in range(A_MATS):
        ag.settle(a)
    datt, dmix = na, dd
    mid_backward(picked, attn_out, up, down, dnm, gains, cols, datt, dd, small.at[0])
    rows_out = pltpu.make_async_copy(dd, new_rows, tok_sem.at[0])
    rows_out.start()
    step(2, "d2", "u2")
    rows_out.wait()
    out_backward(datt, mixed, wa, dmix)
    pl.semaphore_wait(opened, 1)
    step(1, "o")
    step(4, "d1", "u1")
    step(5, "d0", "u0")
    norm_again(picked, gains, cols, na)

    @pl.loop(0, seqs)
    def _(s):
        attention_backward(qkv, probs, mixed, dmix, s, slots, scale)

        @pl.when(s == 0)
        def _():
            step(2, "o")
            step(6, "d0", "u0")

        @pl.when(s == 1)
        def _():
            step(7, "d0", "u0")

        @pl.when(s == 2)
        def _():
            step(3, "d2", "u2")
            step(8, "d0", "u0")

        @pl.when(s == 3)
        def _():
            step(3, "o")

    for m, name in enumerate("qkv"):
        terms[m][...] = grad_of(na, qkv[m]).reshape(wa.shape[1:])
        step(1, name)
        if m == 0:
            step(5, "d1", "u1")
        if m > 0:
            step(2, "qkv"[m - 1])
    step(4, "d2", "u2", "o")
    qkv_normed(qkv, wa, down)
    step(2, "v")
    step(3, "q")
    step(6, "d1", "u1")
    first_backward(picked, up, down, dnm, gains, cols, dd, small.at[0])
    grads_out = pltpu.make_async_copy(dd, new_grads, tok_sem.at[1])
    grads_out.start()
    sums = SmallSum(me, small, inbox, rs_send, rs_recv, sem_at)
    sums.step(0)
    step(3, "k")
    step(4, "q")
    step(7, "d1", "u1")
    sums.step(1)
    step(5, "d2", "u2", "o")
    step(3, "v")
    step(4, "k")
    sums.step(2)
    step(6, "d2", "u2", "o")
    step(4, "v")
    step(8, "d1", "u1")
    sums.step(3)
    step(5, "q")
    step(7, "d2", "u2", "o")
    step(5, "k")
    step(6, "q")
    sums.step(4)
    step(5, "v")
    step(6, "k")
    step(7, "q")
    step(8, "d2", "u2", "o")
    step(6, "v")
    step(7, "k", "v")
    step(8, *"qkv")
    small_out[...] = small[4]
    for i, dst in enumerate((fa, fu, fd)):
        pltpu.make_async_copy(dst, dst, out_sem.at[i]).wait()
    grads_out.wait()


def place_kernel(idx, tokens, cot, new_rows, new_grads, fa, fu, fd,
                 out, grad, gq, gk, gv, go, gup, gdown):
    s = pl.program_id(0)
    length, slots = tokens.shape[0], idx.shape[1]
    spot = lax.broadcasted_iota(jnp.int32, (length, slots), 0)
    hot = jnp.where(spot == idx[pl.ds(s, 1), :], 1.0, 0.0)
    hit = jnp.sum(hot, axis=1, keepdims=True) > 0
    hot = hot.astype(BF)
    for src, rows, dst in ((tokens, new_rows, out), (cot, new_grads, grad)):
        dst[...] = jnp.where(hit, nn(hot, rows[...]), src[...].astype(F32)).astype(BF)
    for m, g in enumerate((gq, gk, gv, go)):
        g[...] = fa[m, 0].astype(F32)
    quarter = 256
    ff_own = gup.shape[1] // 4
    for c in range(CHUNKS):
        for j in range(4):
            gup[:, j * ff_own + c * quarter : j * ff_own + (c + 1) * quarter] = fu[c, 0, :, j * quarter : (j + 1) * quarter].astype(F32)
        gdown[c, 0] = fd[c, 0].astype(F32)


def remote_params(collective_id, limit=60):
    return pltpu.CompilerParams(
        collective_id=collective_id, has_side_effects=True, vmem_limit_bytes=limit * 2**20
    )


def over_groups(groups, terms):
    if groups == 1:
        return terms
    dp = groups * PLANE
    total = [t.astype(F32) for t in terms]
    for k in range(groups.bit_length() - 1):
        hop = PLANE << k
        pairs = [(i, i ^ hop) for i in range(dp)]
        total = [t + lax.ppermute(t, "dp", pairs) for t in total]
    return total


def body(depth, groups, tokens, row_index, row_valid, w_query, w_key, w_value, w_out, w_up, w_down,
         gain_attn, gain_mlp, w_router, cotangent):
    seqs, slots = row_index.shape
    width = tokens.shape[1]
    own = w_query.shape[0]
    ff = w_up.shape[1]
    length = tokens.shape[0] // seqs
    total = seqs * slots
    rq, cw = own // 4, ff // CHUNKS
    dq = w_down.shape[0] // (4 * CHUNKS)
    sd = jax.ShapeDtypeStruct
    hbm, vm = pl.BlockSpec(memory_space=pl.ANY), pl.BlockSpec(memory_space=pltpu.VMEM)
    sem = pltpu.SemaphoreType.DMA
    vmem = pltpu.VMEM
    z = lax.axis_index("fsdp")
    gains3 = (gain_attn, gain_mlp, w_router)
    squares = [w.reshape(2, 2, rq, width) for w in (w_query, w_key, w_value, w_out)]
    sa, su, sdn = (A_MATS, depth, 2, 2, rq, width), (CHUNKS, depth, 2, 2, rq, cw), (CHUNKS, depth, 2, 2, dq, width)
    narr = Gather.ARRAYS
    rows = (total, width)
    work = (4, 2, 2, total // 16, cw)
    regular = pltpu.SemaphoreType.REGULAR
    blocks = (seqs, 4, 2, 2, length // 16, width)
    new_rows, new_grads, fa, fu, fd, sums = pl.pallas_call(
        functools.partial(block_kernel, depth),
        out_shape=(
            sd(rows, BF), sd(rows, BF), sd(sa[:1] + sa[2:], BF), sd(su[:1] + su[2:], BF), sd(sdn[:1] + sdn[2:], BF),
            sd((8, width), F32),
        ),
        in_specs=[hbm, hbm, vm, vm] + [hbm] * 6 + [vm] * 3,
        out_specs=(hbm,) * 5 + (vm,),
        scratch_shapes=[
            vmem(sa, BF), vmem(su, BF), vmem(sdn, BF), vmem(rows, BF), vmem(rows, BF), vmem((total, 128), F32),
            vmem(rows, BF), vmem((width, total), BF), vmem(rows, BF), vmem((3,) + rows, BF), vmem((3,) + work, BF),
            vmem(rows, BF), vmem(rows, F32), vmem(work, BF), vmem(work, BF), vmem(rows, F32), vmem(rows, F32),
            vmem((8, width), F32), vmem((8, width), F32), vmem((depth - 1, 8, width), F32), vmem((5, 8, width), F32), vmem((2 + depth, 8, width), F32),
            sem((2,)), sem((2 * narr,)), sem((3,)), sem((2 * narr,)), sem((5 * narr,)),
            sem((2 * narr + 2,)), sem((7 * narr + 5,)), regular((narr,)), regular,
        ]
        + chunk_boxes(rq, width, dq, cw),
        compiler_params=remote_params(0, 63),
    )(
        tokens.reshape(blocks), cotangent.reshape(blocks), row_index, row_valid, *squares,
        w_up.reshape(2, 2, rq, ff), w_down.reshape(CHUNKS, 2, 2, dq, width), *gains3,
    )
    fa, fu, fd, sums = over_groups(groups, (fa, fu, fd, sums))
    out, grad, gq, gk, gv, go, gup, gdown = pl.pallas_call(
        place_kernel,
        grid=(seqs,),
        out_shape=(sd(tokens.shape, BF), sd(tokens.shape, BF)) + (sd((own, width), F32),) * 4 + (sd((own, ff), F32), sd((CHUNKS, 4, dq, width), F32)),
        in_specs=[pl.BlockSpec((seqs, slots), lambda s: (0, 0))] + [pl.BlockSpec((length, width), lambda s: (s, 0))] * 2
        + [pl.BlockSpec((slots, width), lambda s: (s, 0))] * 2
        + [pl.BlockSpec((A_MATS, 1, rq, width), lambda s: (0, s, 0, 0)), pl.BlockSpec((CHUNKS, 1, rq, cw), lambda s: (0, s, 0, 0)), pl.BlockSpec((CHUNKS, 1, dq, width), lambda s: (0, s, 0, 0))],
        out_specs=[pl.BlockSpec((length, width), lambda s: (s, 0))] * 2 + [pl.BlockSpec((rq, width), lambda s: (s, 0))] * 4
        + [pl.BlockSpec((rq, ff), lambda s: (s, 0)), pl.BlockSpec((CHUNKS, 1, dq, width), lambda s: (0, s, 0, 0))],
        compiler_params=pltpu.CompilerParams(vmem_limit_bytes=62 * 2**20),
    )(row_index, tokens, cotangent, new_rows, new_grads, fa.reshape(A_MATS, 4, rq, width), fu.reshape(CHUNKS, 4, rq, cw), fd.reshape(CHUNKS, 4, dq, width))
    vec = lax.dynamic_slice(sums, (0, z * own), (3, own))
    return (out, grad, gq, gk, gv, go, gup, gdown.reshape(w_down.shape), vec[0], vec[1], vec[2])


def solution(mesh):
    depth = mesh.shape["fsdp"]
    both = P(("dp", "fsdp"), None)
    weight, vector = P("fsdp", None), P("fsdp")
    return jax.shard_map(
        functools.partial(body, depth, mesh.shape["dp"] // PLANE),
        mesh=mesh,
        in_specs=(both,) * 3 + (weight,) * 6 + (vector,) * 3 + (both,),
        out_specs=(both, both) + (weight,) * 6 + (vector,) * 3,
        check_vma=False,
    )
```

```python
import functools

import jax
import jax.numpy as jnp
from jax import lax
from jax.experimental import pallas as pl
from jax.experimental.pallas import tpu as pltpu

from jax.sharding import PartitionSpec as P

HEADS = 12
EPS = 1e-06
NEG = -1e30
BF = jnp.bfloat16
F32 = jnp.float32
GATE, R1, R2, LIVE, DLOG, POS = range(6)


def nn(a, b):
    return lax.dot_general(a, b, (((1,), (0,)), ((), ())), preferred_element_type=F32)


def nt(a, b):
    return lax.dot_general(a, b, (((1,), (1,)), ((), ())), preferred_element_type=F32)


def tn(a, b):
    return lax.dot_general(a, b, (((0,), (0,)), ((), ())), preferred_element_type=F32)


def flat(v):
    return v.reshape(-1, v.shape[-1])


class Picker:
    def __init__(self, tokens, cot, picked, up, cols, bufs, sems):
        self.srcs, self.dsts, self.cols, self.bufs, self.sems = (tokens, cot), (picked, up), cols, bufs, sems

    def fetch(self, s, b):
        width = self.srcs[b].shape[-1]
        dst = self.bufs[b].at[:, :, :, :, 0:width]
        return pltpu.make_async_copy(self.srcs[b].at[s], dst, self.sems.at[b])

    def start(self, s):
        for b in range(2):
            self.fetch(s, b).start()

    def turn(self, idx, valid):
        seqs, slots = idx.shape
        for what, k in ((idx, POS), (valid, LIVE)):
            rows8 = what[...].astype(F32)
            if seqs < 8:
                rows8 = jnp.concatenate([rows8, jnp.zeros((8 - seqs, slots), F32)], axis=0)
            turned = rows8.T
            for s in range(seqs):
                self.cols[s * slots : (s + 1) * slots, k : k + 1] = turned[:, s : s + 1]

    def pick(self, s, slots, more):
        width = self.srcs[0].shape[-1]
        rows = slice(s * slots, (s + 1) * slots)
        length = self.bufs[0].shape[0] * self.bufs[0].shape[1] * self.bufs[0].shape[2] * self.bufs[0].shape[3]
        lane = lax.broadcasted_iota(jnp.int32, (slots, length), 1).astype(F32)
        hot = jnp.where(lane == self.cols[rows, POS : POS + 1], 1.0, 0.0).astype(BF)
        for b in range(2):
            self.fetch(s, b).wait()
            self.dsts[b][rows, :] = nn(hot, flat(self.bufs[b][:, :, :, :, 0:width])).astype(BF)
            if more:
                self.fetch(s + 1, b).start()


def norm_phase(picked, gains, cols, na, tile=256):
    total = picked.shape[0]

    @pl.loop(0, total // tile)
    def _(i):
        rows = pl.ds(pl.multiple_of(i * tile, tile), tile)
        x = picked[rows, :].astype(F32)
        cols[rows, GATE : GATE + 1] = jax.nn.sigmoid(
            jnp.sum(x * gains[2:3, :], axis=1, keepdims=True)
        )
        r1 = lax.rsqrt(jnp.mean(x * x, axis=1, keepdims=True) + EPS)
        cols[rows, R1 : R1 + 1] = r1
        na[rows, :] = (x * r1 * gains[0:1, :]).astype(BF)


def norm_again(picked, gains, cols, na, tile=256):
    @pl.loop(0, picked.shape[0] // tile)
    def _(i):
        rows = pl.ds(pl.multiple_of(i * tile, tile), tile)
        x = picked[rows, :].astype(F32)
        na[rows, :] = (x * cols[rows, R1 : R1 + 1] * gains[0:1, :]).astype(BF)


def qkv_one(na, wa, qkv, scale, m):
    @pl.loop(0, na.shape[1] // 256)
    def _(n):
        at = pl.ds(pl.multiple_of(n * 256, 256), 256)
        out = nn(na[...], flat(wa[m, :, :, :, :, at]))
        if m == 0:
            out = out * scale
        qkv[m, :, at] = out.astype(BF)


def two_heads(v2, low_half):
    zero = jnp.zeros_like(v2)
    return jnp.concatenate([jnp.where(low_half, v2, zero), jnp.where(low_half, zero, v2)], axis=0)


def prob_spot(s, p, slots):
    at = pl.ds(pl.multiple_of(s * slots, slots), slots)
    return (p // 2, slice(2 * (p % 2), 2 * (p % 2) + 2), slice(None), slice(None), slice(None), at)


def attention_forward(idx, valid, cols, qkv, probs, mixed, s):
    slots = idx.shape[1]
    width = mixed.shape[1]
    rows = pl.ds(pl.multiple_of(s * slots, slots), slots)
    low_half = lax.broadcasted_iota(jnp.int32, (slots, 128), 1) < 64
    mine = cols[rows, POS : POS + 1]
    other = idx[pl.ds(s, 1), :].astype(F32)
    seen = ((other < mine) & (valid[pl.ds(s, 1), :] > 0)) | (other == mine)
    bias = jnp.where(seen, 0.0, NEG)
    bias = jnp.concatenate([bias, bias], axis=0)
    for p in range(width // 128):
        at = slice(p * 128, p * 128 + 128)
        q2 = two_heads(qkv[0, rows, at], low_half)
        scores = nt(q2, qkv[1, rows, at]) + bias
        e = jnp.exp(scores - jnp.max(scores, axis=1, keepdims=True))
        pr = (e * (1.0 / jnp.sum(e, axis=1, keepdims=True))).astype(BF)
        spot = prob_spot(s, p, slots)
        probs[spot] = pr.reshape(2, 2, 2, 64, slots)
        o = nn(pr, qkv[2, rows, at])
        mixed[rows, at] = jnp.where(low_half, o[:slots], o[slots:]).astype(BF)


def attention_backward(qkv, probs, mixed, dmix, s, slots, scale):
    width = mixed.shape[1]
    rows = pl.ds(pl.multiple_of(s * slots, slots), slots)
    low_half = lax.broadcasted_iota(jnp.int32, (slots, 128), 1) < 64
    for p in range(width // 128):
        at = slice(p * 128, p * 128 + 128)
        do2 = two_heads(dmix[rows, at], low_half)
        o2 = mixed[rows, at].astype(F32)
        o2 = jnp.concatenate([o2, o2], axis=0)
        delta = jnp.sum(do2.astype(F32) * o2, axis=1, keepdims=True)
        k2 = qkv[1, rows, at]
        dp = nt(do2, qkv[2, rows, at])
        pr = flat(probs[prob_spot(s, p, slots)])
        ds = (pr.astype(F32) * (dp - delta)).astype(BF)
        q2 = two_heads(qkv[0, rows, at], low_half)
        dq = nn(ds, k2) * scale
        qkv[0, rows, at] = jnp.where(low_half, dq[:slots], dq[slots:]).astype(BF)
        qkv[1, rows, at] = tn(ds, q2).astype(BF)
        qkv[2, rows, at] = tn(pr, do2).astype(BF)


def out_phase(mixed, wa, attn_out):
    width = mixed.shape[1]

    @pl.loop(0, width // 256)
    def _(n):
        at = pl.ds(pl.multiple_of(n * 256, 256), 256)
        attn_out[:, at] = nn(mixed[...], flat(wa[3, :, :, :, :, at]))


def mid_norm(picked, attn_out, up, gains, cols, nm, nmt, dd, tile=256):
    total = picked.shape[0]
    for i in range(total // tile):
        rows = slice(i * tile, (i + 1) * tile)
        hidden = picked[rows, :].astype(F32) + cols[rows, GATE : GATE + 1] * attn_out[rows, :]
        r2 = lax.rsqrt(jnp.mean(hidden * hidden, axis=1, keepdims=True) + EPS)
        cols[rows, R2 : R2 + 1] = r2
        normed = (hidden * r2 * gains[1:2, :]).astype(BF)
        nm[rows, :] = normed
        nmt[:, rows] = normed.T
        dd[rows, :] = (up[rows, :].astype(F32) * cols[rows, LIVE : LIVE + 1]).astype(BF)


def gelu_both(u):
    k = 0.7978845608028654
    u2 = u * u
    t = jnp.tanh(u * (k + (k * 0.044715) * u2))
    half = 0.5 + 0.5 * t
    act = u * half
    slope = half + act * (1.0 - t) * (k + (3 * k * 0.044715) * u2)
    return act, slope


def mlp_up(nm, dd, wu, wd, act, dup, c, n):
    at = pl.ds(pl.multiple_of(n * 256, 256), 256)
    w_up, w_down = flat(wu[c, :, :, :, :, at]), flat(wd[c, n])
    tall = nm.shape[0] // act.shape[0]
    for i in range(act.shape[0]):
        rows = slice(i * tall, (i + 1) * tall)
        u = nn(nm[rows, :], w_up)
        dact = nt(dd[rows, :], w_down)
        a, slope = gelu_both(u)
        shape = act.shape[1:4] + (256,)
        act[i, :, :, :, at] = a.astype(BF).reshape(shape)
        dup[i, :, :, :, at] = (slope * dact).astype(BF).reshape(shape)


def mlp_down(act, wd, down, c):
    @pl.loop(0, down.shape[1] // 256)
    def _(n):
        at = pl.ds(pl.multiple_of(n * 256, 256), 256)
        out = nn(flat(act[...]), flat(wd[c, :, :, :, :, at]))
        down[:, at] = out if c == 0 else down[:, at] + out


def mlp_dnormed(dup, wu, dnm, c):
    @pl.loop(0, 2)
    def _(i):
        half = dnm.shape[0] // 2
        rows = pl.ds(pl.multiple_of(i * half, half), half)
        out = nt(flat(dup[pl.ds(2 * i, 2)]), flat(wu[c]))
        dnm[rows, :] = out if c == 0 else dnm[rows, :] + out


def mlp_grad_down(act, dd, wd, c):
    @pl.loop(0, act.shape[-1] // 256)
    def _(n):
        at = pl.ds(pl.multiple_of(n * 256, 256), 256)
        g = tn(flat(act[:, :, :, :, at]), dd[...]).astype(BF)
        wd[c, n] = g.reshape(wd.shape[2:])


def mlp_grad_up(nmt, dup, wu, c):
    @pl.loop(0, dup.shape[-1] // 512)
    def _(n):
        at = pl.ds(pl.multiple_of(n * 512, 512), 512)
        g = nn(nmt[...], flat(dup[:, :, :, :, at])).astype(BF)
        wu[c, :, :, :, :, at] = g.reshape(wu.shape[1:5] + (512,))


def mid_backward(picked, attn_out, up, down, dnm, gains, cols, datt, new_rows, small, tile=128):
    total = picked.shape[0]
    small[...] = jnp.zeros_like(small)

    @pl.loop(0, total // tile)
    def _(i):
        rows = pl.ds(pl.multiple_of(i * tile, tile), tile)
        x = picked[rows, :].astype(F32)
        gate = cols[rows, GATE : GATE + 1]
        live = cols[rows, LIVE : LIVE + 1]
        r = cols[rows, R2 : R2 + 1]
        ao = attn_out[rows, :]
        branch = gate * ao
        hidden = x + branch
        new_rows[rows, :] = (x + live * (branch + down[rows, :])).astype(BF)
        d = dnm[rows, :]
        hr = hidden * r
        dh = d * hr
        small[1:2, :] += jnp.sum(dh, axis=0, keepdims=True)
        mean = jnp.mean(dh * gains[1:2, :], axis=1, keepdims=True)
        d_hidden = r * (gains[1:2, :] * d - hr * mean)
        dnm[rows, :] = d_hidden
        d_branch = live * up[rows, :].astype(F32) + d_hidden
        d_logit = jnp.sum(d_branch * ao, axis=1, keepdims=True) * gate * (1.0 - gate)
        cols[rows, DLOG : DLOG + 1] = d_logit
        small[2:3, :] += jnp.sum(x * d_logit, axis=0, keepdims=True)
        datt[rows, :] = (d_branch * gate).astype(BF)


def out_backward(datt, mixed, wa, dmix):
    total, width = datt.shape

    @pl.loop(0, 2)
    def _(i):
        half = total // 2
        rows = pl.ds(pl.multiple_of(i * half, half), half)
        dmix[rows, :] = nt(datt[rows, :], flat(wa[3])).astype(BF)

    wa[3] = grad_of(mixed, datt[...]).reshape(wa.shape[1:])


def grad_of(left, right):
    parts = [tn(left[:, n * 384 : n * 384 + 384], right).astype(BF) for n in range(2)]
    return jnp.concatenate(parts, axis=0)


def qkv_normed(dqkv, wa, dnorm, beat):
    total = dqkv.shape[1]

    @pl.loop(0, 4)
    def _(i):
        part = total // 4
        rows = pl.ds(pl.multiple_of(i * part, part), part)
        dnorm[rows, :] = (
            nt(dqkv[0, rows, :], flat(wa[0]))
            + nt(dqkv[1, rows, :], flat(wa[1]))
            + nt(dqkv[2, rows, :], flat(wa[2]))
        )
        beat(i)


def first_backward(picked, up, dnorm, dhid, gains, cols, new_grads, small, beat, tile=128):
    total = picked.shape[0]

    @pl.loop(0, total // tile)
    def _(i):
        rows = pl.ds(pl.multiple_of(i * tile, tile), tile)
        x = picked[rows, :].astype(F32)
        r = cols[rows, R1 : R1 + 1]
        d = dnorm[rows, :]
        xr = x * r
        dx = d * xr
        small[0:1, :] += jnp.sum(dx, axis=0, keepdims=True)
        mean = jnp.mean(dx * gains[0:1, :], axis=1, keepdims=True)
        d_first = r * (gains[0:1, :] * d - xr * mean)
        d_picked = d_first + dhid[rows, :] + cols[rows, DLOG : DLOG + 1] * gains[2:3, :]
        new_grads[rows, :] = (up[rows, :].astype(F32) + d_picked).astype(BF)
        beat(i)


MESH_ID = pl.DeviceIdType.MESH
A_MATS, CHUNKS, PLANE = 4, 3, 8


class Place:
    def __init__(self, depth):
        dp = lax.axis_index("dp")
        self.depth = depth
        self.z = lax.axis_index("fsdp")
        self.core = lax.rem(dp, 2)
        self.x = lax.rem(lax.div(dp, 2), 2)
        self.y = lax.rem(lax.div(dp, 4), 2)
        self.sib = (dp + 1 - 2 * self.core, self.z)
        self.xn = (dp + 2 - 4 * self.x, self.z)
        self.yn = (dp + 4 - 8 * self.y, self.z)
        self.dp = dp

    def ahead(self, o):
        return lax.rem(self.z + o, self.depth)

    def behind(self, o):
        return lax.rem(self.z + self.depth - o, self.depth)

    def at_z(self, z):
        return (self.dp, z)

    def greet(self):
        barrier = pltpu.get_barrier_semaphore()
        peers = [self.sib, self.xn, self.yn]
        peers += [self.at_z(self.ahead(o)) for o in range(1, self.depth)]
        for peer in peers:
            pl.semaphore_signal(barrier, inc=1, device_id=peer, device_id_type=MESH_ID)
        pl.semaphore_wait(barrier, len(peers))


def half_of(ref, core):
    width = ref.shape[-1] // 2
    return pl.ds(pl.multiple_of(core * width, 128), width)


class Gather:
    SENDS, RECVS = 2, 5
    CORE, Z, X, Y, FAR = range(5)
    ARRAYS = A_MATS + 2 * CHUNKS

    def __init__(self, me, wa, wu, wd, sends, recvs):
        self.me, self.refs, self.sends, self.recvs = me, (wa, wu, wd), sends, recvs

    def array(self, a):
        wa, wu, wd = self.refs
        if a < A_MATS:
            return wa.at[a]
        return (wd if a % 2 else wu).at[(a - A_MATS) // 2]

    def piece(self, a, zi, xi, yi, core):
        ref = self.array(a)
        return ref.at[zi, xi, yi, :, half_of(ref, core)]

    def way(self, a):
        return a % 2

    def copy(self, a, kind, ref, dev):
        send = self.sends.at[a * self.SENDS + (0 if kind == self.CORE else 1)]
        recv = self.recvs.at[a * self.RECVS + kind]
        return pltpu.make_async_remote_copy(
            src_ref=ref, dst_ref=ref, send_sem=send, recv_sem=recv, device_id=dev, device_id_type=MESH_ID
        )

    def mine(self, a, zi, flip_x=False, flip_y=False):
        m = self.me
        return self.piece(a, zi, 1 - m.x if flip_x else m.x, 1 - m.y if flip_y else m.y, m.core)

    def took(self, a, kind):
        self.copy(a, kind, self.mine(a, slice(0, self.me.depth - 1)), self.me.xn).wait_recv()

    def core_copy(self, a, core):
        ref = self.array(a)
        return self.copy(a, self.CORE, ref.at[:, :, :, :, half_of(ref, core)], self.me.sib)

    def origins(self):
        return range(1, self.me.depth)

    def send_z(self, a):
        m = self.me
        for o in self.origins():
            self.copy(a, self.Z, self.mine(a, m.z), m.at_z(m.ahead(o))).start()

    def spread(self, a):
        m = self.me
        self.took(a, self.Z)
        for o in self.origins():
            self.copy(a, self.X, self.mine(a, m.behind(o)), m.xn).start()
            self.copy(a, self.Y, self.mine(a, m.behind(o)), m.yn).start()

    def forward(self, a):
        m, by_x = self.me, self.way(a) == 0
        self.took(a, self.X if by_x else self.Y)
        for o in self.origins():
            ref = self.mine(a, m.behind(o), by_x, not by_x)
            self.copy(a, self.FAR, ref, m.yn if by_x else m.xn).start()

    def across(self, a):
        self.took(a, self.Y if self.way(a) == 0 else self.X)
        self.took(a, self.FAR)
        self.core_copy(a, self.me.core).start()

    def ready(self, a):
        self.core_copy(a, 1 - self.me.core).wait_recv()

    def settle(self, a):
        m, ref = self.me, self.array(a)
        self.core_copy(a, m.core).wait_send()
        sent = ref.at[0 : m.depth - 1, :, :, :, half_of(ref, m.core)]
        self.copy(a, self.Z, sent, m.xn).wait_send()


class Owned:
    def __init__(self, me, shards, wa, wu, wd, sems):
        wq, wk, wv, wo, up, down = shards
        z, core = me.z, me.core
        half = half_of(wa, core)
        self.copies = {a: [] for a in range(Gather.ARRAYS)}
        for m, w in enumerate((wq, wk, wv, wo)):
            self.copies[m].append((w.at[:, :, :, half], wa.at[m, z, :, :, :, half]))
        ff_own = up.shape[-1] // me.depth
        for c in range(CHUNKS):
            for j in range(2):
                block = 2 * core + j
                src = up.at[:, :, :, pl.ds(pl.multiple_of(block * ff_own + c * 256, 128), 256)]
                dst = wu.at[c, z, :, :, :, pl.ds(pl.multiple_of(block * 256, 128), 256)]
                self.copies[A_MATS + 2 * c].append((src, dst))
            self.copies[A_MATS + 1 + 2 * c].append((down.at[c, :, :, :, half], wd.at[c, z, :, :, :, half]))
        self.sems = sems

    def all_of(self, a):
        for i, (src, dst) in enumerate(self.copies[a]):
            yield pltpu.make_async_copy(src, dst, self.sems.at[2 * a + i])

    def start(self, a):
        for c in self.all_of(a):
            c.start()

    def wait(self, a):
        for c in self.all_of(a):
            c.wait()


class Reduce:
    SENDS, RECVS = 2, 7
    CORE, FIRST, SECOND, Z, BACK, FAR, LAST = range(7)

    def __init__(
        self, me, w, from_core, from_x, from_y, then_x, then_y, from_z, sends, recvs, frees, at, way
    ):
        self.me, self.w, self.way, self.free, base = me, w, way, frees.at[at], at
        self.from_core, self.from_x, self.from_y = from_core, from_x, from_y
        self.then_x, self.then_y, self.from_z = then_x, then_y, from_z
        self.sends, self.recvs, self.base = sends, recvs, base
        self.mine, self.theirs = half_of(w, me.core), half_of(w, 1 - me.core)

    def copy(self, kind, src, dst, dev):
        small = kind in (self.Z, self.BACK, self.FAR)
        send = self.sends.at[self.base * self.SENDS + small]
        recv = self.recvs.at[self.base * self.RECVS + kind]
        return pltpu.make_async_remote_copy(
            src_ref=src, dst_ref=dst, send_sem=send, recv_sem=recv, device_id=dev, device_id_type=MESH_ID
        )

    def took(self, kind, ref):
        self.copy(kind, ref, ref, self.me.sib).wait_recv()

    def sent(self, kind, ref):
        self.copy(kind, ref, ref, self.me.sib).wait_send()

    def z_copy(self, o):
        m = self.me
        src = self.w.at[m.ahead(o), m.x, m.y, :, self.mine]
        return self.copy(self.Z, src, self.from_z.at[o - 1], m.at_z(m.ahead(o)))

    def back(self, kind, xi, yi, dev):
        ref = self.from_core.at[0, xi, yi]
        return self.copy(kind, ref, ref, dev)

    def add(self, at, arrived):
        self.w[at] = self.w[at] + arrived

    def t1(self):
        self.copy(self.CORE, self.w.at[:, :, :, :, self.theirs], self.from_core, self.me.sib).start()

    def t2(self):
        m, w = self.me, self.w
        self.took(self.CORE, self.from_core)

        @pl.loop(0, 2 * m.depth)
        def _(i):
            zi, xi = lax.div(i, 2), lax.rem(i, 2)
            self.add((zi, xi, slice(None), slice(None), self.mine), self.from_core[zi, xi])

        pl.semaphore_signal(self.free, inc=1, device_id=m.sib, device_id_type=MESH_ID)
        self.copy(self.FIRST, w.at[0:2, 1 - m.x, :, :, self.mine], self.from_x, m.xn).start()
        self.copy(self.FIRST, w.at[2:4, :, 1 - m.y, :, self.mine], self.from_y, m.yn).start()

    def t3(self):
        m, w = self.me, self.w
        self.took(self.FIRST, w.at[0:2, :, :, :, self.mine])

        @pl.loop(0, 2)
        def _(zi):
            self.add((zi, m.x, slice(None), slice(None), self.mine), self.from_x[zi])
            self.add((2 + zi, slice(None), m.y, slice(None), self.mine), self.from_y[zi])

        self.copy(self.SECOND, w.at[0:2, m.x, 1 - m.y, :, self.mine], self.then_y, m.yn).start()
        self.copy(self.SECOND, w.at[2:4, 1 - m.x, m.y, :, self.mine], self.then_x, m.xn).start()

    def t4(self):
        m = self.me
        self.took(self.SECOND, self.w.at[0:2, 0:2, 0, :, self.mine])
        self.add((slice(0, 2), m.x, m.y, slice(None), self.mine), self.then_y[...])
        self.add((slice(2, 4), m.x, m.y, slice(None), self.mine), self.then_x[...])
        for o in range(1, m.depth):
            self.z_copy(o).start()

    def t5(self):
        m = self.me
        total = self.w[m.z, m.x, m.y, :, self.mine].astype(F32)
        self.took(self.Z, self.from_z)
        for o in range(1, m.depth):
            total = total + self.from_z[o - 1].astype(F32)
        self.from_core[0, m.x, m.y] = total.astype(BF)
        self.back(self.BACK, m.x, m.y, m.xn).start()
        self.back(self.BACK, m.x, m.y, m.yn).start()

    def t6(self):
        m = self.me
        self.took(self.BACK, self.from_core.at[0, 0:2, 0])
        if self.way == 0:
            self.back(self.FAR, 1 - m.x, m.y, m.yn).start()
        else:
            self.back(self.FAR, m.x, 1 - m.y, m.xn).start()

    def t7(self):
        m = self.me
        self.took(self.FAR, self.from_core.at[0, 0, 0])
        pl.semaphore_wait(self.free, 1)
        self.copy(self.LAST, self.from_core.at[0], self.from_core.at[1], m.sib).start()

    def t8(self):
        m = self.me
        self.took(self.LAST, self.from_core.at[1])
        self.sent(self.CORE, self.w)
        self.sent(self.Z, self.w.at[0 : m.depth - 1, 0:2, 0, :, self.mine])


class SmallSum:
    def __init__(self, me, small, inbox, sends, recvs, base):
        self.me, self.small, self.inbox = me, small, inbox
        self.sends, self.recvs, self.base = sends, recvs, base

    def copy(self, k, src, dst, dev):
        return pltpu.make_async_remote_copy(
            src_ref=src, dst_ref=dst, send_sem=self.sends.at[self.base[0]], recv_sem=self.recvs.at[self.base[1] + k],
            device_id=dev, device_id_type=MESH_ID,
        )

    def peer(self, k):
        return (self.me.sib, self.me.xn, self.me.yn)[k]

    def step(self, k):
        m, small, inbox = self.me, self.small, self.inbox
        if 1 <= k <= 3:
            self.copy(k - 1, small.at[0], inbox.at[k - 1], m.sib).wait_recv()
            small[k] = small[k - 1] + inbox[k - 1]
        if k <= 2:
            self.copy(k, small.at[k], inbox.at[k], self.peer(k)).start()
        if k == 3:
            for o in range(1, m.depth):
                self.copy(3, small.at[3], inbox.at[2 + o], m.at_z(m.ahead(o))).start()
        if k == 4:
            self.copy(3, inbox.at[3:], inbox.at[3:], m.sib).wait_recv()
            total = small[3]
            for o in range(1, m.depth):
                total = total + inbox[2 + o]
            small[4] = total
            self.copy(3, inbox, inbox, m.sib).wait_send()


def chunk_boxes(rows_a, width, rows_d, ff_c):
    def boxes(n, rows, cols, first):
        def box(*lead):
            return pltpu.VMEM((n,) + lead + (rows, cols), BF)

        return ([box(4, 2, 2)] if first else []) + [box(2, 2), box(2, 2), box(2), box(2), box(3)]

    return (
        boxes(CHUNKS, rows_a, ff_c // 2, True)
        + boxes(CHUNKS, rows_d, width // 2, True)
        + boxes(A_MATS, rows_a, width // 2, False)
    )


def block_kernel(
    depth, tokens, cot, idx, valid, wq, wk, wv, wo, up_in, down_in, gain1, gain2, gain3,
    new_rows, new_grads, fa, fu, fd, small_out,
    wa, wu, wd, picked, up, cols, na, nmt, dd, qkv, probs, mixed, attn_out, act, dup, down, dnm,
    gains, gpad, gbox, small, inbox,
    tok_sem, own_sem, out_sem, ag_send, ag_recv, rs_send, rs_recv, frees, opened, *boxes,
):
    seqs, slots = idx.shape
    width = picked.shape[1]
    scale = (width // HEADS) ** -0.5
    rows_a = wa.shape[-2]
    half = width // 2
    me = Place(depth)
    me.greet()
    own = Owned(me, (wq, wk, wv, wo, up_in, down_in), wa, wu, wd, own_sem)
    ag = Gather(me, wa, wu, wd, ag_send, ag_recv)
    sem_at = (20, 70)
    others = range(1, depth)

    def gain_copy(o):
        return pltpu.make_async_remote_copy(
            src_ref=gpad, dst_ref=gbox.at[o - 1], send_sem=rs_send.at[21], recv_sem=rs_recv.at[74],
            device_id=me.at_z(me.ahead(o)), device_id_type=MESH_ID,
        )

    own.start(0)
    own.start(1)
    picker = Picker(tokens, cot, picked, up, cols, (act, dup), tok_sem)
    picker.start(0)
    for a in range(2, Gather.ARRAYS):
        own.start(a)
    own.wait(0)
    ag.send_z(0)
    picker.turn(idx, valid)
    own.wait(1)
    ag.send_z(1)
    owned = gain1.shape[0]
    spot = lax.broadcasted_iota(jnp.int32, (owned, width), 1) - lax.broadcasted_iota(jnp.int32, (owned, width), 0)
    spot = jnp.where(spot == me.z * owned, 1.0, 0.0).astype(BF)
    gpad[...] = jnp.zeros_like(gpad)
    for i, g in enumerate((gain1, gain2, gain3)):
        gpad[i : i + 1, :] = nn(g[...].astype(F32).reshape(1, owned).astype(BF), spot)
    for o in others:
        gain_copy(o).start()
    picker.pick(0, slots, True)
    for a in range(2, Gather.ARRAYS):
        own.wait(a)
    ag.send_z(2)
    ag.spread(0)
    picker.pick(1, slots, True)
    ag.send_z(3)
    picker.pick(2, slots, True)
    ag.send_z(4)
    ag.forward(0)
    ag.spread(1)
    picker.pick(3, slots, False)
    pltpu.make_async_remote_copy(
        src_ref=gbox, dst_ref=gbox, send_sem=rs_send.at[21], recv_sem=rs_recv.at[74],
        device_id=me.sib, device_id_type=MESH_ID,
    ).wait()
    total = gpad[...]
    for o in others:
        total = total + gbox[o - 1]
    gains[...] = total
    norm_phase(picked, gains, cols, na)
    ag.across(0)
    ag.send_z(5)
    ag.forward(1)
    ag.spread(2)
    ag.ready(0)
    qkv_one(na, wa, qkv, scale, 0)
    ag.across(1)
    ag.send_z(6)
    ag.forward(2)
    ag.ready(1)
    qkv_one(na, wa, qkv, scale, 1)
    ag.across(2)
    ag.spread(3)
    ag.ready(2)
    qkv_one(na, wa, qkv, scale, 2)
    ag.forward(3)
    ag.spread(4)
    ag.send_z(7)

    @pl.loop(0, seqs)
    def _(s):
        attention_forward(idx, valid, cols, qkv, probs, mixed, s)

        @pl.when(s == 0)
        def _():
            ag.across(3)
            ag.spread(5)

        @pl.when(s == 1)
        def _():
            ag.forward(4)
            ag.send_z(8)
            ag.send_z(9)

        @pl.when(s == 2)
        def _():
            ag.forward(5)
            ag.across(4)

        @pl.when(s == 3)
        def _():
            ag.spread(6)

    ag.ready(3)
    out_phase(mixed, wa, attn_out)
    ag.across(5)
    mid_norm(picked, attn_out, up, gains, cols, na, nmt, dd)
    ag.forward(6)
    ag.spread(7)

    ubox, dbox, abox = boxes[0:6], boxes[6:12], boxes[12:17]
    reducers = {}

    def reducer(name, at, w, core_box, rest, i, way):
        reducers[name] = Reduce(me, w, core_box, *[x.at[i] for x in rest], rs_send, rs_recv, frees, at, way)

    for c in range(CHUNKS):
        reducer("u%d" % c, c, wu.at[c], ubox[0].at[c], ubox[1:], c, 0)
        reducer("d%d" % c, 3 + c, wd.at[c], dbox[0].at[c], dbox[1:], c, 1)
    spots = ((act, 0), (act, half), (dup, 0), (dup, half))
    terms = [probs.at[m, :, :, :, 0:rows_a, 0:width] for m in range(3)] + [wa.at[3]]
    for m, name in enumerate("qkvo"):
        ref, lane = spots[m]
        box = ref.at[:, :, :, 0:rows_a, lane : lane + half]
        reducer(name, 6 + m, terms[m], box, abox, m, m % 2)
    finals = {"q": (fa, 0), "k": (fa, 1), "v": (fa, 2), "o": (fa, 3)}
    for c in range(CHUNKS):
        finals["u%d" % c] = (fu, c)
        finals["d%d" % c] = (fd, c)
    order = list(finals)

    def result_copies(name):
        dst, i = finals[name]
        box = reducers[name].from_core
        for h, core in ((0, me.core), (1, 1 - me.core)):
            yield pltpu.make_async_copy(box.at[h], dst.at[i, :, :, :, half_of(dst, core)], out_sem.at[{"u": 1, "d": 2}.get(name[0], 0)])

    def step(k, *names):
        for name in names:
            getattr(reducers[name], "t%d" % k)()
            if k == 8:
                for c in result_copies(name):
                    c.start()

    for c in range(CHUNKS):
        for a in (A_MATS + 2 * c, A_MATS + 1 + 2 * c):
            ag.ready(a)

        @pl.loop(0, 4)
        def _(n):
            mlp_up(na, dd, wu, wd, act, dup, c, n)
            if c > 0:

                @pl.when(n == 1)
                def _():
                    step(2, "d%d" % (c - 1), "u%d" % (c - 1))

        if c == 0:
            ag.across(6)
            ag.spread(8)
            ag.forward(7)
        if c == 1:
            ag.across(9)
        mlp_down(act, wd, down, c)
        mlp_dnormed(dup, wu, dnm, c)
        if c == 0:
            ag.across(7)
            ag.spread(9)
        if c == 2:
            step(4, "d0", "u0")
        ag.settle(A_MATS + 2 * c)
        ag.settle(A_MATS + 1 + 2 * c)
        mlp_grad_down(act, dd, wd, c)
        step(1, "d%d" % c)
        if c == 0:
            ag.forward(8)
        mlp_grad_up(nmt, dup, wu, c)
        if c == 0:
            ag.across(8)
            ag.forward(9)
        step(1, "u%d" % c)
        if c > 0:
            step(3, "d%d" % (c - 1), "u%d" % (c - 1))
    pl.semaphore_signal(opened, inc=1, device_id=me.sib, device_id_type=MESH_ID)
    for a in range(A_MATS):
        ag.settle(a)
    datt, dmix = na, dd
    mid_backward(picked, attn_out, up, down, dnm, gains, cols, datt, dd, small.at[0])
    rows_out = pltpu.make_async_copy(dd, new_rows, tok_sem.at[0])
    rows_out.start()
    step(2, "d2", "u2")
    rows_out.wait()
    out_backward(datt, mixed, wa, dmix)
    pl.semaphore_wait(opened, 1)
    step(1, "o")
    step(4, "d1", "u1")
    step(5, "d0", "u0")
    norm_again(picked, gains, cols, na)

    @pl.loop(0, seqs)
    def _(s):
        attention_backward(qkv, probs, mixed, dmix, s, slots, scale)

        @pl.when(s == 0)
        def _():
            step(2, "o")
            step(6, "d0", "u0")

        @pl.when(s == 1)
        def _():
            step(7, "d0", "u0")

        @pl.when(s == 2)
        def _():
            step(3, "d2", "u2")
            step(8, "d0", "u0")

        @pl.when(s == 3)
        def _():
            step(3, "o")

    for m, name in enumerate("qkv"):
        terms[m][...] = grad_of(na, qkv[m]).reshape(wa.shape[1:])
        step(1, name)
        if m == 0:
            step(5, "d1", "u1")
        if m > 0:
            step(2, "qkv"[m - 1])
    step(4, "d2", "u2")

    def at_beats(*todo):
        def beat(i):
            for k, work in todo:

                @pl.when(i == k)
                def _():
                    for t, *names in work:
                        step(t, *names)

        return beat

    qkv_normed(
        qkv, wa, down, at_beats((0, [(2, "v")]), (1, [(4, "o")]), (2, [(3, "q")]), (3, [(6, "d1", "u1"), (3, "k")]))
    )
    first_backward(
        picked, up, down, dnm, gains, cols, dd, small.at[0],
        at_beats((2, [(7, "d1", "u1")]), (4, [(3, "v"), (4, "q")])),
    )
    grads_out = pltpu.make_async_copy(dd, new_grads, tok_sem.at[1])
    grads_out.start()
    sums = SmallSum(me, small, inbox, rs_send, rs_recv, sem_at)
    sums.step(0)
    step(4, "k")
    step(5, "d2", "u2")
    sums.step(1)
    step(5, "o")
    step(4, "v")
    step(8, "d1", "u1")
    sums.step(2)
    step(6, "d2", "u2", "o")
    sums.step(3)
    step(5, "q")
    step(7, "d2", "u2", "o")
    step(5, "k")
    sums.step(4)
    step(6, "q")
    step(5, "v")
    step(6, "k")
    step(7, "q")
    step(8, "d2", "u2", "o")
    step(6, "v")
    step(7, "k", "v")
    step(8, *"qkv")
    small_out[...] = small[4]
    for i, dst in enumerate((fa, fu, fd)):
        pltpu.make_async_copy(dst, dst, out_sem.at[i]).wait()
    grads_out.wait()


def place_kernel(depth, idx, tokens, cot, new_rows, new_grads, fa, fu, fd, sums,
                 out, grad, gq, gk, gv, go, gup, gdown, g1, g2, g3):
    s = pl.program_id(0)
    length, slots = tokens.shape[0], idx.shape[1]
    spot = lax.broadcasted_iota(jnp.int32, (length, slots), 0)
    hot = jnp.where(spot == idx[pl.ds(s, 1), :], 1.0, 0.0)
    hit = jnp.sum(hot, axis=1, keepdims=True) > 0
    hot = hot.astype(BF)
    for src, rows, dst in ((tokens, new_rows, out), (cot, new_grads, grad)):
        dst[...] = jnp.where(hit, nn(hot, rows[...]), src[...].astype(F32)).astype(BF)
    place_weights(fa, fu, fd, gq, gk, gv, go, gup, gdown)
    own = g1.shape[0]
    for k in range(depth):

        @pl.when((s == 0) & (lax.axis_index("fsdp") == k))
        def _():
            for i, g in enumerate((g1, g2, g3)):
                g[...] = sums[i, k * own : (k + 1) * own]


def place_weights(fa, fu, fd, gq, gk, gv, go, gup, gdown):
    for m, g in enumerate((gq, gk, gv, go)):
        g[...] = fa[m, 0].astype(F32)
    quarter = 256
    ff_own = gup.shape[1] // 4
    for c in range(CHUNKS):
        for j in range(4):
            gup[:, j * ff_own + c * quarter : j * ff_own + (c + 1) * quarter] = fu[c, 0, :, j * quarter : (j + 1) * quarter].astype(F32)
        gdown[c, 0] = fd[c, 0].astype(F32)


def remote_params(collective_id, limit=60):
    return pltpu.CompilerParams(
        collective_id=collective_id, has_side_effects=True, vmem_limit_bytes=limit * 2**20
    )


def over_groups(groups, terms):
    if groups == 1:
        return terms
    dp = groups * PLANE
    total = [t.astype(F32) for t in terms]
    for k in range(groups.bit_length() - 1):
        hop = PLANE << k
        pairs = [(i, i ^ hop) for i in range(dp)]
        total = [t + lax.ppermute(t, "dp", pairs) for t in total]
    return total


def body(depth, groups, tokens, row_index, row_valid, w_query, w_key, w_value, w_out, w_up, w_down,
         gain_attn, gain_mlp, w_router, cotangent):
    seqs, slots = row_index.shape
    width = tokens.shape[1]
    own = w_query.shape[0]
    ff = w_up.shape[1]
    length = tokens.shape[0] // seqs
    total = seqs * slots
    rq, cw = own // 4, ff // CHUNKS
    dq = w_down.shape[0] // (4 * CHUNKS)
    sd = jax.ShapeDtypeStruct
    hbm, vm = pl.BlockSpec(memory_space=pl.ANY), pl.BlockSpec(memory_space=pltpu.VMEM)
    sem = pltpu.SemaphoreType.DMA
    vmem = pltpu.VMEM
    gains3 = (gain_attn, gain_mlp, w_router)
    squares = [w.reshape(2, 2, rq, width) for w in (w_query, w_key, w_value, w_out)]
    sa, su, sdn = (A_MATS, depth, 2, 2, rq, width), (CHUNKS, depth, 2, 2, rq, cw), (CHUNKS, depth, 2, 2, dq, width)
    narr = Gather.ARRAYS
    rows = (total, width)
    work = (4, 2, 2, total // 16, cw)
    regular = pltpu.SemaphoreType.REGULAR
    blocks = (seqs, 4, 2, 2, length // 16, width)
    new_rows, new_grads, fa, fu, fd, sums = pl.pallas_call(
        functools.partial(block_kernel, depth),
        out_shape=(
            sd(rows, BF), sd(rows, BF), sd(sa[:1] + sa[2:], BF), sd(su[:1] + su[2:], BF), sd(sdn[:1] + sdn[2:], BF),
            sd((8, width), F32),
        ),
        in_specs=[hbm, hbm, vm, vm] + [hbm] * 6 + [vm] * 3,
        out_specs=(hbm,) * 5 + (vm,),
        scratch_shapes=[
            vmem(sa, BF), vmem(su, BF), vmem(sdn, BF), vmem(rows, BF), vmem(rows, BF), vmem((total, 128), F32),
            vmem(rows, BF), vmem((width, total), BF), vmem(rows, BF), vmem((3,) + rows, BF), vmem((3,) + work, BF),
            vmem(rows, BF), vmem(rows, F32), vmem(work, BF), vmem(work, BF), vmem(rows, F32), vmem(rows, F32),
            vmem((8, width), F32), vmem((8, width), F32), vmem((depth - 1, 8, width), F32), vmem((5, 8, width), F32), vmem((2 + depth, 8, width), F32),
            sem((2,)), sem((2 * narr,)), sem((3,)), sem((2 * narr,)), sem((5 * narr,)),
            sem((2 * narr + 2,)), sem((7 * narr + 5,)), regular((narr,)), regular,
        ]
        + chunk_boxes(rq, width, dq, cw),
        compiler_params=remote_params(0, 63),
    )(
        tokens.reshape(blocks), cotangent.reshape(blocks), row_index, row_valid, *squares,
        w_up.reshape(2, 2, rq, ff), w_down.reshape(CHUNKS, 2, 2, dq, width), *gains3,
    )
    fa, fu, fd, sums = over_groups(groups, (fa, fu, fd, sums))

    def by_seq(*shape):
        return pl.BlockSpec(shape, lambda i: (i,) + (0,) * (len(shape) - 1))

    def by_quarter(*shape):
        return pl.BlockSpec(shape, lambda i: (0, i) + (0,) * (len(shape) - 2))

    out, grad, gq, gk, gv, go, gup, gdown, g1, g2, g3 = pl.pallas_call(
        functools.partial(place_kernel, depth),
        grid=(seqs,),
        out_shape=(sd(tokens.shape, BF),) * 2
        + (sd((own, width), F32),) * 4
        + (sd((own, ff), F32), sd((CHUNKS, 4, dq, width), F32))
        + (sd((own,), F32),) * 3,
        in_specs=[pl.BlockSpec((seqs, slots), lambda i: (0, 0))]
        + [by_seq(length, width)] * 2
        + [by_seq(slots, width)] * 2
        + [by_quarter(A_MATS, 1, rq, width), by_quarter(CHUNKS, 1, rq, cw), by_quarter(CHUNKS, 1, dq, width)]
        + [pl.BlockSpec((8, width), lambda i: (0, 0))],
        out_specs=[by_seq(length, width)] * 2
        + [by_seq(rq, width)] * 4
        + [by_seq(rq, ff), by_quarter(CHUNKS, 1, dq, width)]
        + [pl.BlockSpec((own,), lambda i: (0,))] * 3,
        compiler_params=pltpu.CompilerParams(vmem_limit_bytes=62 * 2**20),
    )(
        row_index, tokens, cotangent, new_rows, new_grads, fa.reshape(A_MATS, 4, rq, width),
        fu.reshape(CHUNKS, 4, rq, cw), fd.reshape(CHUNKS, 4, dq, width), sums,
    )
    return (out, grad, gq, gk, gv, go, gup, gdown.reshape(w_down.shape), g1, g2, g3)


def solution(mesh):
    depth = mesh.shape["fsdp"]
    both = P(("dp", "fsdp"), None)
    weight, vector = P("fsdp", None), P("fsdp")
    return jax.shard_map(
        functools.partial(body, depth, mesh.shape["dp"] // PLANE),
        mesh=mesh,
        in_specs=(both,) * 3 + (weight,) * 6 + (vector,) * 3 + (both,),
        out_specs=(both, both) + (weight,) * 6 + (vector,) * 3,
        check_vma=False,
    )
```

```python
import functools

import jax
import jax.numpy as jnp
from jax import lax
from jax.experimental import pallas as pl
from jax.experimental.pallas import tpu as pltpu

from jax.sharding import PartitionSpec as P

HEADS = 12
EPS = 1e-06
NEG = -1e30
BF = jnp.bfloat16
F32 = jnp.float32
GATE, R1, R2, LIVE, DLOG, POS = range(6)


def nn(a, b):
    return lax.dot_general(a, b, (((1,), (0,)), ((), ())), preferred_element_type=F32)


def nt(a, b):
    return lax.dot_general(a, b, (((1,), (1,)), ((), ())), preferred_element_type=F32)


def tn(a, b):
    return lax.dot_general(a, b, (((0,), (0,)), ((), ())), preferred_element_type=F32)


def flat(v):
    return v.reshape(-1, v.shape[-1])


class Picker:
    def __init__(self, tokens, cot, picked, up, cols, bufs, sems):
        self.srcs, self.dsts, self.cols, self.bufs, self.sems = (tokens, cot), (picked, up), cols, bufs, sems

    def fetch(self, s, b):
        width = self.srcs[b].shape[-1]
        dst = self.bufs[b].at[:, :, :, :, 0:width]
        return pltpu.make_async_copy(self.srcs[b].at[s], dst, self.sems.at[b])

    def start(self, s):
        for b in range(2):
            self.fetch(s, b).start()

    def turn(self, idx, valid):
        seqs, slots = idx.shape
        for what, k in ((idx, POS), (valid, LIVE)):
            rows8 = what[...].astype(F32)
            if seqs < 8:
                rows8 = jnp.concatenate([rows8, jnp.zeros((8 - seqs, slots), F32)], axis=0)
            turned = rows8.T
            for s in range(seqs):
                self.cols[s * slots : (s + 1) * slots, k : k + 1] = turned[:, s : s + 1]

    def pick(self, s, slots, more):
        width = self.srcs[0].shape[-1]
        rows = slice(s * slots, (s + 1) * slots)
        length = self.bufs[0].shape[0] * self.bufs[0].shape[1] * self.bufs[0].shape[2] * self.bufs[0].shape[3]
        lane = lax.broadcasted_iota(jnp.int32, (slots, length), 1).astype(F32)
        hot = jnp.where(lane == self.cols[rows, POS : POS + 1], 1.0, 0.0).astype(BF)
        for b in range(2):
            self.fetch(s, b).wait()
            self.dsts[b][rows, :] = nn(hot, flat(self.bufs[b][:, :, :, :, 0:width])).astype(BF)
            if more:
                self.fetch(s + 1, b).start()


def norm_phase(picked, gains, cols, na, tile=256):
    total = picked.shape[0]

    @pl.loop(0, total // tile)
    def _(i):
        rows = pl.ds(pl.multiple_of(i * tile, tile), tile)
        x = picked[rows, :].astype(F32)
        cols[rows, GATE : GATE + 1] = jax.nn.sigmoid(
            jnp.sum(x * gains[2:3, :], axis=1, keepdims=True)
        )
        r1 = lax.rsqrt(jnp.mean(x * x, axis=1, keepdims=True) + EPS)
        cols[rows, R1 : R1 + 1] = r1
        na[rows, :] = (x * r1 * gains[0:1, :]).astype(BF)


def norm_again(picked, gains, cols, na, tile=256):
    @pl.loop(0, picked.shape[0] // tile)
    def _(i):
        rows = pl.ds(pl.multiple_of(i * tile, tile), tile)
        x = picked[rows, :].astype(F32)
        na[rows, :] = (x * cols[rows, R1 : R1 + 1] * gains[0:1, :]).astype(BF)


def qkv_one(na, wa, qkv, scale, m):
    @pl.loop(0, na.shape[1] // 256)
    def _(n):
        at = pl.ds(pl.multiple_of(n * 256, 256), 256)
        out = nn(na[...], flat(wa[m, :, :, :, :, at]))
        if m == 0:
            out = out * scale
        qkv[m, :, at] = out.astype(BF)


def two_heads(v2, low_half):
    zero = jnp.zeros_like(v2)
    return jnp.concatenate([jnp.where(low_half, v2, zero), jnp.where(low_half, zero, v2)], axis=0)


def prob_spot(s, p, slots):
    at = pl.ds(pl.multiple_of(s * slots, slots), slots)
    return (p // 2, slice(2 * (p % 2), 2 * (p % 2) + 2), slice(None), slice(None), slice(None), at)


def attention_forward(idx, valid, cols, qkv, probs, mixed, s):
    slots = idx.shape[1]
    width = mixed.shape[1]
    rows = pl.ds(pl.multiple_of(s * slots, slots), slots)
    low_half = lax.broadcasted_iota(jnp.int32, (slots, 128), 1) < 64
    mine = cols[rows, POS : POS + 1]
    other = idx[pl.ds(s, 1), :].astype(F32)
    seen = ((other < mine) & (valid[pl.ds(s, 1), :] > 0)) | (other == mine)
    bias = jnp.where(seen, 0.0, NEG)
    bias = jnp.concatenate([bias, bias], axis=0)
    for p in range(width // 128):
        at = slice(p * 128, p * 128 + 128)
        q2 = two_heads(qkv[0, rows, at], low_half)
        scores = nt(q2, qkv[1, rows, at]) + bias
        e = jnp.exp(scores - jnp.max(scores, axis=1, keepdims=True))
        pr = (e * (1.0 / jnp.sum(e, axis=1, keepdims=True))).astype(BF)
        spot = prob_spot(s, p, slots)
        probs[spot] = pr.reshape(2, 2, 2, 64, slots)
        o = nn(pr, qkv[2, rows, at])
        mixed[rows, at] = jnp.where(low_half, o[:slots], o[slots:]).astype(BF)


def attention_backward(qkv, probs, mixed, dmix, s, slots, scale):
    width = mixed.shape[1]
    rows = pl.ds(pl.multiple_of(s * slots, slots), slots)
    low_half = lax.broadcasted_iota(jnp.int32, (slots, 128), 1) < 64
    for p in range(width // 128):
        at = slice(p * 128, p * 128 + 128)
        do2 = two_heads(dmix[rows, at], low_half)
        o2 = mixed[rows, at].astype(F32)
        o2 = jnp.concatenate([o2, o2], axis=0)
        delta = jnp.sum(do2.astype(F32) * o2, axis=1, keepdims=True)
        k2 = qkv[1, rows, at]
        dp = nt(do2, qkv[2, rows, at])
        pr = flat(probs[prob_spot(s, p, slots)])
        ds = (pr.astype(F32) * (dp - delta)).astype(BF)
        q2 = two_heads(qkv[0, rows, at], low_half)
        dq = nn(ds, k2) * scale
        qkv[0, rows, at] = jnp.where(low_half, dq[:slots], dq[slots:]).astype(BF)
        qkv[1, rows, at] = tn(ds, q2).astype(BF)
        qkv[2, rows, at] = tn(pr, do2).astype(BF)


def out_phase(mixed, wa, attn_out):
    width = mixed.shape[1]

    @pl.loop(0, width // 256)
    def _(n):
        at = pl.ds(pl.multiple_of(n * 256, 256), 256)
        attn_out[:, at] = nn(mixed[...], flat(wa[3, :, :, :, :, at]))


def mid_norm(picked, attn_out, up, gains, cols, nm, nmt, dd, tile=256):
    total = picked.shape[0]
    for i in range(total // tile):
        rows = slice(i * tile, (i + 1) * tile)
        hidden = picked[rows, :].astype(F32) + cols[rows, GATE : GATE + 1] * attn_out[rows, :]
        r2 = lax.rsqrt(jnp.mean(hidden * hidden, axis=1, keepdims=True) + EPS)
        cols[rows, R2 : R2 + 1] = r2
        normed = (hidden * r2 * gains[1:2, :]).astype(BF)
        nm[rows, :] = normed
        nmt[:, rows] = normed.T
        dd[rows, :] = (up[rows, :].astype(F32) * cols[rows, LIVE : LIVE + 1]).astype(BF)


def gelu_both(u):
    k = 0.7978845608028654
    u2 = u * u
    t = jnp.tanh(u * (k + (k * 0.044715) * u2))
    half = 0.5 + 0.5 * t
    act = u * half
    slope = half + act * (1.0 - t) * (k + (3 * k * 0.044715) * u2)
    return act, slope


def mlp_up(nm, dd, wu, wd, act, dup, c, n):
    at = pl.ds(pl.multiple_of(n * 256, 256), 256)
    w_up, w_down = flat(wu[c, :, :, :, :, at]), flat(wd[c, n])
    tall = nm.shape[0] // act.shape[0]
    for i in range(act.shape[0]):
        rows = slice(i * tall, (i + 1) * tall)
        u = nn(nm[rows, :], w_up)
        dact = nt(dd[rows, :], w_down)
        a, slope = gelu_both(u)
        shape = act.shape[1:4] + (256,)
        act[i, :, :, :, at] = a.astype(BF).reshape(shape)
        dup[i, :, :, :, at] = (slope * dact).astype(BF).reshape(shape)


def mlp_down(act, wd, down, c):
    @pl.loop(0, down.shape[1] // 256)
    def _(n):
        at = pl.ds(pl.multiple_of(n * 256, 256), 256)
        out = nn(flat(act[...]), flat(wd[c, :, :, :, :, at]))
        down[:, at] = out if c == 0 else down[:, at] + out


def mlp_dnormed(dup, wu, dnm, c):
    @pl.loop(0, 2)
    def _(i):
        half = dnm.shape[0] // 2
        rows = pl.ds(pl.multiple_of(i * half, half), half)
        out = nt(flat(dup[pl.ds(2 * i, 2)]), flat(wu[c]))
        dnm[rows, :] = out if c == 0 else dnm[rows, :] + out


def mlp_grad_down(act, dd, wd, c):
    @pl.loop(0, act.shape[-1] // 256)
    def _(n):
        at = pl.ds(pl.multiple_of(n * 256, 256), 256)
        g = tn(flat(act[:, :, :, :, at]), dd[...]).astype(BF)
        wd[c, n] = g.reshape(wd.shape[2:])


def mlp_grad_up(nmt, dup, wu, c):
    @pl.loop(0, dup.shape[-1] // 512)
    def _(n):
        at = pl.ds(pl.multiple_of(n * 512, 512), 512)
        g = nn(nmt[...], flat(dup[:, :, :, :, at])).astype(BF)
        wu[c, :, :, :, :, at] = g.reshape(wu.shape[1:5] + (512,))


def mid_backward(picked, attn_out, up, down, dnm, gains, cols, datt, new_rows, small, tile=128):
    total = picked.shape[0]
    small[...] = jnp.zeros_like(small)

    @pl.loop(0, total // tile)
    def _(i):
        rows = pl.ds(pl.multiple_of(i * tile, tile), tile)
        x = picked[rows, :].astype(F32)
        gate = cols[rows, GATE : GATE + 1]
        live = cols[rows, LIVE : LIVE + 1]
        r = cols[rows, R2 : R2 + 1]
        ao = attn_out[rows, :]
        branch = gate * ao
        hidden = x + branch
        new_rows[rows, :] = (x + live * (branch + down[rows, :])).astype(BF)
        d = dnm[rows, :]
        hr = hidden * r
        dh = d * hr
        small[1:2, :] += jnp.sum(dh, axis=0, keepdims=True)
        mean = jnp.mean(dh * gains[1:2, :], axis=1, keepdims=True)
        d_hidden = r * (gains[1:2, :] * d - hr * mean)
        dnm[rows, :] = d_hidden
        d_branch = live * up[rows, :].astype(F32) + d_hidden
        d_logit = jnp.sum(d_branch * ao, axis=1, keepdims=True) * gate * (1.0 - gate)
        cols[rows, DLOG : DLOG + 1] = d_logit
        small[2:3, :] += jnp.sum(x * d_logit, axis=0, keepdims=True)
        datt[rows, :] = (d_branch * gate).astype(BF)


def out_backward(datt, mixed, wa, dmix):
    total, width = datt.shape

    @pl.loop(0, 2)
    def _(i):
        half = total // 2
        rows = pl.ds(pl.multiple_of(i * half, half), half)
        dmix[rows, :] = nt(datt[rows, :], flat(wa[3])).astype(BF)

    wa[3] = grad_of(mixed, datt[...]).reshape(wa.shape[1:])


def grad_of(left, right):
    parts = [tn(left[:, n * 384 : n * 384 + 384], right).astype(BF) for n in range(2)]
    return jnp.concatenate(parts, axis=0)


def qkv_normed(dqkv, wa, dnorm, beat):
    total = dqkv.shape[1]

    @pl.loop(0, 4)
    def _(i):
        part = total // 4
        rows = pl.ds(pl.multiple_of(i * part, part), part)
        dnorm[rows, :] = (
            nt(dqkv[0, rows, :], flat(wa[0]))
            + nt(dqkv[1, rows, :], flat(wa[1]))
            + nt(dqkv[2, rows, :], flat(wa[2]))
        )
        beat(i)


def first_backward(picked, up, dnorm, dhid, gains, cols, new_grads, small, beat, tile=128):
    total = picked.shape[0]

    @pl.loop(0, total // tile)
    def _(i):
        rows = pl.ds(pl.multiple_of(i * tile, tile), tile)
        x = picked[rows, :].astype(F32)
        r = cols[rows, R1 : R1 + 1]
        d = dnorm[rows, :]
        xr = x * r
        dx = d * xr
        small[0:1, :] += jnp.sum(dx, axis=0, keepdims=True)
        mean = jnp.mean(dx * gains[0:1, :], axis=1, keepdims=True)
        d_first = r * (gains[0:1, :] * d - xr * mean)
        d_picked = d_first + dhid[rows, :] + cols[rows, DLOG : DLOG + 1] * gains[2:3, :]
        new_grads[rows, :] = (up[rows, :].astype(F32) + d_picked).astype(BF)
        beat(i)


MESH_ID = pl.DeviceIdType.MESH
A_MATS, CHUNKS, PLANE = 4, 3, 8


class Place:
    def __init__(self, depth):
        dp = lax.axis_index("dp")
        self.depth = depth
        self.z = lax.axis_index("fsdp")
        self.core = lax.rem(dp, 2)
        self.x = lax.rem(lax.div(dp, 2), 2)
        self.y = lax.rem(lax.div(dp, 4), 2)
        self.sib = (dp + 1 - 2 * self.core, self.z)
        self.xn = (dp + 2 - 4 * self.x, self.z)
        self.yn = (dp + 4 - 8 * self.y, self.z)
        self.dp = dp

    def ahead(self, o):
        return lax.rem(self.z + o, self.depth)

    def behind(self, o):
        return lax.rem(self.z + self.depth - o, self.depth)

    def at_z(self, z):
        return (self.dp, z)

    def greet(self):
        barrier = pltpu.get_barrier_semaphore()
        peers = [self.sib, self.xn, self.yn]
        peers += [self.at_z(self.ahead(o)) for o in range(1, self.depth)]
        for peer in peers:
            pl.semaphore_signal(barrier, inc=1, device_id=peer, device_id_type=MESH_ID)
        pl.semaphore_wait(barrier, len(peers))


def half_of(ref, core):
    width = ref.shape[-1] // 2
    return pl.ds(pl.multiple_of(core * width, 128), width)


class Gather:
    SENDS, RECVS = 2, 5
    CORE, Z, X, Y, FAR = range(5)
    ARRAYS = A_MATS + 2 * CHUNKS

    def __init__(self, me, wa, wu, wd, sends, recvs):
        self.me, self.refs, self.sends, self.recvs = me, (wa, wu, wd), sends, recvs

    def array(self, a):
        wa, wu, wd = self.refs
        if a < A_MATS:
            return wa.at[a]
        return (wd if a % 2 else wu).at[(a - A_MATS) // 2]

    def piece(self, a, zi, xi, yi, core):
        ref = self.array(a)
        return ref.at[zi, xi, yi, :, half_of(ref, core)]

    def way(self, a):
        return a % 2

    def copy(self, a, kind, ref, dev):
        send = self.sends.at[a * self.SENDS + (0 if kind == self.CORE else 1)]
        recv = self.recvs.at[a * self.RECVS + kind]
        return pltpu.make_async_remote_copy(
            src_ref=ref, dst_ref=ref, send_sem=send, recv_sem=recv, device_id=dev, device_id_type=MESH_ID
        )

    def mine(self, a, zi, flip_x=False, flip_y=False):
        m = self.me
        return self.piece(a, zi, 1 - m.x if flip_x else m.x, 1 - m.y if flip_y else m.y, m.core)

    def took(self, a, kind):
        self.copy(a, kind, self.mine(a, slice(0, self.me.depth - 1)), self.me.xn).wait_recv()

    def core_copy(self, a, core):
        ref = self.array(a)
        return self.copy(a, self.CORE, ref.at[:, :, :, :, half_of(ref, core)], self.me.sib)

    def origins(self):
        return range(1, self.me.depth)

    def send_z(self, a):
        m = self.me
        for o in self.origins():
            self.copy(a, self.Z, self.mine(a, m.z), m.at_z(m.ahead(o))).start()

    def spread(self, a):
        m = self.me
        self.took(a, self.Z)
        for o in self.origins():
            self.copy(a, self.X, self.mine(a, m.behind(o)), m.xn).start()
            self.copy(a, self.Y, self.mine(a, m.behind(o)), m.yn).start()

    def forward(self, a):
        m, by_x = self.me, self.way(a) == 0
        self.took(a, self.X if by_x else self.Y)
        for o in self.origins():
            ref = self.mine(a, m.behind(o), by_x, not by_x)
            self.copy(a, self.FAR, ref, m.yn if by_x else m.xn).start()

    def across(self, a):
        self.took(a, self.Y if self.way(a) == 0 else self.X)
        self.took(a, self.FAR)
        self.core_copy(a, self.me.core).start()

    def ready(self, a):
        self.core_copy(a, 1 - self.me.core).wait_recv()

    def settle(self, a):
        m, ref = self.me, self.array(a)
        self.core_copy(a, m.core).wait_send()
        sent = ref.at[0 : m.depth - 1, :, :, :, half_of(ref, m.core)]
        self.copy(a, self.Z, sent, m.xn).wait_send()


class Owned:
    def __init__(self, me, shards, wa, wu, wd, sems):
        wq, wk, wv, wo, up, down = shards
        z, core = me.z, me.core
        half = half_of(wa, core)
        self.copies = {a: [] for a in range(Gather.ARRAYS)}
        for m, w in enumerate((wq, wk, wv, wo)):
            self.copies[m].append((w.at[:, :, :, half], wa.at[m, z, :, :, :, half]))
        ff_own = up.shape[-1] // me.depth
        for c in range(CHUNKS):
            for j in range(2):
                block = 2 * core + j
                src = up.at[:, :, :, pl.ds(pl.multiple_of(block * ff_own + c * 256, 128), 256)]
                dst = wu.at[c, z, :, :, :, pl.ds(pl.multiple_of(block * 256, 128), 256)]
                self.copies[A_MATS + 2 * c].append((src, dst))
            self.copies[A_MATS + 1 + 2 * c].append((down.at[c, :, :, :, half], wd.at[c, z, :, :, :, half]))
        self.sems = sems

    def all_of(self, a):
        for i, (src, dst) in enumerate(self.copies[a]):
            yield pltpu.make_async_copy(src, dst, self.sems.at[2 * a + i])

    def start(self, a):
        for c in self.all_of(a):
            c.start()

    def wait(self, a):
        for c in self.all_of(a):
            c.wait()


class Reduce:
    SENDS, RECVS = 2, 7
    CORE, FIRST, SECOND, Z, BACK, FAR, LAST = range(7)

    def __init__(
        self, me, w, from_core, from_x, from_y, then_x, then_y, from_z, sends, recvs, frees, at, way
    ):
        self.me, self.w, self.way, self.free, base = me, w, way, frees.at[at], at
        self.from_core, self.from_x, self.from_y = from_core, from_x, from_y
        self.then_x, self.then_y, self.from_z = then_x, then_y, from_z
        self.sends, self.recvs, self.base = sends, recvs, base
        self.mine, self.theirs = half_of(w, me.core), half_of(w, 1 - me.core)

    def copy(self, kind, src, dst, dev):
        small = kind in (self.Z, self.BACK, self.FAR)
        send = self.sends.at[self.base * self.SENDS + small]
        recv = self.recvs.at[self.base * self.RECVS + kind]
        return pltpu.make_async_remote_copy(
            src_ref=src, dst_ref=dst, send_sem=send, recv_sem=recv, device_id=dev, device_id_type=MESH_ID
        )

    def took(self, kind, ref):
        self.copy(kind, ref, ref, self.me.sib).wait_recv()

    def sent(self, kind, ref):
        self.copy(kind, ref, ref, self.me.sib).wait_send()

    def z_copy(self, o):
        m = self.me
        src = self.w.at[m.ahead(o), m.x, m.y, :, self.mine]
        return self.copy(self.Z, src, self.from_z.at[o - 1], m.at_z(m.ahead(o)))

    def back(self, kind, xi, yi, dev):
        ref = self.from_core.at[0, xi, yi]
        return self.copy(kind, ref, ref, dev)

    def add(self, at, arrived):
        self.w[at] = self.w[at] + arrived

    def t1(self):
        self.copy(self.CORE, self.w.at[:, :, :, :, self.theirs], self.from_core, self.me.sib).start()

    def t2(self):
        m, w = self.me, self.w
        self.took(self.CORE, self.from_core)

        @pl.loop(0, 2 * m.depth)
        def _(i):
            zi, xi = lax.div(i, 2), lax.rem(i, 2)
            self.add((zi, xi, slice(None), slice(None), self.mine), self.from_core[zi, xi])

        pl.semaphore_signal(self.free, inc=1, device_id=m.sib, device_id_type=MESH_ID)
        self.copy(self.FIRST, w.at[0:2, 1 - m.x, :, :, self.mine], self.from_x, m.xn).start()
        self.copy(self.FIRST, w.at[2:4, :, 1 - m.y, :, self.mine], self.from_y, m.yn).start()

    def t3(self):
        m, w = self.me, self.w
        self.took(self.FIRST, w.at[0:2, :, :, :, self.mine])

        @pl.loop(0, 2)
        def _(zi):
            self.add((zi, m.x, slice(None), slice(None), self.mine), self.from_x[zi])
            self.add((2 + zi, slice(None), m.y, slice(None), self.mine), self.from_y[zi])

        self.copy(self.SECOND, w.at[0:2, m.x, 1 - m.y, :, self.mine], self.then_y, m.yn).start()
        self.copy(self.SECOND, w.at[2:4, 1 - m.x, m.y, :, self.mine], self.then_x, m.xn).start()

    def t4(self):
        m = self.me
        self.took(self.SECOND, self.w.at[0:2, 0:2, 0, :, self.mine])
        self.add((slice(0, 2), m.x, m.y, slice(None), self.mine), self.then_y[...])
        self.add((slice(2, 4), m.x, m.y, slice(None), self.mine), self.then_x[...])
        for o in range(1, m.depth):
            self.z_copy(o).start()

    def t5(self):
        m = self.me
        total = self.w[m.z, m.x, m.y, :, self.mine].astype(F32)
        self.took(self.Z, self.from_z)
        for o in range(1, m.depth):
            total = total + self.from_z[o - 1].astype(F32)
        self.from_core[0, m.x, m.y] = total.astype(BF)
        self.back(self.BACK, m.x, m.y, m.xn).start()
        self.back(self.BACK, m.x, m.y, m.yn).start()

    def t6(self):
        m = self.me
        self.took(self.BACK, self.from_core.at[0, 0:2, 0])
        if self.way == 0:
            self.back(self.FAR, 1 - m.x, m.y, m.yn).start()
        else:
            self.back(self.FAR, m.x, 1 - m.y, m.xn).start()

    def t7(self):
        m = self.me
        self.took(self.FAR, self.from_core.at[0, 0, 0])
        pl.semaphore_wait(self.free, 1)
        self.copy(self.LAST, self.from_core.at[0], self.from_core.at[1], m.sib).start()

    def t8(self):
        m = self.me
        self.took(self.LAST, self.from_core.at[1])
        self.sent(self.CORE, self.w)
        self.sent(self.Z, self.w.at[0 : m.depth - 1, 0:2, 0, :, self.mine])


class SmallSum:
    def __init__(self, me, small, inbox, sends, recvs, base):
        self.me, self.small, self.inbox = me, small, inbox
        self.sends, self.recvs, self.base = sends, recvs, base

    def copy(self, k, src, dst, dev):
        return pltpu.make_async_remote_copy(
            src_ref=src, dst_ref=dst, send_sem=self.sends.at[self.base[0]], recv_sem=self.recvs.at[self.base[1] + k],
            device_id=dev, device_id_type=MESH_ID,
        )

    def peer(self, k):
        return (self.me.sib, self.me.xn, self.me.yn)[k]

    def step(self, k):
        m, small, inbox = self.me, self.small, self.inbox
        if 1 <= k <= 3:
            self.copy(k - 1, small.at[0], inbox.at[k - 1], m.sib).wait_recv()
            small[k] = small[k - 1] + inbox[k - 1]
        if k <= 2:
            self.copy(k, small.at[k], inbox.at[k], self.peer(k)).start()
        if k == 3:
            for o in range(1, m.depth):
                self.copy(3, small.at[3], inbox.at[2 + o], m.at_z(m.ahead(o))).start()
        if k == 4:
            self.copy(3, inbox.at[3:], inbox.at[3:], m.sib).wait_recv()
            total = small[3]
            for o in range(1, m.depth):
                total = total + inbox[2 + o]
            small[4] = total
            self.copy(3, inbox, inbox, m.sib).wait_send()


def chunk_boxes(rows_a, width, rows_d, ff_c):
    def boxes(n, rows, cols, first):
        def box(*lead):
            return pltpu.VMEM((n,) + lead + (rows, cols), BF)

        return ([box(4, 2, 2)] if first else []) + [box(2, 2), box(2, 2), box(2), box(2), box(3)]

    return (
        boxes(CHUNKS, rows_a, ff_c // 2, True)
        + boxes(CHUNKS, rows_d, width // 2, True)
        + boxes(A_MATS, rows_a, width // 2, False)
    )


def block_kernel(
    depth, tokens, cot, idx, valid, wq, wk, wv, wo, up_in, down_in, gain1, gain2, gain3,
    new_rows, new_grads, fa, fu, fd, small_out,
    wa, wu, wd, picked, up, cols, na, nmt, dd, qkv, probs, mixed, attn_out, act, dup, down, dnm,
    gains, gpad, gbox, small, inbox,
    tok_sem, own_sem, out_sem, ag_send, ag_recv, rs_send, rs_recv, frees, opened, *boxes,
):
    seqs, slots = idx.shape
    width = picked.shape[1]
    scale = (width // HEADS) ** -0.5
    rows_a = wa.shape[-2]
    half = width // 2
    me = Place(depth)
    me.greet()
    own = Owned(me, (wq, wk, wv, wo, up_in, down_in), wa, wu, wd, own_sem)
    ag = Gather(me, wa, wu, wd, ag_send, ag_recv)
    sem_at = (20, 70)
    others = range(1, depth)

    def gain_copy(o):
        return pltpu.make_async_remote_copy(
            src_ref=gpad, dst_ref=gbox.at[o - 1], send_sem=rs_send.at[21], recv_sem=rs_recv.at[74],
            device_id=me.at_z(me.ahead(o)), device_id_type=MESH_ID,
        )

    own.start(0)
    own.start(1)
    picker = Picker(tokens, cot, picked, up, cols, (act, dup), tok_sem)
    picker.start(0)
    for a in range(2, Gather.ARRAYS):
        own.start(a)
    own.wait(0)
    ag.send_z(0)
    picker.turn(idx, valid)
    own.wait(1)
    ag.send_z(1)
    owned = gain1.shape[0]
    spot = lax.broadcasted_iota(jnp.int32, (owned, width), 1) - lax.broadcasted_iota(jnp.int32, (owned, width), 0)
    spot = jnp.where(spot == me.z * owned, 1.0, 0.0).astype(BF)
    gpad[...] = jnp.zeros_like(gpad)
    for i, g in enumerate((gain1, gain2, gain3)):
        gpad[i : i + 1, :] = nn(g[...].astype(F32).reshape(1, owned).astype(BF), spot)
    for o in others:
        gain_copy(o).start()
    picker.pick(0, slots, True)
    for a in range(2, Gather.ARRAYS):
        own.wait(a)
    ag.send_z(2)
    ag.spread(0)
    picker.pick(1, slots, True)
    ag.send_z(3)
    picker.pick(2, slots, True)
    ag.send_z(4)
    ag.forward(0)
    ag.spread(1)
    picker.pick(3, slots, False)
    pltpu.make_async_remote_copy(
        src_ref=gbox, dst_ref=gbox, send_sem=rs_send.at[21], recv_sem=rs_recv.at[74],
        device_id=me.sib, device_id_type=MESH_ID,
    ).wait()
    total = gpad[...]
    for o in others:
        total = total + gbox[o - 1]
    gains[...] = total
    norm_phase(picked, gains, cols, na)
    ag.across(0)
    ag.send_z(5)
    ag.forward(1)
    ag.spread(2)
    ag.ready(0)
    qkv_one(na, wa, qkv, scale, 0)
    ag.across(1)
    ag.send_z(6)
    ag.forward(2)
    ag.ready(1)
    qkv_one(na, wa, qkv, scale, 1)
    ag.across(2)
    ag.spread(3)
    ag.ready(2)
    qkv_one(na, wa, qkv, scale, 2)
    ag.forward(3)
    ag.spread(4)
    ag.send_z(7)

    @pl.loop(0, seqs)
    def _(s):
        attention_forward(idx, valid, cols, qkv, probs, mixed, s)

        @pl.when(s == 0)
        def _():
            ag.across(3)
            ag.spread(5)

        @pl.when(s == 1)
        def _():
            ag.forward(4)
            ag.send_z(8)
            ag.send_z(9)

        @pl.when(s == 2)
        def _():
            ag.forward(5)
            ag.across(4)

        @pl.when(s == 3)
        def _():
            ag.spread(6)

    ag.ready(3)
    out_phase(mixed, wa, attn_out)
    ag.across(5)
    mid_norm(picked, attn_out, up, gains, cols, na, nmt, dd)
    ag.forward(6)
    ag.spread(7)

    ubox, dbox, abox = boxes[0:6], boxes[6:12], boxes[12:17]
    reducers = {}

    def reducer(name, at, w, core_box, rest, i, way):
        reducers[name] = Reduce(me, w, core_box, *[x.at[i] for x in rest], rs_send, rs_recv, frees, at, way)

    for c in range(CHUNKS):
        reducer("u%d" % c, c, wu.at[c], ubox[0].at[c], ubox[1:], c, 0)
        reducer("d%d" % c, 3 + c, wd.at[c], dbox[0].at[c], dbox[1:], c, 1)
    spots = ((act, 0), (act, half), (dup, 0), (dup, half))
    terms = [probs.at[m, :, :, :, 0:rows_a, 0:width] for m in range(3)] + [wa.at[3]]
    for m, name in enumerate("qkvo"):
        ref, lane = spots[m]
        box = ref.at[:, :, :, 0:rows_a, lane : lane + half]
        reducer(name, 6 + m, terms[m], box, abox, m, m % 2)
    finals = {"q": (fa, 0), "k": (fa, 1), "v": (fa, 2), "o": (fa, 3)}
    for c in range(CHUNKS):
        finals["u%d" % c] = (fu, c)
        finals["d%d" % c] = (fd, c)
    order = list(finals)

    def result_copies(name):
        dst, i = finals[name]
        box = reducers[name].from_core
        for h, core in ((0, me.core), (1, 1 - me.core)):
            yield pltpu.make_async_copy(box.at[h], dst.at[i, :, :, :, half_of(dst, core)], out_sem.at[{"u": 1, "d": 2}.get(name[0], 0)])

    def step(k, *names):
        for name in names:
            getattr(reducers[name], "t%d" % k)()
            if k == 8:
                for c in result_copies(name):
                    c.start()

    for c in range(CHUNKS):
        for a in (A_MATS + 2 * c, A_MATS + 1 + 2 * c):
            ag.ready(a)

        @pl.loop(0, 4)
        def _(n):
            mlp_up(na, dd, wu, wd, act, dup, c, n)
            if c > 0:

                @pl.when(n == 1)
                def _():
                    step(2, "d%d" % (c - 1), "u%d" % (c - 1))

        if c == 0:
            ag.across(6)
            ag.spread(8)
            ag.forward(7)
        if c == 1:
            ag.across(9)
        mlp_down(act, wd, down, c)
        mlp_dnormed(dup, wu, dnm, c)
        if c == 0:
            ag.across(7)
            ag.spread(9)
        if c == 2:
            step(4, "d0", "u0")
        ag.settle(A_MATS + 2 * c)
        ag.settle(A_MATS + 1 + 2 * c)
        mlp_grad_down(act, dd, wd, c)
        step(1, "d%d" % c)
        if c == 0:
            ag.forward(8)
        mlp_grad_up(nmt, dup, wu, c)
        if c == 0:
            ag.across(8)
            ag.forward(9)
        step(1, "u%d" % c)
        if c > 0:
            step(3, "d%d" % (c - 1), "u%d" % (c - 1))
    pl.semaphore_signal(opened, inc=1, device_id=me.sib, device_id_type=MESH_ID)
    for a in range(A_MATS):
        ag.settle(a)
    datt, dmix = na, dd
    mid_backward(picked, attn_out, up, down, dnm, gains, cols, datt, dd, small.at[0])
    rows_out = pltpu.make_async_copy(dd, new_rows, tok_sem.at[0])
    rows_out.start()
    step(2, "d2", "u2")
    rows_out.wait()
    out_backward(datt, mixed, wa, dmix)
    pl.semaphore_wait(opened, 1)
    step(1, "o")
    step(4, "d1", "u1")
    step(5, "d0", "u0")
    norm_again(picked, gains, cols, na)

    @pl.loop(0, seqs)
    def _(s):
        attention_backward(qkv, probs, mixed, dmix, s, slots, scale)

        @pl.when(s == 0)
        def _():
            step(2, "o")
            step(6, "d0", "u0")

        @pl.when(s == 1)
        def _():
            step(7, "d0", "u0")

        @pl.when(s == 2)
        def _():
            step(3, "d2", "u2")
            step(8, "d0", "u0")

        @pl.when(s == 3)
        def _():
            step(3, "o")

    for m, name in enumerate("qkv"):
        terms[m][...] = grad_of(na, qkv[m]).reshape(wa.shape[1:])
        step(1, name)
        if m == 0:
            step(5, "d1", "u1")
        if m > 0:
            step(2, "qkv"[m - 1])
    step(4, "d2", "u2")

    def at_beats(*todo):
        def beat(i):
            for k, work in todo:

                @pl.when(i == k)
                def _():
                    for t, *names in work:
                        step(t, *names)

        return beat

    qkv_normed(
        qkv, wa, down, at_beats((0, [(2, "v")]), (1, [(4, "o")]), (2, [(3, "q")]), (3, [(6, "d1", "u1"), (3, "k")]))
    )
    first_backward(
        picked, up, down, dnm, gains, cols, dd, small.at[0],
        at_beats((2, [(7, "d1", "u1")]), (4, [(3, "v"), (4, "q")])),
    )
    grads_out = pltpu.make_async_copy(dd, new_grads, tok_sem.at[1])
    grads_out.start()
    sums = SmallSum(me, small, inbox, rs_send, rs_recv, sem_at)
    sums.step(0)
    step(4, "k")
    step(4, "v")
    sums.step(1)
    step(5, "d2", "u2")
    step(5, "o")
    sums.step(2)
    step(5, "q")
    step(5, "k")
    sums.step(3)
    step(5, "v")
    step(6, "d2", "u2", "o")
    step(6, "q")
    step(6, "k")
    sums.step(4)
    step(6, "v")
    step(7, "d2", "u2", "o")
    step(7, "q", "k", "v")
    step(8, "d1", "u1", "d2", "u2", "o", "q", "k", "v")
    small_out[...] = small[4]
    for i, dst in enumerate((fa, fu, fd)):
        pltpu.make_async_copy(dst, dst, out_sem.at[i]).wait()
    grads_out.wait()


def place_kernel(depth, idx, tokens, cot, new_rows, new_grads, fa, fu, fd, sums,
                 out, grad, gq, gk, gv, go, gup, gdown, g1, g2, g3):
    s = pl.program_id(0)
    length, slots = tokens.shape[0], idx.shape[1]
    spot = lax.broadcasted_iota(jnp.int32, (length, slots), 0)
    hot = jnp.where(spot == idx[pl.ds(s, 1), :], 1.0, 0.0)
    hit = jnp.sum(hot, axis=1, keepdims=True) > 0
    hot = hot.astype(BF)
    for src, rows, dst in ((tokens, new_rows, out), (cot, new_grads, grad)):
        dst[...] = jnp.where(hit, nn(hot, rows[...]), src[...].astype(F32)).astype(BF)
    place_weights(fa, fu, fd, gq, gk, gv, go, gup, gdown)
    own = g1.shape[0]
    for k in range(depth):

        @pl.when((s == 0) & (lax.axis_index("fsdp") == k))
        def _():
            for i, g in enumerate((g1, g2, g3)):
                g[...] = sums[i, k * own : (k + 1) * own]


def place_weights(fa, fu, fd, gq, gk, gv, go, gup, gdown):
    for m, g in enumerate((gq, gk, gv, go)):
        g[...] = fa[m, 0].astype(F32)
    quarter = 256
    ff_own = gup.shape[1] // 4
    for c in range(CHUNKS):
        for j in range(4):
            gup[:, j * ff_own + c * quarter : j * ff_own + (c + 1) * quarter] = fu[c, 0, :, j * quarter : (j + 1) * quarter].astype(F32)
        gdown[c, 0] = fd[c, 0].astype(F32)


def remote_params(collective_id, limit=60):
    return pltpu.CompilerParams(
        collective_id=collective_id, has_side_effects=True, vmem_limit_bytes=limit * 2**20
    )


def over_groups(groups, terms):
    if groups == 1:
        return terms
    dp = groups * PLANE
    total = [t.astype(F32) for t in terms]
    for k in range(groups.bit_length() - 1):
        hop = PLANE << k
        pairs = [(i, i ^ hop) for i in range(dp)]
        total = [t + lax.ppermute(t, "dp", pairs) for t in total]
    return total


def body(depth, groups, tokens, row_index, row_valid, w_query, w_key, w_value, w_out, w_up, w_down,
         gain_attn, gain_mlp, w_router, cotangent):
    seqs, slots = row_index.shape
    width = tokens.shape[1]
    own = w_query.shape[0]
    ff = w_up.shape[1]
    length = tokens.shape[0] // seqs
    total = seqs * slots
    rq, cw = own // 4, ff // CHUNKS
    dq = w_down.shape[0] // (4 * CHUNKS)
    sd = jax.ShapeDtypeStruct
    hbm, vm = pl.BlockSpec(memory_space=pl.ANY), pl.BlockSpec(memory_space=pltpu.VMEM)
    sem = pltpu.SemaphoreType.DMA
    vmem = pltpu.VMEM
    gains3 = (gain_attn, gain_mlp, w_router)
    squares = [w.reshape(2, 2, rq, width) for w in (w_query, w_key, w_value, w_out)]
    sa, su, sdn = (A_MATS, depth, 2, 2, rq, width), (CHUNKS, depth, 2, 2, rq, cw), (CHUNKS, depth, 2, 2, dq, width)
    narr = Gather.ARRAYS
    rows = (total, width)
    work = (4, 2, 2, total // 16, cw)
    regular = pltpu.SemaphoreType.REGULAR
    blocks = (seqs, 4, 2, 2, length // 16, width)
    new_rows, new_grads, fa, fu, fd, sums = pl.pallas_call(
        functools.partial(block_kernel, depth),
        out_shape=(
            sd(rows, BF), sd(rows, BF), sd(sa[:1] + sa[2:], BF), sd(su[:1] + su[2:], BF), sd(sdn[:1] + sdn[2:], BF),
            sd((8, width), F32),
        ),
        in_specs=[hbm, hbm, vm, vm] + [hbm] * 6 + [vm] * 3,
        out_specs=(hbm,) * 5 + (vm,),
        scratch_shapes=[
            vmem(sa, BF), vmem(su, BF), vmem(sdn, BF), vmem(rows, BF), vmem(rows, BF), vmem((total, 128), F32),
            vmem(rows, BF), vmem((width, total), BF), vmem(rows, BF), vmem((3,) + rows, BF), vmem((3,) + work, BF),
            vmem(rows, BF), vmem(rows, F32), vmem(work, BF), vmem(work, BF), vmem(rows, F32), vmem(rows, F32),
            vmem((8, width), F32), vmem((8, width), F32), vmem((depth - 1, 8, width), F32), vmem((5, 8, width), F32), vmem((2 + depth, 8, width), F32),
            sem((2,)), sem((2 * narr,)), sem((3,)), sem((2 * narr,)), sem((5 * narr,)),
            sem((2 * narr + 2,)), sem((7 * narr + 5,)), regular((narr,)), regular,
        ]
        + chunk_boxes(rq, width, dq, cw),
        compiler_params=remote_params(0, 63),
    )(
        tokens.reshape(blocks), cotangent.reshape(blocks), row_index, row_valid, *squares,
        w_up.reshape(2, 2, rq, ff), w_down.reshape(CHUNKS, 2, 2, dq, width), *gains3,
    )
    fa, fu, fd, sums = over_groups(groups, (fa, fu, fd, sums))

    def by_seq(*shape):
        return pl.BlockSpec(shape, lambda i: (i,) + (0,) * (len(shape) - 1))

    def by_quarter(*shape):
        return pl.BlockSpec(shape, lambda i: (0, i) + (0,) * (len(shape) - 2))

    out, grad, gq, gk, gv, go, gup, gdown, g1, g2, g3 = pl.pallas_call(
        functools.partial(place_kernel, depth),
        grid=(seqs,),
        out_shape=(sd(tokens.shape, BF),) * 2
        + (sd((own, width), F32),) * 4
        + (sd((own, ff), F32), sd((CHUNKS, 4, dq, width), F32))
        + (sd((own,), F32),) * 3,
        in_specs=[pl.BlockSpec((seqs, slots), lambda i: (0, 0))]
        + [by_seq(length, width)] * 2
        + [by_seq(slots, width)] * 2
        + [by_quarter(A_MATS, 1, rq, width), by_quarter(CHUNKS, 1, rq, cw), by_quarter(CHUNKS, 1, dq, width)]
        + [pl.BlockSpec((8, width), lambda i: (0, 0))],
        out_specs=[by_seq(length, width)] * 2
        + [by_seq(rq, width)] * 4
        + [by_seq(rq, ff), by_quarter(CHUNKS, 1, dq, width)]
        + [pl.BlockSpec((own,), lambda i: (0,))] * 3,
        compiler_params=pltpu.CompilerParams(vmem_limit_bytes=62 * 2**20),
    )(
        row_index, tokens, cotangent, new_rows, new_grads, fa.reshape(A_MATS, 4, rq, width),
        fu.reshape(CHUNKS, 4, rq, cw), fd.reshape(CHUNKS, 4, dq, width), sums,
    )
    return (out, grad, gq, gk, gv, go, gup, gdown.reshape(w_down.shape), g1, g2, g3)


def solution(mesh):
    depth = mesh.shape["fsdp"]
    both = P(("dp", "fsdp"), None)
    weight, vector = P("fsdp", None), P("fsdp")
    return jax.shard_map(
        functools.partial(body, depth, mesh.shape["dp"] // PLANE),
        mesh=mesh,
        in_specs=(both,) * 3 + (weight,) * 6 + (vector,) * 3 + (both,),
        out_specs=(both, both) + (weight,) * 6 + (vector,) * 3,
        check_vma=False,
    )
```

```python
import functools

import jax
import jax.numpy as jnp
from jax import lax
from jax.experimental import pallas as pl
from jax.experimental.pallas import tpu as pltpu

from jax.sharding import PartitionSpec as P

HEADS = 12
EPS = 1e-06
NEG = -1e30
BF = jnp.bfloat16
F32 = jnp.float32
GATE, R1, R2, LIVE, DLOG, POS = range(6)


def nn(a, b):
    return lax.dot_general(a, b, (((1,), (0,)), ((), ())), preferred_element_type=F32)


def nt(a, b):
    return lax.dot_general(a, b, (((1,), (1,)), ((), ())), preferred_element_type=F32)


def tn(a, b):
    return lax.dot_general(a, b, (((0,), (0,)), ((), ())), preferred_element_type=F32)


def flat(v):
    return v.reshape(-1, v.shape[-1])


class Picker:
    def __init__(self, tokens, cot, picked, up, cols, bufs, sems):
        self.srcs, self.dsts, self.cols, self.bufs, self.sems = (tokens, cot), (picked, up), cols, bufs, sems

    def fetch(self, s, b):
        width = self.srcs[b].shape[-1]
        dst = self.bufs[b].at[:, :, :, :, 0:width]
        return pltpu.make_async_copy(self.srcs[b].at[s], dst, self.sems.at[b])

    def start(self, s):
        for b in range(2):
            self.fetch(s, b).start()

    def turn(self, idx, valid):
        seqs, slots = idx.shape
        for what, k in ((idx, POS), (valid, LIVE)):
            rows8 = what[...].astype(F32)
            if seqs < 8:
                rows8 = jnp.concatenate([rows8, jnp.zeros((8 - seqs, slots), F32)], axis=0)
            turned = rows8.T
            for s in range(seqs):
                self.cols[s * slots : (s + 1) * slots, k : k + 1] = turned[:, s : s + 1]

    def pick(self, s, slots, more):
        width = self.srcs[0].shape[-1]
        rows = slice(s * slots, (s + 1) * slots)
        length = self.bufs[0].shape[0] * self.bufs[0].shape[1] * self.bufs[0].shape[2] * self.bufs[0].shape[3]
        lane = lax.broadcasted_iota(jnp.int32, (slots, length), 1).astype(F32)
        hot = jnp.where(lane == self.cols[rows, POS : POS + 1], 1.0, 0.0).astype(BF)
        for b in range(2):
            self.fetch(s, b).wait()
            self.dsts[b][rows, :] = nn(hot, flat(self.bufs[b][:, :, :, :, 0:width])).astype(BF)
            if more:
                self.fetch(s + 1, b).start()


def norm_phase(picked, gains, cols, na, tile=256):
    total = picked.shape[0]

    @pl.loop(0, total // tile)
    def _(i):
        rows = pl.ds(pl.multiple_of(i * tile, tile), tile)
        x = picked[rows, :].astype(F32)
        cols[rows, GATE : GATE + 1] = jax.nn.sigmoid(
            jnp.sum(x * gains[2:3, :], axis=1, keepdims=True)
        )
        r1 = lax.rsqrt(jnp.mean(x * x, axis=1, keepdims=True) + EPS)
        cols[rows, R1 : R1 + 1] = r1
        na[rows, :] = (x * r1 * gains[0:1, :]).astype(BF)


def norm_again(picked, gains, cols, na, tile=256):
    @pl.loop(0, picked.shape[0] // tile)
    def _(i):
        rows = pl.ds(pl.multiple_of(i * tile, tile), tile)
        x = picked[rows, :].astype(F32)
        na[rows, :] = (x * cols[rows, R1 : R1 + 1] * gains[0:1, :]).astype(BF)


def qkv_one(na, wa, qkv, scale, m):
    @pl.loop(0, na.shape[1] // 256)
    def _(n):
        at = pl.ds(pl.multiple_of(n * 256, 256), 256)
        out = nn(na[...], flat(wa[m, :, :, :, :, at]))
        if m == 0:
            out = out * scale
        qkv[m, :, at] = out.astype(BF)


def two_heads(v2, low_half):
    zero = jnp.zeros_like(v2)
    return jnp.concatenate([jnp.where(low_half, v2, zero), jnp.where(low_half, zero, v2)], axis=0)


def prob_spot(s, p, slots):
    at = pl.ds(pl.multiple_of(s * slots, slots), slots)
    return (p // 2, slice(2 * (p % 2), 2 * (p % 2) + 2), slice(None), slice(None), slice(None), at)


def attention_forward(idx, valid, cols, qkv, probs, mixed, s):
    slots = idx.shape[1]
    width = mixed.shape[1]
    rows = pl.ds(pl.multiple_of(s * slots, slots), slots)
    low_half = lax.broadcasted_iota(jnp.int32, (slots, 128), 1) < 64
    mine = cols[rows, POS : POS + 1]
    other = idx[pl.ds(s, 1), :].astype(F32)
    seen = ((other < mine) & (valid[pl.ds(s, 1), :] > 0)) | (other == mine)
    bias = jnp.where(seen, 0.0, NEG)
    bias = jnp.concatenate([bias, bias], axis=0)
    for p in range(width // 128):
        at = slice(p * 128, p * 128 + 128)
        q2 = two_heads(qkv[0, rows, at], low_half)
        scores = nt(q2, qkv[1, rows, at]) + bias
        e = jnp.exp(scores - jnp.max(scores, axis=1, keepdims=True))
        pr = (e * (1.0 / jnp.sum(e, axis=1, keepdims=True))).astype(BF)
        spot = prob_spot(s, p, slots)
        probs[spot] = pr.reshape(2, 2, 2, 64, slots)
        o = nn(pr, qkv[2, rows, at])
        mixed[rows, at] = jnp.where(low_half, o[:slots], o[slots:]).astype(BF)


def attention_backward(qkv, probs, mixed, dmix, s, slots, scale):
    width = mixed.shape[1]
    rows = pl.ds(pl.multiple_of(s * slots, slots), slots)
    low_half = lax.broadcasted_iota(jnp.int32, (slots, 128), 1) < 64
    for p in range(width // 128):
        at = slice(p * 128, p * 128 + 128)
        do2 = two_heads(dmix[rows, at], low_half)
        o2 = mixed[rows, at].astype(F32)
        o2 = jnp.concatenate([o2, o2], axis=0)
        delta = jnp.sum(do2.astype(F32) * o2, axis=1, keepdims=True)
        k2 = qkv[1, rows, at]
        dp = nt(do2, qkv[2, rows, at])
        pr = flat(probs[prob_spot(s, p, slots)])
        ds = (pr.astype(F32) * (dp - delta)).astype(BF)
        q2 = two_heads(qkv[0, rows, at], low_half)
        dq = nn(ds, k2) * scale
        qkv[0, rows, at] = jnp.where(low_half, dq[:slots], dq[slots:]).astype(BF)
        qkv[1, rows, at] = tn(ds, q2).astype(BF)
        qkv[2, rows, at] = tn(pr, do2).astype(BF)


def out_phase(mixed, wa, attn_out):
    width = mixed.shape[1]

    @pl.loop(0, width // 256)
    def _(n):
        at = pl.ds(pl.multiple_of(n * 256, 256), 256)
        attn_out[:, at] = nn(mixed[...], flat(wa[3, :, :, :, :, at]))


def mid_norm(picked, attn_out, up, gains, cols, nm, nmt, dd, tile=256):
    total = picked.shape[0]
    for i in range(total // tile):
        rows = slice(i * tile, (i + 1) * tile)
        hidden = picked[rows, :].astype(F32) + cols[rows, GATE : GATE + 1] * attn_out[rows, :]
        r2 = lax.rsqrt(jnp.mean(hidden * hidden, axis=1, keepdims=True) + EPS)
        cols[rows, R2 : R2 + 1] = r2
        normed = (hidden * r2 * gains[1:2, :]).astype(BF)
        nm[rows, :] = normed
        nmt[:, rows] = normed.T
        dd[rows, :] = (up[rows, :].astype(F32) * cols[rows, LIVE : LIVE + 1]).astype(BF)


def gelu_both(u):
    k = 0.7978845608028654
    u2 = u * u
    t = jnp.tanh(u * (k + (k * 0.044715) * u2))
    half = 0.5 + 0.5 * t
    act = u * half
    slope = half + act * (1.0 - t) * (k + (3 * k * 0.044715) * u2)
    return act, slope


def mlp_up(nm, dd, wu, wd, act, dup, c, n):
    at = pl.ds(pl.multiple_of(n * 256, 256), 256)
    w_up, w_down = flat(wu[c, :, :, :, :, at]), flat(wd[c, n])
    tall = nm.shape[0] // act.shape[0]
    for i in range(act.shape[0]):
        rows = slice(i * tall, (i + 1) * tall)
        u = nn(nm[rows, :], w_up)
        dact = nt(dd[rows, :], w_down)
        a, slope = gelu_both(u)
        shape = act.shape[1:4] + (256,)
        act[i, :, :, :, at] = a.astype(BF).reshape(shape)
        dup[i, :, :, :, at] = (slope * dact).astype(BF).reshape(shape)


def mlp_down(act, wd, down, c):
    @pl.loop(0, down.shape[1] // 256)
    def _(n):
        at = pl.ds(pl.multiple_of(n * 256, 256), 256)
        out = nn(flat(act[...]), flat(wd[c, :, :, :, :, at]))
        down[:, at] = out if c == 0 else down[:, at] + out


def mlp_dnormed(dup, wu, dnm, c):
    @pl.loop(0, 2)
    def _(i):
        half = dnm.shape[0] // 2
        rows = pl.ds(pl.multiple_of(i * half, half), half)
        out = nt(flat(dup[pl.ds(2 * i, 2)]), flat(wu[c]))
        dnm[rows, :] = out if c == 0 else dnm[rows, :] + out


def mlp_grad_down(act, dd, wd, c):
    @pl.loop(0, act.shape[-1] // 512)
    def _(n):
        at = pl.ds(pl.multiple_of(n * 512, 512), 512)
        g = tn(flat(act[:, :, :, :, at]), dd[...]).astype(BF)
        wd[c, pl.ds(2 * n, 2)] = g.reshape((2,) + wd.shape[2:])


def mlp_grad_up(nmt, dup, wu, c):
    @pl.loop(0, dup.shape[-1] // 512)
    def _(n):
        at = pl.ds(pl.multiple_of(n * 512, 512), 512)
        g = nn(nmt[...], flat(dup[:, :, :, :, at])).astype(BF)
        wu[c, :, :, :, :, at] = g.reshape(wu.shape[1:5] + (512,))


def mid_backward(picked, attn_out, up, down, dnm, gains, cols, datt, new_rows, small, tile=128):
    total = picked.shape[0]
    small[...] = jnp.zeros_like(small)

    @pl.loop(0, total // tile)
    def _(i):
        rows = pl.ds(pl.multiple_of(i * tile, tile), tile)
        x = picked[rows, :].astype(F32)
        gate = cols[rows, GATE : GATE + 1]
        live = cols[rows, LIVE : LIVE + 1]
        r = cols[rows, R2 : R2 + 1]
        ao = attn_out[rows, :]
        branch = gate * ao
        hidden = x + branch
        new_rows[rows, :] = (x + live * (branch + down[rows, :])).astype(BF)
        d = dnm[rows, :]
        hr = hidden * r
        dh = d * hr
        small[1:2, :] += jnp.sum(dh, axis=0, keepdims=True)
        mean = jnp.mean(dh * gains[1:2, :], axis=1, keepdims=True)
        d_hidden = r * (gains[1:2, :] * d - hr * mean)
        dnm[rows, :] = d_hidden
        d_branch = live * up[rows, :].astype(F32) + d_hidden
        d_logit = jnp.sum(d_branch * ao, axis=1, keepdims=True) * gate * (1.0 - gate)
        cols[rows, DLOG : DLOG + 1] = d_logit
        small[2:3, :] += jnp.sum(x * d_logit, axis=0, keepdims=True)
        datt[rows, :] = (d_branch * gate).astype(BF)


def out_backward(datt, mixed, wa, dmix):
    total, width = datt.shape

    @pl.loop(0, 2)
    def _(i):
        half = total // 2
        rows = pl.ds(pl.multiple_of(i * half, half), half)
        dmix[rows, :] = nt(datt[rows, :], flat(wa[3])).astype(BF)

    wa[3] = grad_of(mixed, datt[...]).reshape(wa.shape[1:])


def grad_of(left, right):
    parts = [tn(left[:, n * 384 : n * 384 + 384], right).astype(BF) for n in range(2)]
    return jnp.concatenate(parts, axis=0)


def qkv_normed(dqkv, wa, dnorm, beat):
    total = dqkv.shape[1]

    @pl.loop(0, 4)
    def _(i):
        part = total // 4
        rows = pl.ds(pl.multiple_of(i * part, part), part)
        dnorm[rows, :] = (
            nt(dqkv[0, rows, :], flat(wa[0]))
            + nt(dqkv[1, rows, :], flat(wa[1]))
            + nt(dqkv[2, rows, :], flat(wa[2]))
        )
        beat(i)


def first_backward(picked, up, dnorm, dhid, gains, cols, new_grads, small, beat, tile=128):
    total = picked.shape[0]

    @pl.loop(0, total // tile)
    def _(i):
        rows = pl.ds(pl.multiple_of(i * tile, tile), tile)
        x = picked[rows, :].astype(F32)
        r = cols[rows, R1 : R1 + 1]
        d = dnorm[rows, :]
        xr = x * r
        dx = d * xr
        small[0:1, :] += jnp.sum(dx, axis=0, keepdims=True)
        mean = jnp.mean(dx * gains[0:1, :], axis=1, keepdims=True)
        d_first = r * (gains[0:1, :] * d - xr * mean)
        d_picked = d_first + dhid[rows, :] + cols[rows, DLOG : DLOG + 1] * gains[2:3, :]
        new_grads[rows, :] = (up[rows, :].astype(F32) + d_picked).astype(BF)
        beat(i)


MESH_ID = pl.DeviceIdType.MESH
A_MATS, CHUNKS, PLANE = 4, 3, 8


class Place:
    def __init__(self, depth):
        dp = lax.axis_index("dp")
        self.depth = depth
        self.z = lax.axis_index("fsdp")
        self.core = lax.rem(dp, 2)
        self.x = lax.rem(lax.div(dp, 2), 2)
        self.y = lax.rem(lax.div(dp, 4), 2)
        self.sib = (dp + 1 - 2 * self.core, self.z)
        self.xn = (dp + 2 - 4 * self.x, self.z)
        self.yn = (dp + 4 - 8 * self.y, self.z)
        self.dp = dp

    def ahead(self, o):
        return lax.rem(self.z + o, self.depth)

    def behind(self, o):
        return lax.rem(self.z + self.depth - o, self.depth)

    def at_z(self, z):
        return (self.dp, z)

    def greet(self):
        barrier = pltpu.get_barrier_semaphore()
        peers = [self.sib, self.xn, self.yn]
        peers += [self.at_z(self.ahead(o)) for o in range(1, self.depth)]
        for peer in peers:
            pl.semaphore_signal(barrier, inc=1, device_id=peer, device_id_type=MESH_ID)
        pl.semaphore_wait(barrier, len(peers))


def half_of(ref, core):
    width = ref.shape[-1] // 2
    return pl.ds(pl.multiple_of(core * width, 128), width)


class Gather:
    SENDS, RECVS = 2, 5
    CORE, Z, X, Y, FAR = range(5)
    ARRAYS = A_MATS + 2 * CHUNKS

    def __init__(self, me, wa, wu, wd, sends, recvs):
        self.me, self.refs, self.sends, self.recvs = me, (wa, wu, wd), sends, recvs

    def array(self, a):
        wa, wu, wd = self.refs
        if a < A_MATS:
            return wa.at[a]
        return (wd if a % 2 else wu).at[(a - A_MATS) // 2]

    def piece(self, a, zi, xi, yi, core):
        ref = self.array(a)
        return ref.at[zi, xi, yi, :, half_of(ref, core)]

    def way(self, a):
        return a % 2

    def copy(self, a, kind, ref, dev):
        send = self.sends.at[a * self.SENDS + (0 if kind == self.CORE else 1)]
        recv = self.recvs.at[a * self.RECVS + kind]
        return pltpu.make_async_remote_copy(
            src_ref=ref, dst_ref=ref, send_sem=send, recv_sem=recv, device_id=dev, device_id_type=MESH_ID
        )

    def mine(self, a, zi, flip_x=False, flip_y=False):
        m = self.me
        return self.piece(a, zi, 1 - m.x if flip_x else m.x, 1 - m.y if flip_y else m.y, m.core)

    def took(self, a, kind):
        self.copy(a, kind, self.mine(a, slice(0, self.me.depth - 1)), self.me.xn).wait_recv()

    def core_copy(self, a, core):
        ref = self.array(a)
        return self.copy(a, self.CORE, ref.at[:, :, :, :, half_of(ref, core)], self.me.sib)

    def origins(self):
        return range(1, self.me.depth)

    def send_z(self, a):
        m = self.me
        for o in self.origins():
            self.copy(a, self.Z, self.mine(a, m.z), m.at_z(m.ahead(o))).start()

    def spread(self, a):
        m = self.me
        self.took(a, self.Z)
        for o in self.origins():
            self.copy(a, self.X, self.mine(a, m.behind(o)), m.xn).start()
            self.copy(a, self.Y, self.mine(a, m.behind(o)), m.yn).start()

    def forward(self, a):
        m, by_x = self.me, self.way(a) == 0
        self.took(a, self.X if by_x else self.Y)
        for o in self.origins():
            ref = self.mine(a, m.behind(o), by_x, not by_x)
            self.copy(a, self.FAR, ref, m.yn if by_x else m.xn).start()

    def across(self, a):
        self.took(a, self.Y if self.way(a) == 0 else self.X)
        self.took(a, self.FAR)
        self.core_copy(a, self.me.core).start()

    def ready(self, a):
        self.core_copy(a, 1 - self.me.core).wait_recv()

    def settle(self, a):
        m, ref = self.me, self.array(a)
        self.core_copy(a, m.core).wait_send()
        sent = ref.at[0 : m.depth - 1, :, :, :, half_of(ref, m.core)]
        self.copy(a, self.Z, sent, m.xn).wait_send()


class Owned:
    def __init__(self, me, shards, wa, wu, wd, sems):
        wq, wk, wv, wo, up, down = shards
        z, core = me.z, me.core
        half = half_of(wa, core)
        self.copies = {a: [] for a in range(Gather.ARRAYS)}
        for m, w in enumerate((wq, wk, wv, wo)):
            self.copies[m].append((w.at[:, :, :, half], wa.at[m, z, :, :, :, half]))
        ff_own = up.shape[-1] // me.depth
        for c in range(CHUNKS):
            for j in range(2):
                block = 2 * core + j
                src = up.at[:, :, :, pl.ds(pl.multiple_of(block * ff_own + c * 256, 128), 256)]
                dst = wu.at[c, z, :, :, :, pl.ds(pl.multiple_of(block * 256, 128), 256)]
                self.copies[A_MATS + 2 * c].append((src, dst))
            self.copies[A_MATS + 1 + 2 * c].append((down.at[c, :, :, :, half], wd.at[c, z, :, :, :, half]))
        self.sems = sems

    def all_of(self, a):
        for i, (src, dst) in enumerate(self.copies[a]):
            yield pltpu.make_async_copy(src, dst, self.sems.at[2 * a + i])

    def start(self, a):
        for c in self.all_of(a):
            c.start()

    def wait(self, a):
        for c in self.all_of(a):
            c.wait()


class Reduce:
    SENDS, RECVS = 2, 7
    CORE, FIRST, SECOND, Z, BACK, FAR, LAST = range(7)

    def __init__(
        self, me, w, from_core, from_x, from_y, then_x, then_y, from_z, sends, recvs, frees, at, way
    ):
        self.me, self.w, self.way, self.free, base = me, w, way, frees.at[at], at
        self.from_core, self.from_x, self.from_y = from_core, from_x, from_y
        self.then_x, self.then_y, self.from_z = then_x, then_y, from_z
        self.sends, self.recvs, self.base = sends, recvs, base
        self.mine, self.theirs = half_of(w, me.core), half_of(w, 1 - me.core)

    def copy(self, kind, src, dst, dev):
        small = kind in (self.Z, self.BACK, self.FAR)
        send = self.sends.at[self.base * self.SENDS + small]
        recv = self.recvs.at[self.base * self.RECVS + kind]
        return pltpu.make_async_remote_copy(
            src_ref=src, dst_ref=dst, send_sem=send, recv_sem=recv, device_id=dev, device_id_type=MESH_ID
        )

    def took(self, kind, ref):
        self.copy(kind, ref, ref, self.me.sib).wait_recv()

    def sent(self, kind, ref):
        self.copy(kind, ref, ref, self.me.sib).wait_send()

    def z_copy(self, o):
        m = self.me
        src = self.w.at[m.ahead(o), m.x, m.y, :, self.mine]
        return self.copy(self.Z, src, self.from_z.at[o - 1], m.at_z(m.ahead(o)))

    def back(self, kind, xi, yi, dev):
        ref = self.from_core.at[0, xi, yi]
        return self.copy(kind, ref, ref, dev)

    def add(self, at, arrived):
        self.w[at] = self.w[at] + arrived

    def t1(self):
        self.copy(self.CORE, self.w.at[:, :, :, :, self.theirs], self.from_core, self.me.sib).start()

    def t2(self):
        m, w = self.me, self.w
        self.took(self.CORE, self.from_core)

        @pl.loop(0, 2 * m.depth)
        def _(i):
            zi, xi = lax.div(i, 2), lax.rem(i, 2)
            self.add((zi, xi, slice(None), slice(None), self.mine), self.from_core[zi, xi])

        pl.semaphore_signal(self.free, inc=1, device_id=m.sib, device_id_type=MESH_ID)
        self.copy(self.FIRST, w.at[0:2, 1 - m.x, :, :, self.mine], self.from_x, m.xn).start()
        self.copy(self.FIRST, w.at[2:4, :, 1 - m.y, :, self.mine], self.from_y, m.yn).start()

    def t3(self):
        m, w = self.me, self.w
        self.took(self.FIRST, w.at[0:2, :, :, :, self.mine])

        @pl.loop(0, 2)
        def _(zi):
            self.add((zi, m.x, slice(None), slice(None), self.mine), self.from_x[zi])
            self.add((2 + zi, slice(None), m.y, slice(None), self.mine), self.from_y[zi])

        self.copy(self.SECOND, w.at[0:2, m.x, 1 - m.y, :, self.mine], self.then_y, m.yn).start()
        self.copy(self.SECOND, w.at[2:4, 1 - m.x, m.y, :, self.mine], self.then_x, m.xn).start()

    def t4(self):
        m = self.me
        self.took(self.SECOND, self.w.at[0:2, 0:2, 0, :, self.mine])
        self.add((slice(0, 2), m.x, m.y, slice(None), self.mine), self.then_y[...])
        self.add((slice(2, 4), m.x, m.y, slice(None), self.mine), self.then_x[...])
        for o in range(1, m.depth):
            self.z_copy(o).start()

    def t5(self):
        m = self.me
        total = self.w[m.z, m.x, m.y, :, self.mine].astype(F32)
        self.took(self.Z, self.from_z)
        for o in range(1, m.depth):
            total = total + self.from_z[o - 1].astype(F32)
        self.from_core[0, m.x, m.y] = total.astype(BF)
        self.back(self.BACK, m.x, m.y, m.xn).start()
        self.back(self.BACK, m.x, m.y, m.yn).start()

    def t6(self):
        m = self.me
        self.took(self.BACK, self.from_core.at[0, 0:2, 0])
        if self.way == 0:
            self.back(self.FAR, 1 - m.x, m.y, m.yn).start()
        else:
            self.back(self.FAR, m.x, 1 - m.y, m.xn).start()

    def t7(self):
        m = self.me
        self.took(self.FAR, self.from_core.at[0, 0, 0])
        pl.semaphore_wait(self.free, 1)
        self.copy(self.LAST, self.from_core.at[0], self.from_core.at[1], m.sib).start()

    def t8(self):
        m = self.me
        self.took(self.LAST, self.from_core.at[1])
        self.sent(self.CORE, self.w)
        self.sent(self.Z, self.w.at[0 : m.depth - 1, 0:2, 0, :, self.mine])


class SmallSum:
    def __init__(self, me, small, inbox, sends, recvs, base):
        self.me, self.small, self.inbox = me, small, inbox
        self.sends, self.recvs, self.base = sends, recvs, base

    def copy(self, k, src, dst, dev):
        return pltpu.make_async_remote_copy(
            src_ref=src, dst_ref=dst, send_sem=self.sends.at[self.base[0]], recv_sem=self.recvs.at[self.base[1] + k],
            device_id=dev, device_id_type=MESH_ID,
        )

    def peer(self, k):
        return (self.me.sib, self.me.xn, self.me.yn)[k]

    def step(self, k):
        m, small, inbox = self.me, self.small, self.inbox
        if 1 <= k <= 3:
            self.copy(k - 1, small.at[0], inbox.at[k - 1], m.sib).wait_recv()
            small[k] = small[k - 1] + inbox[k - 1]
        if k <= 2:
            self.copy(k, small.at[k], inbox.at[k], self.peer(k)).start()
        if k == 3:
            for o in range(1, m.depth):
                self.copy(3, small.at[3], inbox.at[2 + o], m.at_z(m.ahead(o))).start()
        if k == 4:
            self.copy(3, inbox.at[3:], inbox.at[3:], m.sib).wait_recv()
            total = small[3]
            for o in range(1, m.depth):
                total = total + inbox[2 + o]
            small[4] = total
            self.copy(3, inbox, inbox, m.sib).wait_send()


def chunk_boxes(rows_a, width, rows_d, ff_c):
    def boxes(n, rows, cols, first):
        def box(*lead):
            return pltpu.VMEM((n,) + lead + (rows, cols), BF)

        return ([box(4, 2, 2)] if first else []) + [box(2, 2), box(2, 2), box(2), box(2), box(3)]

    return (
        boxes(CHUNKS, rows_a, ff_c // 2, True)
        + boxes(CHUNKS, rows_d, width // 2, True)
        + boxes(A_MATS, rows_a, width // 2, False)
    )


def block_kernel(
    depth, tokens, cot, idx, valid, wq, wk, wv, wo, up_in, down_in, gain1, gain2, gain3,
    new_rows, new_grads, fa, fu, fd, small_out,
    wa, wu, wd, picked, up, cols, na, nmt, dd, qkv, probs, mixed, attn_out, act, dup, down, dnm,
    gains, gpad, gbox, small, inbox,
    tok_sem, own_sem, out_sem, ag_send, ag_recv, rs_send, rs_recv, frees, opened, *boxes,
):
    seqs, slots = idx.shape
    width = picked.shape[1]
    scale = (width // HEADS) ** -0.5
    rows_a = wa.shape[-2]
    half = width // 2
    me = Place(depth)
    me.greet()
    own = Owned(me, (wq, wk, wv, wo, up_in, down_in), wa, wu, wd, own_sem)
    ag = Gather(me, wa, wu, wd, ag_send, ag_recv)
    sem_at = (20, 70)
    others = range(1, depth)

    def gain_copy(o):
        return pltpu.make_async_remote_copy(
            src_ref=gpad, dst_ref=gbox.at[o - 1], send_sem=rs_send.at[21], recv_sem=rs_recv.at[74],
            device_id=me.at_z(me.ahead(o)), device_id_type=MESH_ID,
        )

    own.start(0)
    own.start(1)
    picker = Picker(tokens, cot, picked, up, cols, (act, dup), tok_sem)
    picker.start(0)
    for a in range(2, Gather.ARRAYS):
        own.start(a)
    own.wait(0)
    ag.send_z(0)
    picker.turn(idx, valid)
    own.wait(1)
    ag.send_z(1)
    owned = gain1.shape[0]
    spot = lax.broadcasted_iota(jnp.int32, (owned, width), 1) - lax.broadcasted_iota(jnp.int32, (owned, width), 0)
    spot = jnp.where(spot == me.z * owned, 1.0, 0.0).astype(BF)
    gpad[...] = jnp.zeros_like(gpad)
    for i, g in enumerate((gain1, gain2, gain3)):
        gpad[i : i + 1, :] = nn(g[...].astype(F32).reshape(1, owned).astype(BF), spot)
    for o in others:
        gain_copy(o).start()
    picker.pick(0, slots, True)
    for a in range(2, Gather.ARRAYS):
        own.wait(a)
    ag.send_z(2)
    ag.spread(0)
    picker.pick(1, slots, True)
    ag.send_z(3)
    picker.pick(2, slots, True)
    ag.send_z(4)
    ag.forward(0)
    ag.spread(1)
    picker.pick(3, slots, False)
    pltpu.make_async_remote_copy(
        src_ref=gbox, dst_ref=gbox, send_sem=rs_send.at[21], recv_sem=rs_recv.at[74],
        device_id=me.sib, device_id_type=MESH_ID,
    ).wait()
    total = gpad[...]
    for o in others:
        total = total + gbox[o - 1]
    gains[...] = total
    norm_phase(picked, gains, cols, na)
    ag.across(0)
    ag.send_z(5)
    ag.forward(1)
    ag.spread(2)
    ag.ready(0)
    qkv_one(na, wa, qkv, scale, 0)
    ag.across(1)
    ag.send_z(6)
    ag.forward(2)
    ag.ready(1)
    qkv_one(na, wa, qkv, scale, 1)
    ag.across(2)
    ag.spread(3)
    ag.ready(2)
    qkv_one(na, wa, qkv, scale, 2)
    ag.forward(3)
    ag.spread(4)
    ag.send_z(7)

    @pl.loop(0, seqs)
    def _(s):
        attention_forward(idx, valid, cols, qkv, probs, mixed, s)

        @pl.when(s == 0)
        def _():
            ag.across(3)
            ag.spread(5)

        @pl.when(s == 1)
        def _():
            ag.forward(4)
            ag.send_z(8)
            ag.send_z(9)

        @pl.when(s == 2)
        def _():
            ag.forward(5)
            ag.across(4)

        @pl.when(s == 3)
        def _():
            ag.spread(6)

    ag.ready(3)
    out_phase(mixed, wa, attn_out)
    ag.across(5)
    mid_norm(picked, attn_out, up, gains, cols, na, nmt, dd)
    ag.forward(6)
    ag.spread(7)

    ubox, dbox, abox = boxes[0:6], boxes[6:12], boxes[12:17]
    reducers = {}

    def reducer(name, at, w, core_box, rest, i, way):
        reducers[name] = Reduce(me, w, core_box, *[x.at[i] for x in rest], rs_send, rs_recv, frees, at, way)

    for c in range(CHUNKS):
        reducer("u%d" % c, c, wu.at[c], ubox[0].at[c], ubox[1:], c, 0)
        reducer("d%d" % c, 3 + c, wd.at[c], dbox[0].at[c], dbox[1:], c, 1)
    spots = ((act, 0), (act, half), (dup, 0), (dup, half))
    terms = [probs.at[m, :, :, :, 0:rows_a, 0:width] for m in range(3)] + [wa.at[3]]
    for m, name in enumerate("qkvo"):
        ref, lane = spots[m]
        box = ref.at[:, :, :, 0:rows_a, lane : lane + half]
        reducer(name, 6 + m, terms[m], box, abox, m, m % 2)
    finals = {"q": (fa, 0), "k": (fa, 1), "v": (fa, 2), "o": (fa, 3)}
    for c in range(CHUNKS):
        finals["u%d" % c] = (fu, c)
        finals["d%d" % c] = (fd, c)
    order = list(finals)

    def result_copies(name):
        dst, i = finals[name]
        box = reducers[name].from_core
        for h, core in ((0, me.core), (1, 1 - me.core)):
            yield pltpu.make_async_copy(box.at[h], dst.at[i, :, :, :, half_of(dst, core)], out_sem.at[{"u": 1, "d": 2}.get(name[0], 0)])

    def step(k, *names):
        for name in names:
            getattr(reducers[name], "t%d" % k)()
            if k == 8:
                for c in result_copies(name):
                    c.start()

    for c in range(CHUNKS):
        for a in (A_MATS + 2 * c, A_MATS + 1 + 2 * c):
            ag.ready(a)

        @pl.loop(0, 4)
        def _(n):
            mlp_up(na, dd, wu, wd, act, dup, c, n)
            if c > 0:

                @pl.when(n == 1)
                def _():
                    step(2, "d%d" % (c - 1), "u%d" % (c - 1))

        if c == 0:
            ag.across(6)
            ag.spread(8)
            ag.forward(7)
        if c == 1:
            ag.across(9)
        mlp_down(act, wd, down, c)
        mlp_dnormed(dup, wu, dnm, c)
        if c == 0:
            ag.across(7)
            ag.spread(9)
        if c == 2:
            step(4, "d0", "u0")
        ag.settle(A_MATS + 2 * c)
        ag.settle(A_MATS + 1 + 2 * c)
        mlp_grad_down(act, dd, wd, c)
        step(1, "d%d" % c)
        if c == 0:
            ag.forward(8)
        mlp_grad_up(nmt, dup, wu, c)
        if c == 0:
            ag.across(8)
            ag.forward(9)
        step(1, "u%d" % c)
        if c > 0:
            step(3, "d%d" % (c - 1), "u%d" % (c - 1))
    pl.semaphore_signal(opened, inc=1, device_id=me.sib, device_id_type=MESH_ID)
    for a in range(A_MATS):
        ag.settle(a)
    datt, dmix = na, dd
    mid_backward(picked, attn_out, up, down, dnm, gains, cols, datt, dd, small.at[0])
    rows_out = pltpu.make_async_copy(dd, new_rows, tok_sem.at[0])
    rows_out.start()
    step(2, "d2", "u2")
    rows_out.wait()
    out_backward(datt, mixed, wa, dmix)
    pl.semaphore_wait(opened, 1)
    step(1, "o")
    step(4, "d1", "u1")
    step(5, "d0", "u0")
    norm_again(picked, gains, cols, na)

    @pl.loop(0, seqs)
    def _(s):
        attention_backward(qkv, probs, mixed, dmix, s, slots, scale)

        @pl.when(s == 0)
        def _():
            step(2, "o")
            step(6, "d0", "u0")

        @pl.when(s == 1)
        def _():
            step(7, "d0", "u0")

        @pl.when(s == 2)
        def _():
            step(3, "d2", "u2")
            step(8, "d0", "u0")

        @pl.when(s == 3)
        def _():
            step(3, "o")

    for m, name in enumerate("qkv"):
        terms[m][...] = grad_of(na, qkv[m]).reshape(wa.shape[1:])
        step(1, name)
        if m == 0:
            step(5, "d1", "u1")
        if m > 0:
            step(2, "qkv"[m - 1])
    step(4, "d2", "u2")

    def at_beats(*todo):
        def beat(i):
            for k, work in todo:

                @pl.when(i == k)
                def _():
                    for t, *names in work:
                        step(t, *names)

        return beat

    qkv_normed(
        qkv, wa, down, at_beats((0, [(2, "v")]), (1, [(4, "o")]), (2, [(3, "q")]), (3, [(6, "d1", "u1"), (3, "k")]))
    )
    first_backward(
        picked, up, down, dnm, gains, cols, dd, small.at[0],
        at_beats((2, [(7, "d1", "u1")]), (4, [(3, "v"), (4, "q")])),
    )
    grads_out = pltpu.make_async_copy(dd, new_grads, tok_sem.at[1])
    grads_out.start()
    sums = SmallSum(me, small, inbox, rs_send, rs_recv, sem_at)
    sums.step(0)
    step(4, "k")
    step(4, "v")
    sums.step(1)
    step(5, "d2", "u2")
    step(5, "o")
    sums.step(2)
    step(5, "q")
    step(5, "k")
    sums.step(3)
    step(5, "v")
    step(6, "d2", "u2", "o")
    step(6, "q")
    step(6, "k")
    sums.step(4)
    step(6, "v")
    step(7, "d2", "u2", "o")
    step(7, "q", "k", "v")
    step(8, "d1", "u1", "d2", "u2", "o", "q", "k", "v")
    small_out[...] = small[4]
    for i, dst in enumerate((fa, fu, fd)):
        pltpu.make_async_copy(dst, dst, out_sem.at[i]).wait()
    grads_out.wait()


def place_kernel(depth, idx, tokens, cot, new_rows, new_grads, fa, fu, fd, sums,
                 out, grad, gq, gk, gv, go, gup, gdown, g1, g2, g3):
    s = pl.program_id(0)
    length, slots = tokens.shape[0], idx.shape[1]
    spot = lax.broadcasted_iota(jnp.int32, (length, slots), 0)
    hot = jnp.where(spot == idx[pl.ds(s, 1), :], 1.0, 0.0)
    hit = jnp.sum(hot, axis=1, keepdims=True) > 0
    hot = hot.astype(BF)
    for src, rows, dst in ((tokens, new_rows, out), (cot, new_grads, grad)):
        dst[...] = jnp.where(hit, nn(hot, rows[...]), src[...].astype(F32)).astype(BF)
    place_weights(fa, fu, fd, gq, gk, gv, go, gup, gdown)
    own = g1.shape[0]
    for k in range(depth):

        @pl.when((s == 0) & (lax.axis_index("fsdp") == k))
        def _():
            for i, g in enumerate((g1, g2, g3)):
                g[...] = sums[i, k * own : (k + 1) * own]


def place_weights(fa, fu, fd, gq, gk, gv, go, gup, gdown):
    for m, g in enumerate((gq, gk, gv, go)):
        g[...] = fa[m, 0].astype(F32)
    quarter = 256
    ff_own = gup.shape[1] // 4
    for c in range(CHUNKS):
        for j in range(4):
            gup[:, j * ff_own + c * quarter : j * ff_own + (c + 1) * quarter] = fu[c, 0, :, j * quarter : (j + 1) * quarter].astype(F32)
        gdown[c, 0] = fd[c, 0].astype(F32)


def remote_params(collective_id, limit=60):
    return pltpu.CompilerParams(
        collective_id=collective_id, has_side_effects=True, vmem_limit_bytes=limit * 2**20
    )


def over_groups(groups, terms):
    if groups == 1:
        return terms
    dp = groups * PLANE
    total = [t.astype(F32) for t in terms]
    for k in range(groups.bit_length() - 1):
        hop = PLANE << k
        pairs = [(i, i ^ hop) for i in range(dp)]
        total = [t + lax.ppermute(t, "dp", pairs) for t in total]
    return total


def body(depth, groups, tokens, row_index, row_valid, w_query, w_key, w_value, w_out, w_up, w_down,
         gain_attn, gain_mlp, w_router, cotangent):
    seqs, slots = row_index.shape
    width = tokens.shape[1]
    own = w_query.shape[0]
    ff = w_up.shape[1]
    length = tokens.shape[0] // seqs
    total = seqs * slots
    rq, cw = own // 4, ff // CHUNKS
    dq = w_down.shape[0] // (4 * CHUNKS)
    sd = jax.ShapeDtypeStruct
    hbm, vm = pl.BlockSpec(memory_space=pl.ANY), pl.BlockSpec(memory_space=pltpu.VMEM)
    sem = pltpu.SemaphoreType.DMA
    vmem = pltpu.VMEM
    gains3 = (gain_attn, gain_mlp, w_router)
    squares = [w.reshape(2, 2, rq, width) for w in (w_query, w_key, w_value, w_out)]
    sa, su, sdn = (A_MATS, depth, 2, 2, rq, width), (CHUNKS, depth, 2, 2, rq, cw), (CHUNKS, depth, 2, 2, dq, width)
    narr = Gather.ARRAYS
    rows = (total, width)
    work = (4, 2, 2, total // 16, cw)
    regular = pltpu.SemaphoreType.REGULAR
    blocks = (seqs, 4, 2, 2, length // 16, width)
    new_rows, new_grads, fa, fu, fd, sums = pl.pallas_call(
        functools.partial(block_kernel, depth),
        out_shape=(
            sd(rows, BF), sd(rows, BF), sd(sa[:1] + sa[2:], BF), sd(su[:1] + su[2:], BF), sd(sdn[:1] + sdn[2:], BF),
            sd((8, width), F32),
        ),
        in_specs=[hbm, hbm, vm, vm] + [hbm] * 6 + [vm] * 3,
        out_specs=(hbm,) * 5 + (vm,),
        scratch_shapes=[
            vmem(sa, BF), vmem(su, BF), vmem(sdn, BF), vmem(rows, BF), vmem(rows, BF), vmem((total, 128), F32),
            vmem(rows, BF), vmem((width, total), BF), vmem(rows, BF), vmem((3,) + rows, BF), vmem((3,) + work, BF),
            vmem(rows, BF), vmem(rows, F32), vmem(work, BF), vmem(work, BF), vmem(rows, F32), vmem(rows, F32),
            vmem((8, width), F32), vmem((8, width), F32), vmem((depth - 1, 8, width), F32), vmem((5, 8, width), F32), vmem((2 + depth, 8, width), F32),
            sem((2,)), sem((2 * narr,)), sem((3,)), sem((2 * narr,)), sem((5 * narr,)),
            sem((2 * narr + 2,)), sem((7 * narr + 5,)), regular((narr,)), regular,
        ]
        + chunk_boxes(rq, width, dq, cw),
        compiler_params=remote_params(0, 63),
    )(
        tokens.reshape(blocks), cotangent.reshape(blocks), row_index, row_valid, *squares,
        w_up.reshape(2, 2, rq, ff), w_down.reshape(CHUNKS, 2, 2, dq, width), *gains3,
    )
    fa, fu, fd, sums = over_groups(groups, (fa, fu, fd, sums))

    def by_seq(*shape):
        return pl.BlockSpec(shape, lambda i: (i,) + (0,) * (len(shape) - 1))

    def by_quarter(*shape):
        return pl.BlockSpec(shape, lambda i: (0, i) + (0,) * (len(shape) - 2))

    out, grad, gq, gk, gv, go, gup, gdown, g1, g2, g3 = pl.pallas_call(
        functools.partial(place_kernel, depth),
        grid=(seqs,),
        out_shape=(sd(tokens.shape, BF),) * 2
        + (sd((own, width), F32),) * 4
        + (sd((own, ff), F32), sd((CHUNKS, 4, dq, width), F32))
        + (sd((own,), F32),) * 3,
        in_specs=[pl.BlockSpec((seqs, slots), lambda i: (0, 0))]
        + [by_seq(length, width)] * 2
        + [by_seq(slots, width)] * 2
        + [by_quarter(A_MATS, 1, rq, width), by_quarter(CHUNKS, 1, rq, cw), by_quarter(CHUNKS, 1, dq, width)]
        + [pl.BlockSpec((8, width), lambda i: (0, 0))],
        out_specs=[by_seq(length, width)] * 2
        + [by_seq(rq, width)] * 4
        + [by_seq(rq, ff), by_quarter(CHUNKS, 1, dq, width)]
        + [pl.BlockSpec((own,), lambda i: (0,))] * 3,
        compiler_params=pltpu.CompilerParams(vmem_limit_bytes=62 * 2**20),
    )(
        row_index, tokens, cotangent, new_rows, new_grads, fa.reshape(A_MATS, 4, rq, width),
        fu.reshape(CHUNKS, 4, rq, cw), fd.reshape(CHUNKS, 4, dq, width), sums,
    )
    return (out, grad, gq, gk, gv, go, gup, gdown.reshape(w_down.shape), g1, g2, g3)


def solution(mesh):
    depth = mesh.shape["fsdp"]
    both = P(("dp", "fsdp"), None)
    weight, vector = P("fsdp", None), P("fsdp")
    return jax.shard_map(
        functools.partial(body, depth, mesh.shape["dp"] // PLANE),
        mesh=mesh,
        in_specs=(both,) * 3 + (weight,) * 6 + (vector,) * 3 + (both,),
        out_specs=(both, both) + (weight,) * 6 + (vector,) * 3,
        check_vma=False,
    )
```
